128 devices in a mesh: dp: 32 (over x, z, core), tensor: 4 (over y).
Axes of the slice: x: 4, y: 4, z: 4, core: 2. Of those that a mesh axis runs over, the one named last changes fastest.
Arguments:
- pixels: int32 [32, 3, 128, 128], P('dp'), may hold values from 0 to 255
- image_sizes: int32 [32, 2], P('dp'), may hold values from 4 to 128, as said below
- code_indices: int32 [32, 32, 32], P('dp'), may hold values from 0 to 511
- stem_kernel: float32 [4, 4, 3, 256], P(None, None, None, 'tensor'), may hold values from -0.875 to 0.875
- stride_kernels: float32 [2, 4, 4, 256, 256], P(None, None, None, 'tensor'), may hold values from -0.09375 to 0.09375
- block_kernels: float32 [2, 3, 3, 256, 256], P(None, None, None, 'tensor'), may hold values from -0.125 to 0.125
- block_mixers: float32 [2, 256, 256], P(None, 'tensor'), may hold values from -0.375 to 0.375
- pre_project: float32 [256, 64], P('tensor'), may hold values from -0.375 to 0.375
- post_project: float32 [64, 256], P(None, 'tensor'), may hold values from -0.75 to 0.75
- codebook: float32 [512, 64], replicated, may hold values from -4 to 4
- head_kernel: float32 [4, 4, 256, 6], P(None, None, 'tensor'), may hold values from -0.1875 to 0.1875
- first_stem: float32 [4, 4, 3, 256], P(None, None, None, 'tensor')
- first_stride: float32 [2, 4, 4, 256, 256], P(None, None, None, 'tensor')
- first_block: float32 [2, 3, 3, 256, 256], P(None, None, None, 'tensor')
- first_mixer: float32 [2, 256, 256], P(None, 'tensor')
- first_pre: float32 [256, 64], P('tensor')
- first_post: float32 [64, 256], P(None, 'tensor')
- first_codes: float32 [512, 64], replicated
- first_head: float32 [4, 4, 256, 6], P(None, None, 'tensor')
- second_stem: float32 [4, 4, 3, 256], P(None, None, None, 'tensor')
- second_stride: float32 [2, 4, 4, 256, 256], P(None, None, None, 'tensor')
- second_block: float32 [2, 3, 3, 256, 256], P(None, None, None, 'tensor')
- second_mixer: float32 [2, 256, 256], P(None, 'tensor')
- second_pre: float32 [256, 64], P('tensor')
- second_post: float32 [64, 256], P(None, 'tensor')
- second_codes: float32 [512, 64], replicated
- second_head: float32 [4, 4, 256, 6], P(None, None, 'tensor')
Outputs:
- loss_terms: float32 [4], replicated
- grad_norm: float32 [], replicated
- stem_updated: float32 [4, 4, 3, 256], P(None, None, None, 'tensor')
- stride_updated: float32 [2, 4, 4, 256, 256], P(None, None, None, 'tensor')
- block_updated: float32 [2, 3, 3, 256, 256], P(None, None, None, 'tensor')
- mixer_updated: float32 [2, 256, 256], P(None, 'tensor')
- pre_updated: float32 [256, 64], P('tensor')
- post_updated: float32 [64, 256], P(None, 'tensor')
- codes_updated: float32 [512, 64], replicated
- head_updated: float32 [4, 4, 256, 6], P(None, None, 'tensor')
- first_stem_new: float32 [4, 4, 3, 256], P(None, None, None, 'tensor')
- first_stride_new: float32 [2, 4, 4, 256, 256], P(None, None, None, 'tensor')
- first_block_new: float32 [2, 3, 3, 256, 256], P(None, None, None, 'tensor')
- first_mixer_new: float32 [2, 256, 256], P(None, 'tensor')
- first_pre_new: float32 [256, 64], P('tensor')
- first_post_new: float32 [64, 256], P(None, 'tensor')
- first_codes_new: float32 [512, 64], replicated
- first_head_new: float32 [4, 4, 256, 6], P(None, None, 'tensor')
- second_stem_new: float32 [4, 4, 3, 256], P(None, None, None, 'tensor')
- second_stride_new: float32 [2, 4, 4, 256, 256], P(None, None, None, 'tensor')
- second_block_new: float32 [2, 3, 3, 256, 256], P(None, None, None, 'tensor')
- second_mixer_new: float32 [2, 256, 256], P(None, 'tensor')
- second_pre_new: float32 [256, 64], P('tensor')
- second_post_new: float32 [64, 256], P(None, 'tensor')
- second_codes_new: float32 [512, 64], replicated
- second_head_new: float32 [4, 4, 256, 6], P(None, None, 'tensor')
The draws below stay inside these ranges and needn't reach their ends.
Inputs may be any that keep to these rules, and one draw needn't show every extreme that they name: `image_sizes`: heights and widths of the valid regions are multiples of 4; some image is 128 by 128.
All inputs are finite; a program needn't handle non-finite values.
Results may differ from the reference program's by a relative error of at most 0.0044.
The reference program's roundings to bfloat16 on the way count: a program that leaves them out, or rounds other values in their place, can miss the bound.
Values may be sent and summed in bfloat16 or wider, within the bound.
No kernel may reach another device: no remote copies, remote signals or barrier semaphores. Data moves between devices by JAX's collectives and lax.ppermute only.
A program may use at most 192 MiB of HBM per device.

```python
import math
import jax
import jax.numpy as jnp
from jax import lax

C = 256
E = 64
K = 512
S = 128
STEP = 10
IMG_DEV = 1
IMAGES = 32
PARAMS = 3510272


clip_norm = 0.002


beta_one = 0.9


beta_two = 0.999


def entry_scale():
    return clip_norm / PARAMS ** 0.5


def first_moment(key, shape):
    sign_key, size_key = jax.random.split(key)
    sign = jnp.where(jax.random.bernoulli(sign_key, 0.5, shape), 1.0, -1.0)
    spread = jnp.exp(jax.random.uniform(size_key, shape, jnp.float32, math.log(0.5), math.log(2.0)))
    return (sign * spread * entry_scale() * (1.0 - beta_one) / beta_one).astype(jnp.float32)


def second_moment(key, shape):
    spread = jnp.exp(jax.random.uniform(key, shape, jnp.float32, math.log(0.5), math.log(8.0)))
    return (spread * entry_scale() ** 2 * (1.0 - beta_two) / beta_two).astype(jnp.float32)


def draw_image_sizes(key, part):
    key = jax.random.fold_in(key, 11)
    side = S // 4
    order = jnp.arange(IMAGES)
    device = order // IMG_DEV
    last = max(IMAGES // IMG_DEV - 1, 1)
    base = side // 2 + (side - side // 2) * device // last
    jitter = jax.random.randint(key, (IMAGES, 2), 0, 2)
    quarter = jnp.maximum(base[:, None] - jitter, 1)
    quarter = jnp.where(order[:, None] == IMAGES - 1, side, quarter)
    return (4 * quarter).astype(jnp.int32)


def draw_first_stem(key, part):
    key = jax.random.fold_in(key, 21)
    return first_moment(key, (4, 4, 3, C))


def draw_first_stride(key, part):
    key = jax.random.fold_in(key, 22)
    return first_moment(key, (2, 4, 4, C, C))


def draw_first_block(key, part):
    key = jax.random.fold_in(key, 23)
    return first_moment(key, (2, 3, 3, C, C))


def draw_first_mixer(key, part):
    key = jax.random.fold_in(key, 24)
    return first_moment(key, (2, C, C))


def draw_first_pre(key, part):
    key = jax.random.fold_in(key, 25)
    return first_moment(key, (C, E))


def draw_first_post(key, part):
    key = jax.random.fold_in(key, 26)
    return first_moment(key, (E, C))


def draw_first_codes(key, part):
    key = jax.random.fold_in(key, 27)
    return first_moment(key, (K, E))


def draw_first_head(key, part):
    key = jax.random.fold_in(key, 28)
    return first_moment(key, (4, 4, C, 6))


def draw_second_stem(key, part):
    key = jax.random.fold_in(key, 31)
    return second_moment(key, (4, 4, 3, C))


def draw_second_stride(key, part):
    key = jax.random.fold_in(key, 32)
    return second_moment(key, (2, 4, 4, C, C))


def draw_second_block(key, part):
    key = jax.random.fold_in(key, 33)
    return second_moment(key, (2, 3, 3, C, C))


def draw_second_mixer(key, part):
    key = jax.random.fold_in(key, 34)
    return second_moment(key, (2, C, C))


def draw_second_pre(key, part):
    key = jax.random.fold_in(key, 35)
    return second_moment(key, (C, E))


def draw_second_post(key, part):
    key = jax.random.fold_in(key, 36)
    return second_moment(key, (E, C))


def draw_second_codes(key, part):
    key = jax.random.fold_in(key, 37)
    return second_moment(key, (K, E))


def draw_second_head(key, part):
    key = jax.random.fold_in(key, 38)
    return second_moment(key, (4, 4, C, 6))


def place_ends(values, rng, low, largest):
    dims = values.shape
    spot = [jax.random.randint(jax.random.fold_in(rng, axis), (), 0, dims[axis]) for axis in range(len(dims))]
    values = values.at[tuple(spot)].set(low)
    longest = dims.index(max(dims))
    spot[longest] = (spot[longest] + 1) % dims[longest]
    return values.at[tuple(spot)].set(largest)


def level_of(own_key, dims, cuts, smallest, largest):
    def one(position, blocks):
        steps = jax.random.uniform(jax.random.fold_in(jax.random.fold_in(own_key, 6), position), (blocks,), jnp.float32, smallest / len(cuts), largest / len(cuts))
        return jnp.repeat(jnp.exp(steps), dims[position] // blocks).reshape((-1,) + (1,) * (len(dims) - position - 1))

    loudness = one(*cuts[0])
    for cut in cuts[1:]:
        loudness = loudness * one(*cut)
    return loudness


def normal_values(rng, dims, width, reach, shards=(), kind=jnp.bfloat16):
    values = jax.random.normal(rng, dims, jnp.float32) * width
    if len(shards) > 0:
        values = level_of(rng, dims, shards, -0.22, 0.18) * values
    return jnp.clip(values, min=-reach, max=reach).astype(kind)


def setup_inputs(seed: int = 0) -> dict:
    keys = jax.random.split(jax.random.key(seed), 28)
    return {
        "pixels": place_ends(jax.random.randint(keys[0], (IMAGES, 3, S, S), 0, 256), jax.random.fold_in(keys[0], 1), 0, 255).astype(jnp.int32),
        "image_sizes": draw_image_sizes(jax.random.fold_in(keys[27], 71), 0),
        "code_indices": place_ends(jax.random.randint(keys[2], (IMAGES, S // 4, S // 4), 0, K), jax.random.fold_in(keys[2], 1), 0, K - 1).astype(jnp.int32),
        "stem_kernel": normal_values(keys[3], (4, 4, 3, C), 48 ** -0.5, 0.875, ((3, 4),), jnp.float32),
        "stride_kernels": normal_values(keys[4], (2, 4, 4, C, C), (16 * C) ** -0.5, 0.09375, ((3, 4),), jnp.float32),
        "block_kernels": normal_values(keys[5], (2, 3, 3, C, C), (9 * C) ** -0.5, 0.125, ((3, 4),), jnp.float32),
        "block_mixers": normal_values(keys[6], (2, C, C), C ** -0.5, 0.375, ((1, 4),), jnp.float32),
        "pre_project": normal_values(keys[7], (C, E), C ** -0.5, 0.375, ((0, 4),), jnp.float32),
        "post_project": normal_values(keys[8], (E, C), E ** -0.5, 0.75, ((1, 4),), jnp.float32),
        "codebook": normal_values(keys[9], (K, E), 0.6, 4.0, (), jnp.float32),
        "head_kernel": normal_values(keys[10], (4, 4, C, 6), (4 * C) ** -0.5, 0.1875, ((2, 4),), jnp.float32),
        "first_stem": draw_first_stem(jax.random.fold_in(keys[27], 71), 0),
        "first_stride": draw_first_stride(jax.random.fold_in(keys[27], 71), 0),
        "first_block": draw_first_block(jax.random.fold_in(keys[27], 71), 0),
        "first_mixer": draw_first_mixer(jax.random.fold_in(keys[27], 71), 0),
        "first_pre": draw_first_pre(jax.random.fold_in(keys[27], 71), 0),
        "first_post": draw_first_post(jax.random.fold_in(keys[27], 71), 0),
        "first_codes": draw_first_codes(jax.random.fold_in(keys[27], 71), 0),
        "first_head": draw_first_head(jax.random.fold_in(keys[27], 71), 0),
        "second_stem": draw_second_stem(jax.random.fold_in(keys[27], 71), 0),
        "second_stride": draw_second_stride(jax.random.fold_in(keys[27], 71), 0),
        "second_block": draw_second_block(jax.random.fold_in(keys[27], 71), 0),
        "second_mixer": draw_second_mixer(jax.random.fold_in(keys[27], 71), 0),
        "second_pre": draw_second_pre(jax.random.fold_in(keys[27], 71), 0),
        "second_post": draw_second_post(jax.random.fold_in(keys[27], 71), 0),
        "second_codes": draw_second_codes(jax.random.fold_in(keys[27], 71), 0),
        "second_head": draw_second_head(jax.random.fold_in(keys[27], 71), 0),
    }


@jax.custom_vjp
def low(v):
    return lax.optimization_barrier(v.astype(jnp.bfloat16)).astype(jnp.float32)

@jax.custom_vjp
def low_back(v):
    return v

def low_keep(v):
    return (low(v), None)

def low_pass(kept, grad):
    return (grad,)

def back_keep(v):
    return (v, None)

def back_low(kept, grad):
    return (low(grad),)
low.defvjp(low_keep, low_pass)
low_back.defvjp(back_keep, back_low)
beta_commit = 0.25
clip_norm = 0.002
beta_one = 0.9
beta_two = 0.999
adam_eps = 1e-08
decay_rate = 0.01
half_bin = 1.0 / 255.0
root_half = 0.7071067811865476

def conv_op(inputs, kernel, stride, dilate, pad):
    return lax.conv_general_dilated(inputs, kernel, (stride, stride), ((pad, pad), (pad, pad)), lhs_dilation=(dilate, dilate), dimension_numbers=('NHWC', 'HWIO', 'NHWC'), precision=lax.Precision.HIGHEST)

def turned(kernel):
    return jnp.swapaxes(low(kernel), 2, 3)

def channel_mix(inputs, matrix):
    return jnp.einsum('bhwc,cd->bhwd', inputs, matrix, precision=lax.Precision.HIGHEST)

def valid_masks(sizes, side):
    rows = jnp.arange(side)
    pix = (rows[None, :, None] < sizes[:, 0, None, None]) & (rows[None, None, :] < sizes[:, 1, None, None])
    lat_rows = jnp.arange(side // 4)
    lat = (lat_rows[None, :, None] < sizes[:, 0, None, None] // 4) & (lat_rows[None, None, :] < sizes[:, 1, None, None] // 4)
    return (pix.astype(jnp.float32), lat.astype(jnp.float32))

def pixel_bits(out, pix, pix_mask):
    target = pix.astype(jnp.float32) / 127.5 - 1.0
    center = jnp.tanh(out[..., 0:3])
    sigma = 0.25 + jax.nn.softplus(out[..., 3:6])
    lower = jnp.where(pix == 0, -40.0, (target - half_bin - center) / sigma)
    upper = jnp.where(pix == 255, 40.0, (target + half_bin - center) / sigma)
    right = 0.5 * (lax.erfc(lower * root_half) - lax.erfc(upper * root_half))
    left = 0.5 * (lax.erfc(-upper * root_half) - lax.erfc(-lower * root_half))
    mass = jnp.where(lower + upper > 0, right, left)
    return -jnp.sum(pix_mask[..., None] * jnp.log(mass)) / math.log(2.0)

def res_block(resid, kernel3, mixer):
    act_in = low(jax.nn.gelu(resid))
    inner = low_back(conv_op(act_in, turned(kernel3), 1, 1, 1))
    act_mid = low(jax.nn.gelu(inner))
    return resid + low_back(channel_mix(act_mid, low(mixer)))

def encode(params, x_in):
    stem, strides, blocks, mixers, pre = (params[0], params[1], params[2], params[3], params[4])
    h_one = low_back(conv_op(low(x_in), low(stem), 2, 1, 1))
    a_one = low(jax.nn.gelu(h_one))
    r_zero = low_back(conv_op(a_one, turned(strides[0]), 2, 1, 1))
    r_one = res_block(r_zero, blocks[0], mixers[0])
    return low_back(channel_mix(low(jax.nn.gelu(r_one)), low(pre)))

def decode(params, latent_q):
    strides, blocks, mixers, post, head = (params[1], params[2], params[3], params[5], params[7])
    r_two = low_back(channel_mix(low(latent_q), low(post)))
    r_three = res_block(r_two, blocks[1], mixers[1])
    a_three = low(jax.nn.gelu(r_three))
    h_four = low_back(conv_op(a_three, turned(strides[1]), 1, 2, 2))
    a_four = low(jax.nn.gelu(h_four))
    return low_back(conv_op(a_four, low(head), 1, 2, 2))

def image_terms(params, x_in, pix, pix_mask, lat_mask, idx, z_fixed, e_fixed):
    latent = encode(params, x_in)
    entries = jnp.take(params[6], idx, axis=0)
    out = decode(params, latent + (e_fixed - z_fixed))
    bits = pixel_bits(out, pix, pix_mask)
    vq = jnp.sum(lat_mask[..., None] * ((z_fixed - entries) ** 2 + beta_commit * (latent - e_fixed) ** 2))
    return (bits, vq)

def adam(weight, moment, second, grad, rate):
    m_new = beta_one * moment + (1.0 - beta_one) * grad
    v_new = beta_two * second + (1.0 - beta_two) * grad * grad
    m_hat = m_new / (1.0 - beta_one ** STEP)
    v_hat = v_new / (1.0 - beta_two ** STEP)
    return (weight - rate * (m_hat / (jnp.sqrt(v_hat) + adam_eps) + decay_rate * weight), m_new, v_new)

def reference(pixels, image_sizes, code_indices, stem_kernel, stride_kernels, block_kernels, block_mixers, pre_project, post_project, codebook, head_kernel, first_stem, first_stride, first_block, first_mixer, first_pre, first_post, first_codes, first_head, second_stem, second_stride, second_block, second_mixer, second_pre, second_post, second_codes, second_head):
    params = (stem_kernel, stride_kernels, block_kernels, block_mixers, pre_project, post_project, codebook, head_kernel)
    firsts = (first_stem, first_stride, first_block, first_mixer, first_pre, first_post, first_codes, first_head)
    seconds = (second_stem, second_stride, second_block, second_mixer, second_pre, second_post, second_codes, second_head)
    pixels_last = jnp.transpose(pixels, (0, 2, 3, 1))
    pix_mask, lat_mask = valid_masks(image_sizes, S)
    pix_total = 3.0 * jnp.sum(pix_mask)
    lat_total = E * jnp.sum(lat_mask)

    def one_image(carry, item):
        grads, bits_sum, vq_sum = carry
        pix, pmask, lmask, idx = item
        x_in = (pmask[..., None] * (pix.astype(jnp.float32) / 127.5 - 1.0))[None]
        z_fixed = encode(params, x_in)
        e_fixed = jnp.take(codebook, idx, axis=0)[None]

        def terms(p):
            return image_terms(p, x_in, pix[None], pmask[None], lmask[None], idx[None], z_fixed, e_fixed)
        (bits, vq), pull = jax.vjp(terms, params)
        got = pull((1.0 / pix_total, 1.0 / lat_total))[0]
        grads = jax.tree.map(lambda a, b: a + b, grads, got)
        return ((grads, bits_sum + bits, vq_sum + vq), None)
    zeros = jax.tree.map(jnp.zeros_like, params)
    start = (zeros, jnp.zeros((), jnp.float32), jnp.zeros((), jnp.float32))
    (grads, bits_sum, vq_sum), unused = lax.scan(one_image, start, (pixels_last, pix_mask, lat_mask, code_indices))
    total = jnp.zeros((), jnp.float32)
    for grad in grads:
        total = total + jnp.sum(grad * grad)
    norm = jnp.sqrt(total)
    factor = jnp.minimum(1.0, clip_norm / (norm + 1e-06))
    rates = (48.0 ** (-0.5), (16.0 * C) ** (-0.5), (9.0 * C) ** (-0.5), C ** (-0.5), C ** (-0.5), E ** (-0.5), 0.6, (4.0 * C) ** (-0.5))
    news = [adam(params[i], firsts[i], seconds[i], factor * grads[i], rates[i]) for i in range(8)]
    loss_terms = jnp.stack([bits_sum, pix_total, vq_sum, lat_total])
    return (loss_terms, norm, news[0][0], news[1][0], news[2][0], news[3][0], news[4][0], news[5][0], news[6][0], news[7][0], news[0][1], news[1][1], news[2][1], news[3][1], news[4][1], news[5][1], news[6][1], news[7][1], news[0][2], news[1][2], news[2][2], news[3][2], news[4][2], news[5][2], news[6][2], news[7][2])
```

```python
import math

import jax
import jax.numpy as jnp
from jax import lax
from jax.experimental import pallas as pl
from jax.experimental.pallas import tpu as pltpu
from jax.sharding import PartitionSpec as P

C = 256
E = 64
STEP = 10
SIDE = 32
CELLS = SIDE * SIDE
PADDED = CELLS + 2 * SIDE

beta_commit = 0.25
clip_norm = 0.002
beta_one = 0.9
beta_two = 0.999
adam_eps = 1e-08
decay_rate = 0.01
half_bin = 1.0 / 255.0
root_half = 0.7071067811865476
gelu_root = 0.7978845608028654
gelu_cube = 0.044715

F32 = jnp.float32
BF16 = jnp.bfloat16

UP_SHIFT = (-1, 0, 0, 1)
DOWN_PARITY = (1, 0, 1, 0)
DOWN_SHIFT = (-1, 0, 0, 1)


def nn(left, right):
    return lax.dot_general(left, right, (((1,), (0,)), ((), ())), preferred_element_type=F32)


def nt(left, right):
    return lax.dot_general(left, right, (((1,), (1,)), ((), ())), preferred_element_type=F32)


def gelu(x):
    return x * (0.5 * (1.0 + jnp.tanh(gelu_root * (x + gelu_cube * (x * x * x)))))


def gelu_slope(x):
    square = x * x
    t = jnp.tanh(gelu_root * (x + gelu_cube * (x * square)))
    return 0.5 * (1.0 + t) + (0.5 * gelu_root) * x * (1.0 - t * t) * (
        1.0 + 3.0 * gelu_cube * square
    )


def columns(shape):
    return lax.broadcasted_iota(jnp.int32, shape, 0) % SIDE


def left_of(x):
    return jnp.where(columns(x.shape) == 0, 0.0, pltpu.roll(x, 1, 0))


def right_of(x):
    return jnp.where(columns(x.shape) == SIDE - 1, 0.0, pltpu.roll(x, x.shape[0] - 1, 0))


def clear_edges(ref, index):
    edge = jnp.zeros((SIDE, C), BF16)
    ref[index, 0:SIDE, :] = edge
    ref[index, PADDED - SIDE : PADDED, :] = edge


def store_three(ref, x):
    for index in range(3):
        clear_edges(ref, index)
    ref[0, SIDE : SIDE + CELLS, :] = left_of(x).astype(BF16)
    ref[1, SIDE : SIDE + CELLS, :] = x.astype(BF16)
    ref[2, SIDE : SIDE + CELLS, :] = right_of(x).astype(BF16)


def store_two(ref, phase, x):
    clear_edges(ref, 2 * phase)
    clear_edges(ref, 2 * phase + 1)
    moved = right_of(x) if phase % 2 == 0 else left_of(x)
    ref[2 * phase, SIDE : SIDE + CELLS, :] = x.astype(BF16)
    ref[2 * phase + 1, SIDE : SIDE + CELLS, :] = moved.astype(BF16)


def window(ref, index, shift):
    return ref[index, (shift + 1) * SIDE : (shift + 1) * SIDE + CELLS, :]


def three(ref, row_shift, col_shift):
    return window(ref, col_shift + 1, row_shift)


def two(ref, phase, row_shift, col_shift):
    return window(ref, 2 * phase + (0 if col_shift == 0 else 1), row_shift)


def own_lanes(x, tensor):
    half = jnp.where(tensor >= 2, x[:, 128:256], x[:, 0:128])
    return jnp.where(tensor % 2 == 1, pltpu.roll(half, 64, 1), half)[:, 0:64]


def lane_grid(shape):
    lane = lax.broadcasted_iota(jnp.int32, shape, 1)
    return lane // SIDE, lane % SIDE


def moved_plane(x, row_shift, col_shift):
    if row_shift == 0 and col_shift == 0:
        return x
    y = pltpu.roll(x, (-(SIDE * row_shift + col_shift)) % CELLS, 1)
    rows, cols = lane_grid(x.shape)
    keep = None
    for index, shift in ((rows, row_shift), (cols, col_shift)):
        if shift != 0:
            ok = (index < SIDE - 1) if shift == 1 else (index > 0)
            keep = ok if keep is None else (keep & ok)
    return jnp.where(keep, y, 0.0)


def gather_weight(ref, parts, tensor, count, rotated):
    for k, part in enumerate(parts):
        start = 64 * k if rotated else pl.multiple_of(((tensor + k) % 4) * 64, 64)
        for tap in range(count):
            ref[tap, pl.ds(start, 64), :] = part[tap]


def same_forward(source, weight_ref):
    total = None
    for row in range(3):
        for col in range(3):
            term = nt(three(source, row - 1, col - 1), weight_ref[3 * row + col])
            total = term if total is None else total + term
    return total


def same_backward(source, weight_ref):
    total = None
    for row in range(3):
        for col in range(3):
            term = nn(three(source, 1 - row, 1 - col), weight_ref[3 * row + col])
            total = term if total is None else total + term
    return total


def down_forward(source, weight_ref):
    total = None
    for row in range(4):
        for col in range(4):
            phase = 2 * DOWN_PARITY[row] + DOWN_PARITY[col]
            term = nt(two(source, phase, DOWN_SHIFT[row], DOWN_SHIFT[col]), weight_ref[4 * row + col])
            total = term if total is None else total + term
    return total


def stem_kernel_body(meta, pix_ref, s0, s1, s2, s3, a_ref, x_ref, stem_ref):
    tensor, high, wide = meta[0], meta[1], meta[2]
    rows, cols = lane_grid((8, CELLS))
    inside = (rows < high) & (cols < wide)
    planes = {}
    for pair in range(8):
        value = jnp.where(inside, pix_ref[pair] / 127.5 - 1.0, 0.0)
        row, col = pair // 2, 2 * (pair % 2)
        planes[row, col] = value
        planes[row, col + 1] = pltpu.roll(value, 4, 0)
    for p in range(2):
        for q in range(2):
            for kh in range(4):
                for kw in range(0, 4, 2):
                    blocks = []
                    for w in (kw, kw + 1):
                        r, s = 2 * p + kh - 1, 2 * q + w - 1
                        blocks.append(moved_plane(planes[r % 4, s % 4], r // 4, s // 4))
                    tap = 4 * kh + kw
                    x_ref[8 * tap : 8 * tap + 16, (2 * p + q) * CELLS : (2 * p + q + 1) * CELLS] = (
                        jnp.concatenate(blocks, 0).astype(BF16)
                    )
    for k, part in enumerate((s0, s1, s2, s3)):
        stem_ref[pl.ds(pl.multiple_of(((tensor + k) % 4) * 64, 64), 64), :] = part[:, 0:128]
    for phase in range(4):
        patch = x_ref[:, phase * CELLS : (phase + 1) * CELLS].T
        store_two(a_ref, phase, gelu(nt(patch, stem_ref[...])))


def down_body(meta, a_ref, w0, w1, w2, w3, r_ref, u_ref, w_ref):
    gather_weight(w_ref, (w0, w1, w2, w3), meta[0], 16, False)
    resid = down_forward(a_ref, w_ref)
    r_ref[...] = resid
    store_three(u_ref, gelu(resid))


def block_forward(resid, u_ref, w_ref, mix_ref, v_ref, q_ref):
    inner = same_forward(u_ref, w_ref)
    v_ref[...] = inner
    act = gelu(inner).astype(BF16)
    q_ref[...] = act
    return resid + nn(act, mix_ref[0])


def encode_body(
    meta, r0_ref, u_ref, b0, b1, b2, b3, m0, m1, m2, m3, s0, s1, s2, s3, entries_ref,
    v_ref, q_ref, r1_ref, diff_ref, zq_ref, r2_ref, u2_ref, vq_ref, w_ref, mix_ref, pre_ref, post_ref,
):
    tensor, high, wide = meta[0], meta[1], meta[2]
    gather_weight(w_ref, (b0, b1, b2, b3), tensor, 9, True)
    gather_weight(mix_ref, (m0, m1, m2, m3), tensor, 1, True)
    for k, part in enumerate((s0, s1, s2, s3)):
        rows = pl.ds(pl.multiple_of(((tensor + k) % 4) * 64, 64), 64)
        pre_ref[rows, :] = part[:, 256:320]
        post_ref[rows, :] = part[:, 320:384]
    resid = block_forward(r0_ref[...], u_ref, w_ref, mix_ref, v_ref, q_ref)
    r1_ref[...] = resid
    latent = nn(gelu(resid).astype(BF16), pre_ref[...])
    entries = entries_ref[...]
    diff = latent - entries
    diff_ref[...] = diff
    code = (latent + (entries - latent)).astype(BF16)
    zq_ref[...] = code
    cell = lax.broadcasted_iota(jnp.int32, (CELLS, E), 0)
    inside = (cell // SIDE < high) & (cell % SIDE < wide)
    vq_ref[0, 0] = (1.0 + beta_commit) * jnp.sum(jnp.where(inside, diff * diff, 0.0))
    resid = nt(code, post_ref[...])
    r2_ref[...] = resid
    store_three(u2_ref, gelu(resid))


def decode_body(
    meta, r2_ref, u_ref, b0, b1, b2, b3, m0, m1, m2, m3,
    v_ref, q_ref, r3_ref, u3_ref, w_ref, mix_ref,
):
    tensor = meta[0]
    gather_weight(w_ref, (b0, b1, b2, b3), tensor, 9, True)
    gather_weight(mix_ref, (m0, m1, m2, m3), tensor, 1, True)
    resid = block_forward(r2_ref[...], u_ref, w_ref, mix_ref, v_ref, q_ref)
    r3_ref[...] = resid
    store_three(u3_ref, gelu(resid))


def poly(x, coefs):
    total = jnp.full_like(x, coefs[0])
    for c in coefs[1:]:
        total = total * x + c
    return total


ERFC_LOW = (
    2.326819970068386e-2, -1.387039388740657e-1, 3.687424674597105e-1, -5.824733027278666e-1,
    6.210004621745983e-1, -4.944515323274145e-1, 3.404879937665872e-1, -2.741127028184656e-1,
    5.638259427386472e-1,
)
ERFC_HIGH = (
    -1.047766399936249e1, 1.297719955372516e1, -7.495518717768503e0, 2.921019019210786e0,
    -1.015265279202700e0, 4.218463358204948e-1, -2.820767439740514e-1, 5.641895067754075e-1,
)
ERF_NEAR = (
    7.853861353153693e-5, -8.010193625184903e-4, 5.188327685732524e-3, -2.685381193529856e-2,
    1.128358514861418e-1, -3.761262582423300e-1, 1.128379165726710e0,
)


def erfc(x):
    size = jnp.abs(x)
    square = x * x
    far_exp = jnp.exp(-square)
    recip = 1.0 / jnp.maximum(size, 0.5)
    y = recip * recip
    far = far_exp * recip * jnp.where(size < 2.0, poly(y, ERFC_LOW), poly(y, ERFC_HIGH))
    far = jnp.where(x < 0, 2.0 - far, far)
    near = 1.0 - x * poly(square, ERF_NEAR)
    return jnp.where(size > 1.0, far, near), far_exp


def likelihood(center_out, scale_out, pix, keep, scale):
    target = pix / 127.5 - 1.0
    center = jnp.tanh(center_out)
    decay = jnp.exp(-jnp.abs(scale_out))
    sigma = 0.25 + (jnp.maximum(scale_out, 0.0) + jnp.log(1.0 + decay))
    gate = jnp.where(scale_out >= 0, 1.0, decay) / (1.0 + decay)
    low_end, high_end = pix == 0.0, pix == 255.0
    lower = jnp.where(low_end, -40.0, (target - half_bin - center) / sigma)
    upper = jnp.where(high_end, 40.0, (target + half_bin - center) / sigma)
    right = lower + upper > 0
    tail_a, exp_a = erfc(jnp.where(right, lower, -upper) * root_half)
    tail_b, exp_b = erfc(jnp.where(right, upper, -lower) * root_half)
    mass = 0.5 * (tail_a - tail_b)
    bits = jnp.where(keep, jnp.log(mass), 0.0)
    density = 1.0 / math.sqrt(2.0 * math.pi)
    slope = jnp.where(keep, scale * density / mass, 0.0)
    low_slope = jnp.where(low_end, 0.0, -slope * jnp.where(right, exp_a, exp_b))
    high_slope = jnp.where(high_end, 0.0, slope * jnp.where(right, exp_b, exp_a))
    center_grad = -(low_slope + high_slope) / sigma
    sigma_grad = -(low_slope * lower + high_slope * upper) / sigma
    return bits, center_grad * (1.0 - center * center), sigma_grad * gate


def head_links():
    for p in range(2):
        for q in range(2):
            for kh in range(4):
                for kw in range(4):
                    up, left = p + UP_SHIFT[kh], q + UP_SHIFT[kw]
                    out = (2 * p + kh % 2, 2 * q + kw % 2)
                    yield out, 4 * kh + kw, 2 * (up % 2) + left % 2, up // 2, left // 2


def block_backward(grad_out, resid_ref, u_ref, v_ref, q_ref, w_ref, mix_ref, dv_ref, g_ref):
    low = grad_out.astype(BF16)
    own_q = q_ref[:, 0:128].astype(F32).T[0:64].astype(BF16)
    g_ref[576:640, :] = nn(own_q, low)
    mid = nt(low, mix_ref[0])
    inner = gelu_slope(v_ref[...]) * mid
    store_three(dv_ref, inner)
    own = inner[:, 0:128].T[0:64].astype(BF16)
    for row in range(3):
        for col in range(3):
            tap = 3 * row + col
            g_ref[64 * tap : 64 * tap + 64, :] = nn(own, three(u_ref, row - 1, col - 1))
    return grad_out + gelu_slope(resid_ref[...]) * same_backward(dv_ref, w_ref)


def decode_back_body(
    meta, total_ref, pix_ref, r3_ref, u3_ref, w0, w1, w2, w3, s0, s1, s2, s3,
    r2_ref, u2_ref, v1_ref, q1_ref, w1_ref, mix_ref, zq_ref, post_ref,
    bits_ref, g_ref, gb_ref, gs_ref, back_ref,
    w_ref, h4_ref, a4_ref, head_ref, prod_ref, q_ref, dh_ref, dv_ref,
):
    tensor, high, wide = meta[0], meta[1], meta[2]
    gather_weight(w_ref, (w0, w1, w2, w3), tensor, 16, True)
    for k, part in enumerate((s0, s1, s2, s3)):
        head_ref[64 * k : 64 * k + 64, :] = part[:, 128:256]
    head = head_ref[...].astype(F32).T.astype(BF16)
    for p in range(2):
        for q in range(2):
            phase = 2 * p + q
            total = None
            for kh in (p, p + 2):
                for kw in (q, q + 2):
                    term = nt(three(u3_ref, UP_SHIFT[kh], UP_SHIFT[kw]), w_ref[4 * kh + kw])
                    total = term if total is None else total + term
            h4_ref[phase] = total
            act = gelu(total).astype(BF16)
            a4_ref[phase] = act
            prod_ref[:, phase * CELLS : (phase + 1) * CELLS] = nt(head, act)
    outs = {}
    for out, tap, phase, up, left in head_links():
        term = moved_plane(
            prod_ref[8 * tap : 8 * tap + 8, phase * CELLS : (phase + 1) * CELLS], up, left
        )
        outs[out] = term if out not in outs else outs[out] + term
    sub = lax.broadcasted_iota(jnp.int32, (8, CELLS), 0)
    rows, cols = lane_grid((8, CELLS))
    keep = (rows < high) & (cols < wide) & (sub % 4 != 3)
    first = sub < 4
    scale = -1.0 / (math.log(2.0) * 48.0 * total_ref[0])
    grads = {}
    bits = None
    for pair in range(8):
        row, col = pair // 2, 2 * (pair % 2)
        one, other = outs[row, col], outs[row, col + 1]
        centers = jnp.where(first, one, pltpu.roll(other, 4, 0))
        scales = jnp.where(first, pltpu.roll(one, 4, 0), other)
        part, center_grad, scale_grad = likelihood(centers, scales, pix_ref[pair], keep, scale)
        bits = part if bits is None else bits + part
        grads[row, col] = jnp.where(first, center_grad, pltpu.roll(scale_grad, 4, 0))
        grads[row, col + 1] = jnp.where(first, pltpu.roll(center_grad, 4, 0), scale_grad)
    bits_ref[0, 0] = -jnp.sum(bits) / math.log(2.0)
    found = {}
    for out, tap, phase, up, left in head_links():
        found[tap, phase] = moved_plane(grads[out], -up, -left)
    for phase in range(4):
        for tap in range(0, 16, 2):
            q_ref[8 * tap : 8 * tap + 16, phase * CELLS : (phase + 1) * CELLS] = jnp.concatenate(
                [found[tap, phase], found[tap + 1, phase]], 0
            ).astype(BF16)
    head_grad = None
    for phase in range(4):
        spread = q_ref[:, phase * CELLS : (phase + 1) * CELLS]
        term = nn(spread, a4_ref[phase, :, 0:64])
        head_grad = term if head_grad is None else head_grad + term
        slope = gelu_slope(h4_ref[phase]) * nn(spread.T, head)
        store_two(dh_ref, phase, slope)
        own = slope[:, 0:128].T[0:64].astype(BF16)
        for kh in (phase // 2, phase // 2 + 2):
            for kw in (phase % 2, phase % 2 + 2):
                tap = 4 * kh + kw
                g_ref[64 * tap : 64 * tap + 64, :] = nn(own, three(u3_ref, UP_SHIFT[kh], UP_SHIFT[kw]))
    total = None
    for kh in range(4):
        for kw in range(4):
            phase = 2 * (kh % 2) + kw % 2
            term = nn(two(dh_ref, phase, -UP_SHIFT[kh], -UP_SHIFT[kw]), w_ref[4 * kh + kw])
            total = term if total is None else total + term
    grad = gelu_slope(r3_ref[...]) * total
    grad = block_backward(grad, r2_ref, u2_ref, v1_ref, q1_ref, w1_ref, mix_ref, dv_ref, gb_ref)
    low = grad.astype(BF16)
    post_grad = nn(zq_ref[...].astype(F32).T.astype(BF16), own_lanes(grad, tensor).astype(BF16))
    gs_ref[...] = jnp.concatenate([post_grad, head_grad[0:64], head_grad[64:128]], 1)
    back_ref[...] = nn(low, post_ref[...])


def split_three(x):
    first = x.astype(BF16)
    rest = x - first.astype(F32)
    second = rest.astype(BF16)
    return first, second, (rest - second.astype(F32)).astype(BF16)


def encode_back_body(
    meta, total_ref, back_ref, diff_ref, codes_ref, r1_ref, pre_ref, s0, x_ref, a_ref,
    r0_ref, u_ref, v_ref, q_ref, wb_ref, mix_ref, w_ref,
    g_ref, gb_ref, gs_ref, gc_ref,
    dv_ref, dr_ref,
):
    tensor, high, wide = meta[0], meta[1], meta[2]
    cell = lax.broadcasted_iota(jnp.int32, (CELLS, E), 0)
    inside = (cell // SIDE < high) & (cell % SIDE < wide)
    scaled = jnp.where(inside, diff_ref[...] / (64.0 * total_ref[0]), 0.0)
    dz = (back_ref[...] + 2.0 * beta_commit * scaled).astype(BF16)
    hot = (lax.broadcasted_iota(jnp.int32, (512, CELLS), 0) == codes_ref[...]).astype(F32).astype(BF16)
    found = [nn(hot, part) for part in split_three(-2.0 * scaled)]
    codes = found[0] + (found[1] + found[2])
    gc_ref[...] = jnp.concatenate([codes[128 * b : 128 * b + 128] for b in range(4)], 1)
    resid = r1_ref[...]
    act = own_lanes(gelu(resid), tensor)
    pre_grad = nn(act.T.astype(BF16), dz)
    grad = gelu_slope(resid) * nt(dz, pre_ref[...])
    grad = block_backward(grad, r0_ref, u_ref, v_ref, q_ref, wb_ref, mix_ref, dv_ref, gb_ref)
    store_three(dr_ref, grad)
    own = own_lanes(grad, tensor).T.astype(BF16)
    for kh in range(4):
        for kw in range(4):
            tap = 4 * kh + kw
            phase = 2 * DOWN_PARITY[kh] + DOWN_PARITY[kw]
            g_ref[64 * tap : 64 * tap + 64, :] = nn(own, two(a_ref, phase, DOWN_SHIFT[kh], DOWN_SHIFT[kw]))
    stem_grad = None
    for phase in range(4):
        total = None
        for kh in range(4):
            for kw in range(4):
                if 2 * DOWN_PARITY[kh] + DOWN_PARITY[kw] == phase:
                    term = nn(three(dr_ref, -DOWN_SHIFT[kh], -DOWN_SHIFT[kw]), w_ref[4 * kh + kw])
                    total = term if total is None else total + term
        patch = x_ref[:, phase * CELLS : (phase + 1) * CELLS]
        before = nt(patch.T, s0[:, 0:128])
        slope = (gelu_slope(before) * own_lanes(total, tensor)).astype(BF16)
        term = nn(patch, slope)
        stem_grad = term if stem_grad is None else stem_grad + term
    gs_ref[...] = jnp.concatenate([pre_grad, stem_grad[0:64], stem_grad[64:128]], 1)


SMEM = pl.BlockSpec(memory_space=pltpu.SMEM)
VMEM = pl.BlockSpec(memory_space=pltpu.VMEM)


def run_kernel(name, body, scalars, arrays, outs, scratch=()):
    shapes = [jax.ShapeDtypeStruct(*(o or ((1, 1), F32))) for o in outs]
    return pl.pallas_call(
        body,
        out_shape=shapes,
        in_specs=[SMEM] * len(scalars) + [VMEM] * len(arrays),
        out_specs=[SMEM if o is None else VMEM for o in outs],
        scratch_shapes=[pltpu.VMEM(*s) for s in scratch],
        compiler_params=pltpu.CompilerParams(vmem_limit_bytes=58 * 2**20),
        name=name,
    )(*scalars, *arrays)


THREE = ((3, PADDED, C), BF16)
EIGHT = ((8, PADDED, C), BF16)
WIDE = ((CELLS, C), F32)
WIDE_LOW = ((CELLS, C), BF16)
NINE = ((9, C, C), BF16)
ONE = ((1, C, C), BF16)
SIXTEEN = ((16, C, C), BF16)


def image_step(meta, cell_total, pix, code_row, entries, small, stride0, stride1, block0, block1, mix0, mix1):
    av, xt = run_kernel("stem", stem_kernel_body, (meta,), (pix, *small), (EIGHT, ((128, 4 * CELLS), BF16)), (((C, 128), BF16),))
    r0, u0, w0 = run_kernel("down", down_body, (meta,), (av, *stride0), (WIDE, THREE, SIXTEEN))
    v0, q0, r1, diff, zq, r2, u2, vq, wb0, mx0, pre, post = run_kernel(
        "encode", encode_body, (meta,), (r0, u0, *block0, *mix0, *small, entries),
        (WIDE, WIDE_LOW, WIDE, ((CELLS, E), F32), ((CELLS, E), BF16), WIDE, THREE, None, NINE, ONE, ((C, E), BF16), ((C, E), BF16)),
    )
    v1, q1, r3, u3, wb1, mx1 = run_kernel(
        "decode", decode_body, (meta,), (r2, u2, *block1, *mix1), (WIDE, WIDE_LOW, WIDE, THREE, NINE, ONE)
    )
    bits, g1, gb1, gs1, back = run_kernel(
        "decode_back", decode_back_body, (meta, cell_total),
        (pix, r3, u3, *stride1, *small, r2, u2, v1, q1, wb1, mx1, zq, post),
        (None, ((1024, C), F32), ((640, C), F32), ((64, 192), F32), ((CELLS, E), F32)),
        (SIXTEEN, ((4, CELLS, C), F32), ((4, CELLS, C), BF16), ((C, 128), BF16), ((128, 4 * CELLS), F32), ((128, 4 * CELLS), BF16), EIGHT, THREE),
    )
    g0, gb0, gs0, gc = run_kernel(
        "encode_back", encode_back_body, (meta, cell_total),
        (back, diff, code_row, r1, pre, small[0], xt, av, r0, u0, v0, q0, wb0, mx0, w0),
        (((1024, C), F32), ((640, C), F32), ((64, 192), F32), ((128, C), F32)),
        (THREE, THREE),
    )
    return bits, vq, g0, gb0, gs0, gc, g1, gb1, gs1


def adam(weight, moment, second, grad, rate):
    m_new = beta_one * moment + (1.0 - beta_one) * grad
    v_new = beta_two * second + (1.0 - beta_two) * grad * grad
    m_hat = m_new / (1.0 - beta_one**STEP)
    v_hat = v_new / (1.0 - beta_two**STEP)
    return (
        weight - rate * (m_hat / (jnp.sqrt(v_hat) + adam_eps) + decay_rate * weight),
        m_new,
        v_new,
    )


def from_neighbours(local):
    return [local] + [
        lax.ppermute(local, "tensor", [((j + k) % 4, j) for j in range(4)]) for k in (1, 2, 3)
    ]


def on_device(
    pixels,
    image_sizes,
    code_indices,
    stem_kernel,
    stride_kernels,
    block_kernels,
    block_mixers,
    pre_project,
    post_project,
    codebook,
    head_kernel,
    *moments,
):
    firsts, seconds = moments[:8], moments[8:]
    params = (
        stem_kernel,
        stride_kernels,
        block_kernels,
        block_mixers,
        pre_project,
        post_project,
        codebook,
        head_kernel,
    )
    tensor = lax.axis_index("tensor")
    stem = jnp.pad(stem_kernel, ((0, 0), (0, 0), (0, 5), (0, 0))).reshape(128, 64).T
    head = head_kernel.reshape(16, 64, 2, 3).transpose(1, 0, 2, 3)
    head = jnp.pad(head, ((0, 0), (0, 0), (0, 0), (0, 1))).reshape(64, 128)
    small = jnp.concatenate([stem, head, pre_project, post_project.T], 1).astype(BF16)
    small = from_neighbours(small)
    stride0 = from_neighbours(stride_kernels[0].reshape(16, 64, C).astype(BF16))
    block0 = from_neighbours(block_kernels[0].reshape(9, 64, C).astype(BF16))
    mix0 = from_neighbours(block_mixers[0].reshape(1, 64, C).astype(BF16))
    block1 = from_neighbours(block_kernels[1].reshape(9, 64, C).astype(BF16))
    mix1 = from_neighbours(block_mixers[1].reshape(1, 64, C).astype(BF16))
    stride1 = from_neighbours(stride_kernels[1].reshape(16, 64, C).astype(BF16))
    pix = pixels.reshape(3, SIDE, 4, SIDE, 4).transpose(2, 4, 0, 1, 3)
    pix = jnp.pad(pix, ((0, 0), (0, 0), (0, 1), (0, 0), (0, 0))).reshape(8, 8, CELLS).astype(F32)
    quarters = image_sizes[0] // 4
    meta = jnp.concatenate([tensor[None].astype(jnp.int32), quarters])
    cells = (quarters[0] * quarters[1]).astype(F32)
    cell_total = lax.psum(cells[None], "dp")
    code_row = code_indices.reshape(1, CELLS)
    entries = jnp.take(codebook, code_row[0], axis=0)
    bits, vq, g0, gb0, gs0, gc, g1, gb1, gs1 = image_step(
        meta, cell_total, pix, code_row, entries, small, stride0, stride1, block0, block1, mix0, mix1
    )
    bits, vq, g0, gb0, gs0, gc, g1, gb1, gs1 = lax.psum(
        (bits, vq, g0, gb0, gs0, gc, g1, gb1, gs1), "dp"
    )
    stem_grad = jnp.concatenate([gs0[:, 64:128], gs0[:, 128:192]], 0).reshape(4, 4, 8, 64)[:, :, 0:3]
    head_grad = jnp.concatenate([gs1[:, 64:128], gs1[:, 128:192]], 0).reshape(4, 4, 2, 4, 64)
    head_grad = head_grad[:, :, :, 0:3].reshape(4, 4, 6, 64).transpose(0, 1, 3, 2)
    code_grad = jnp.concatenate([gc[:, 64 * b : 64 * b + 64] for b in range(4)], 0)
    grads = (
        stem_grad,
        jnp.stack([g0, g1]).reshape(2, 4, 4, 64, C),
        jnp.stack([gb0[0:576], gb1[0:576]]).reshape(2, 3, 3, 64, C),
        jnp.stack([gb0[576:640], gb1[576:640]]),
        gs0[:, 0:64],
        gs1[:, 0:64],
        code_grad,
        head_grad,
    )
    own = jnp.zeros((), F32)
    for index in range(8):
        weight_share = 0.25 if index == 6 else 1.0
        own = own + weight_share * jnp.sum(grads[index] * grads[index])
    norm = jnp.sqrt(lax.psum(own, "tensor"))
    factor = jnp.minimum(1.0, clip_norm / (norm + 1e-06))
    rates = (
        48.0 ** (-0.5),
        (16.0 * C) ** (-0.5),
        (9.0 * C) ** (-0.5),
        C ** (-0.5),
        C ** (-0.5),
        E ** (-0.5),
        0.6,
        (4.0 * C) ** (-0.5),
    )
    news = [adam(params[i], firsts[i], seconds[i], factor * grads[i], rates[i]) for i in range(8)]
    loss_terms = jnp.stack([bits[0, 0], 48.0 * cell_total[0], vq[0, 0], 64.0 * cell_total[0]])
    return (loss_terms, norm, *(n[0] for n in news), *(n[1] for n in news), *(n[2] for n in news))


def solution(mesh):
    in_specs = (
        P("dp", None, None, None),
        P("dp", None),
        P("dp", None, None),
        P(None, None, None, "tensor"),
        P(None, None, None, "tensor", None),
        P(None, None, None, "tensor", None),
        P(None, "tensor", None),
        P("tensor", None),
        P(None, "tensor"),
        P(),
        P(None, None, "tensor", None),
        P(None, None, None, "tensor"),
        P(None, None, None, "tensor", None),
        P(None, None, None, "tensor", None),
        P(None, "tensor", None),
        P("tensor", None),
        P(None, "tensor"),
        P(),
        P(None, None, "tensor", None),
        P(None, None, None, "tensor"),
        P(None, None, None, "tensor", None),
        P(None, None, None, "tensor", None),
        P(None, "tensor", None),
        P("tensor", None),
        P(None, "tensor"),
        P(),
        P(None, None, "tensor", None),
    )
    out_specs = (
        P(),
        P(),
        P(None, None, None, "tensor"),
        P(None, None, None, "tensor", None),
        P(None, None, None, "tensor", None),
        P(None, "tensor", None),
        P("tensor", None),
        P(None, "tensor"),
        P(),
        P(None, None, "tensor", None),
        P(None, None, None, "tensor"),
        P(None, None, None, "tensor", None),
        P(None, None, None, "tensor", None),
        P(None, "tensor", None),
        P("tensor", None),
        P(None, "tensor"),
        P(),
        P(None, None, "tensor", None),
        P(None, None, None, "tensor"),
        P(None, None, None, "tensor", None),
        P(None, None, None, "tensor", None),
        P(None, "tensor", None),
        P("tensor", None),
        P(None, "tensor"),
        P(),
        P(None, None, "tensor", None),
    )
    return jax.shard_map(
        on_device, mesh=mesh, in_specs=in_specs, out_specs=out_specs, check_vma=False
    )
```

```python
import math

import jax
import jax.numpy as jnp
from jax import lax
from jax.experimental import pallas as pl
from jax.experimental.pallas import tpu as pltpu
from jax.sharding import PartitionSpec as P

C = 256
E = 64
STEP = 10
SIDE = 32
CELLS = SIDE * SIDE
PADDED = CELLS + 2 * SIDE

beta_commit = 0.25
clip_norm = 0.002
beta_one = 0.9
beta_two = 0.999
adam_eps = 1e-08
decay_rate = 0.01
half_bin = 1.0 / 255.0
root_half = 0.7071067811865476
gelu_root = 0.7978845608028654
gelu_cube = 0.044715

F32 = jnp.float32
BF16 = jnp.bfloat16

UP_SHIFT = (-1, 0, 0, 1)
DOWN_PARITY = (1, 0, 1, 0)
DOWN_SHIFT = (-1, 0, 0, 1)


def nn(left, right):
    return lax.dot_general(left, right, (((1,), (0,)), ((), ())), preferred_element_type=F32)


def nt(left, right):
    return lax.dot_general(left, right, (((1,), (1,)), ((), ())), preferred_element_type=F32)


def gelu(x):
    return x * (0.5 * (1.0 + jnp.tanh(gelu_root * (x + gelu_cube * (x * x * x)))))


def gelu_slope(x):
    square = x * x
    t = jnp.tanh(gelu_root * (x + gelu_cube * (x * square)))
    return 0.5 * (1.0 + t) + (0.5 * gelu_root) * x * (1.0 - t * t) * (
        1.0 + 3.0 * gelu_cube * square
    )


def columns(shape):
    return lax.broadcasted_iota(jnp.int32, shape, 0) % SIDE


def left_of(x):
    return jnp.where(columns(x.shape) == 0, 0.0, pltpu.roll(x, 1, 0))


def right_of(x):
    return jnp.where(columns(x.shape) == SIDE - 1, 0.0, pltpu.roll(x, x.shape[0] - 1, 0))


def clear_edges(ref, index):
    edge = jnp.zeros((SIDE, C), BF16)
    ref[index, 0:SIDE, :] = edge
    ref[index, PADDED - SIDE : PADDED, :] = edge


def store_three(ref, x):
    for index in range(3):
        clear_edges(ref, index)
    ref[0, SIDE : SIDE + CELLS, :] = left_of(x).astype(BF16)
    ref[1, SIDE : SIDE + CELLS, :] = x.astype(BF16)
    ref[2, SIDE : SIDE + CELLS, :] = right_of(x).astype(BF16)


def store_two(ref, phase, x):
    clear_edges(ref, 2 * phase)
    clear_edges(ref, 2 * phase + 1)
    moved = right_of(x) if phase % 2 == 0 else left_of(x)
    ref[2 * phase, SIDE : SIDE + CELLS, :] = x.astype(BF16)
    ref[2 * phase + 1, SIDE : SIDE + CELLS, :] = moved.astype(BF16)


def window(ref, index, shift):
    return ref[index, (shift + 1) * SIDE : (shift + 1) * SIDE + CELLS, :]


def three(ref, row_shift, col_shift):
    return window(ref, col_shift + 1, row_shift)


def two(ref, phase, row_shift, col_shift):
    return window(ref, 2 * phase + (0 if col_shift == 0 else 1), row_shift)


def own_lanes(x, tensor):
    half = jnp.where(tensor >= 2, x[:, 128:256], x[:, 0:128])
    return jnp.where(tensor % 2 == 1, pltpu.roll(half, 64, 1), half)[:, 0:64]


def lane_grid(shape):
    lane = lax.broadcasted_iota(jnp.int32, shape, 1)
    return lane // SIDE, lane % SIDE


def moved_plane(x, row_shift, col_shift):
    if row_shift == 0 and col_shift == 0:
        return x
    y = pltpu.roll(x, (-(SIDE * row_shift + col_shift)) % CELLS, 1)
    rows, cols = lane_grid(x.shape)
    keep = None
    for index, shift in ((rows, row_shift), (cols, col_shift)):
        if shift != 0:
            ok = (index < SIDE - 1) if shift == 1 else (index > 0)
            keep = ok if keep is None else (keep & ok)
    return jnp.where(keep, y, 0.0)


STRIDE0_ROWS = [(64 * t + 96 * (t // 8), t // 8, 64 * (t % 8) + 96 * (t // 8)) for t in range(16)]
BLOCK_ROWS = [(64 * t, t // 10, 64 * (t % 10)) for t in range(20)]
SMALL_ROW = 512


def block_of(part, row):
    return part[row // 64] if len(part.shape) == 3 else part[row : row + 64, :]


def gather_weight(ref, parts, meta, rows, rotated):
    tensor, core = meta[0], meta[3]
    own, near, far, mine, other = parts
    for part, step in ((own, 0), (near, 1 + 2 * core), (far, 3 - 2 * core)):
        start = 64 * step if rotated else ((tensor + step) % 4) * 64
        if not isinstance(start, int):
            start = pl.multiple_of(start, 64)
        for tap, (row, _, _) in enumerate(rows):
            ref[tap, pl.ds(start, 64), :] = block_of(part, row)
    start = 128 if rotated else pl.multiple_of(((tensor + 2) % 4) * 64, 64)
    for same, part in ((0, mine), (1, other)):

        @pl.when(core == same)
        def _():
            for tap, (_, half, row) in enumerate(rows):
                if half == 0:
                    ref[tap, pl.ds(start, 64), :] = block_of(part, row)

        @pl.when(core != same)
        def _():
            for tap, (_, half, row) in enumerate(rows):
                if half == 1:
                    ref[tap, pl.ds(start, 64), :] = block_of(part, row)


def same_forward(source, weight_ref):
    total = None
    for row in range(3):
        for col in range(3):
            term = nt(three(source, row - 1, col - 1), weight_ref[3 * row + col])
            total = term if total is None else total + term
    return total


def same_backward(source, weight_ref):
    total = None
    for row in range(3):
        for col in range(3):
            term = nn(three(source, 1 - row, 1 - col), weight_ref[3 * row + col])
            total = term if total is None else total + term
    return total


def down_forward(source, weight_ref):
    total = None
    for row in range(4):
        for col in range(4):
            phase = 2 * DOWN_PARITY[row] + DOWN_PARITY[col]
            term = nt(two(source, phase, DOWN_SHIFT[row], DOWN_SHIFT[col]), weight_ref[4 * row + col])
            total = term if total is None else total + term
    return total


def split_three(x):
    first = x.astype(BF16)
    rest = x - first.astype(F32)
    second = rest.astype(BF16)
    return first, second, (rest - second.astype(F32)).astype(BF16)


def one_hot_codes(codes_ref):
    return (
        (lax.broadcasted_iota(jnp.int32, (512, CELLS), 0) == codes_ref[...]).astype(F32).astype(BF16)
    )


def patch_body(
    meta, image_ref, codes_ref, book_ref, pix_out, x_ref, entries_out, pix_ref, entries_ref, sems
):
    high, wide = meta[1], meta[2]
    copies = copy_all(sems, [(pix_ref, pix_out), (entries_ref, entries_out)])
    book = jnp.concatenate(split_three(book_ref[...]), 0)
    found = nn(book, one_hot_codes(codes_ref))
    entries_ref[...] = ((found[0:64] + found[64:128]) + found[128:192]).T
    copies[1].start()
    image = image_ref[...].astype(F32).astype(BF16)
    lane = lax.broadcasted_iota(jnp.int32, (128, CELLS), 1)
    source = lax.broadcasted_iota(jnp.int32, (128, CELLS), 0)
    row = lax.broadcasted_iota(jnp.int32, (384, CELLS), 0)
    own_row = (row // 4) % SIDE == lax.broadcasted_iota(jnp.int32, (384, CELLS), 1) // SIDE
    slot = lax.broadcasted_iota(jnp.int32, (32, 384), 0)
    line = lax.broadcasted_iota(jnp.int32, (32, 384), 1)
    pick = ((line % 4 == slot // 8) & (line // 128 == slot % 8)).astype(F32).astype(BF16)
    planes = {}
    for col in range(4):
        spread = (source == 4 * (lane % SIDE) + col).astype(F32).astype(BF16)
        lined = jnp.where(own_row, nn(image, spread), 0.0).astype(BF16)
        found = nn(pick, lined)
        for r in range(4):
            planes[r, col] = found[8 * r : 8 * r + 8]
    for r in range(4):
        for half in range(2):
            pix_ref[2 * r + half] = planes[r, 2 * half] + pltpu.roll(planes[r, 2 * half + 1], 4, 0)
    copies[0].start()
    rows, cols = lane_grid((8, CELLS))
    channel = lax.broadcasted_iota(jnp.int32, (8, CELLS), 0)
    inside = (rows < high) & (cols < wide) & (channel < 3)
    planes = {key: jnp.where(inside, value / 127.5 - 1.0, 0.0) for key, value in planes.items()}
    moved = {}
    for r in range(-1, 5):
        for c in range(-1, 5):
            moved[r, c] = moved_plane(planes[r % 4, c % 4], r // 4, c // 4)
    for p in range(2):
        for q in range(2):
            for kh in range(4):
                for kw in range(0, 4, 2):
                    r, c = 2 * p + kh - 1, 2 * q + kw - 1
                    tap = 4 * kh + kw
                    x_ref[8 * tap : 8 * tap + 16, (2 * p + q) * CELLS : (2 * p + q + 1) * CELLS] = (
                        jnp.concatenate([moved[r, c], moved[r, c + 1]], 0).astype(BF16)
                    )
    for copy in copies:
        copy.wait()


def pack_stride0_body(meta, stride_ref, stem, head, pre, post, out_ref):
    core = meta[3]
    out_ref[0:512, :] = stride_ref[0:512, :].astype(BF16)
    out_ref[608:1120, :] = stride_ref[512:1024, :].astype(BF16)

    def ordered(x, per):
        count = x.shape[0]
        slot = lax.broadcasted_iota(jnp.int32, (128, count), 0)
        line = lax.broadcasted_iota(jnp.int32, (128, count), 1)
        channel = slot % 8
        if per == 6:
            channel = jnp.where(channel % 4 == 3, per, channel - channel // 4)
        wanted = (slot // 32) * 4 * per + channel * 4 + (slot // 8) % 4
        pick = ((line == wanted) & (channel < per)).astype(F32).astype(BF16)
        return nn(pick, x.astype(BF16)).T

    wide = jnp.concatenate([ordered(stem[...], 3), ordered(head[...], 6)], 1)
    out_ref[512:576, :] = wide.astype(BF16)
    thin = jnp.concatenate([pre[...], post[...].T], 1)
    out_ref[576:608, :] = jnp.concatenate([thin[0:32], thin[32:64]], 1).astype(BF16)


def pack_rest_body(meta, stride_ref, block_ref, mix_ref, blocks_ref, stride1_ref):
    for b in range(2):
        blocks_ref[10 * b : 10 * b + 9] = block_ref[b].astype(BF16)
        blocks_ref[10 * b + 9] = mix_ref[b].astype(BF16)
    stride1_ref[...] = stride_ref[...].astype(BF16)


def block_forward(resid, u_ref, w_ref, v_ref, q_ref):
    inner = same_forward(u_ref, w_ref)
    v_ref[...] = inner
    act = gelu(inner).astype(BF16)
    q_ref[...] = act
    return resid + nn(act, w_ref[9])


def copy_all(sems, pairs):
    return [pltpu.make_async_copy(source, target, sems.at[i]) for i, (source, target) in enumerate(pairs)]


def front_body(
    meta, x_ref, own, near, far, mine, other,
    r_ref, u_ref, a_out, x_out, w_out, stem_out, head_out, pre_out, post_out,
    a_ref, w_ref, stem_ref, head_ref, pre_ref, post_ref, sems,
):
    tensor, core = meta[0], meta[3]
    copies = copy_all(
        sems,
        [(x_ref, x_out), (w_ref, w_out), (stem_ref, stem_out), (head_ref, head_out), (pre_ref, pre_out), (post_ref, post_out)],
    )
    copies += [
        pltpu.make_async_copy(a_ref.at[pl.ds(2 * p, 2)], a_out.at[pl.ds(2 * p, 2)], sems.at[6 + p]) for p in range(4)
    ]
    copies[0].start()
    opposite = pl.multiple_of(512 * (1 - core), 512)
    for part, step, row in (
        (own, 0, SMALL_ROW),
        (near, 1 + 2 * core, SMALL_ROW),
        (far, 3 - 2 * core, SMALL_ROW),
        (mine, 2, opposite),
    ):
        start = pl.multiple_of(((tensor + step) % 4) * 64, 64)
        wide = part[pl.ds(row, 64), :]
        thin = part[pl.ds(row + 64, 32), :]
        stem_ref[pl.ds(start, 64), :] = wide[:, 0:128]
        turned = 64 * step if isinstance(step, int) else pl.multiple_of(64 * step, 64)
        head_ref[pl.ds(turned, 64), :] = wide[:, 128:256]
        for k in range(2):
            rows = pl.ds(start + 32 * k, 32)
            pre_ref[rows, :] = thin[:, 128 * k : 128 * k + 64]
            post_ref[rows, :] = thin[:, 128 * k + 64 : 128 * k + 128]
    gather_weight(w_ref, (own, near, far, mine, other), meta, STRIDE0_ROWS, False)
    for copy in copies[1:6]:
        copy.start()
    for phase in range(4):
        patch = x_ref[:, phase * CELLS : (phase + 1) * CELLS].T
        store_two(a_ref, phase, gelu(nt(patch, stem_ref[...])))
        copies[6 + phase].start()
    resid = down_forward(a_ref, w_ref)
    r_ref[...] = resid
    store_three(u_ref, gelu(resid))
    for copy in copies:
        copy.wait()


def encode_body(
    meta, r0_ref, u_ref, b0, b1, b2, b3, b4, pre_in, post_in, entries_in,
    r2_ref, u2_ref, late_ref, vq_ref, r0_out, u0_out, w_out, v_out, q_out, r1_out, diff_out, zq_out,
    w_ref, v_ref, q_ref, r1_ref, diff_ref, zq_ref, pre_ref, post_ref, entries_ref, sems,
):
    tensor, high, wide = meta[0], meta[1], meta[2]
    copies = copy_all(
        sems,
        [
            (pre_in, pre_ref), (post_in, post_ref), (entries_in, entries_ref), (r0_ref, r0_out), (u_ref, u0_out),
            (w_ref, w_out), (v_ref, v_out), (q_ref, q_out), (r1_ref, r1_out), (diff_ref, diff_out), (zq_ref, zq_out),
        ],
    )
    for copy in copies[0:5]:
        copy.start()
    gather_weight(w_ref, (b0, b1, b2, b3, b4), meta, BLOCK_ROWS[0:10], True)
    copies[5].start()
    resid = block_forward(r0_ref[...], u_ref, w_ref, v_ref, q_ref)
    copies[6].start()
    copies[7].start()
    r1_ref[...] = resid
    copies[8].start()
    for copy in copies[0:3]:
        copy.wait()
    latent = nn(gelu(resid).astype(BF16), pre_ref[...])
    entries = entries_ref[...]
    diff = latent - entries
    diff_ref[...] = diff
    copies[9].start()
    code = (latent + (entries - latent)).astype(BF16)
    zq_ref[...] = code
    copies[10].start()
    cell = lax.broadcasted_iota(jnp.int32, (CELLS, E), 0)
    inside = (cell // SIDE < high) & (cell % SIDE < wide)
    vq_ref[0, 0] = (1.0 + beta_commit) * jnp.sum(jnp.where(inside, diff * diff, 0.0))
    resid = nt(code, post_ref[...])
    r2_ref[...] = resid
    store_three(u2_ref, gelu(resid))
    gather_weight(late_ref, (b0, b1, b2, b3, b4), meta, BLOCK_ROWS[10:20], True)
    for copy in copies[3:]:
        copy.wait()


def poly(x, coefs):
    total = jnp.full_like(x, coefs[0])
    for c in coefs[1:]:
        total = total * x + c
    return total


ERFC_LOW = (
    2.326819970068386e-2, -1.387039388740657e-1, 3.687424674597105e-1, -5.824733027278666e-1,
    6.210004621745983e-1, -4.944515323274145e-1, 3.404879937665872e-1, -2.741127028184656e-1,
    5.638259427386472e-1,
)
ERFC_HIGH = (
    -1.047766399936249e1, 1.297719955372516e1, -7.495518717768503e0, 2.921019019210786e0,
    -1.015265279202700e0, 4.218463358204948e-1, -2.820767439740514e-1, 5.641895067754075e-1,
)
ERF_NEAR = (
    7.853861353153693e-5, -8.010193625184903e-4, 5.188327685732524e-3, -2.685381193529856e-2,
    1.128358514861418e-1, -3.761262582423300e-1, 1.128379165726710e0,
)


def erfc(x):
    size = jnp.abs(x)
    square = x * x
    far_exp = jnp.exp(-square)
    recip = 1.0 / jnp.maximum(size, 0.5)
    y = recip * recip
    far = far_exp * recip * jnp.where(size < 2.0, poly(y, ERFC_LOW), poly(y, ERFC_HIGH))
    far = jnp.where(x < 0, 2.0 - far, far)
    near = 1.0 - x * poly(square, ERF_NEAR)
    return jnp.where(size > 1.0, far, near), far_exp


def likelihood(center_out, scale_out, pix, keep, scale):
    target = pix / 127.5 - 1.0
    center = jnp.tanh(center_out)
    decay = jnp.exp(-jnp.abs(scale_out))
    sigma = 0.25 + (jnp.maximum(scale_out, 0.0) + jnp.log(1.0 + decay))
    gate = jnp.where(scale_out >= 0, 1.0, decay) / (1.0 + decay)
    low_end, high_end = pix == 0.0, pix == 255.0
    lower = jnp.where(low_end, -40.0, (target - half_bin - center) / sigma)
    upper = jnp.where(high_end, 40.0, (target + half_bin - center) / sigma)
    right = lower + upper > 0
    tail_a, exp_a = erfc(jnp.where(right, lower, -upper) * root_half)
    tail_b, exp_b = erfc(jnp.where(right, upper, -lower) * root_half)
    mass = 0.5 * (tail_a - tail_b)
    bits = jnp.where(keep, jnp.log(mass), 0.0)
    density = 1.0 / math.sqrt(2.0 * math.pi)
    slope = jnp.where(keep, scale * density / mass, 0.0)
    low_slope = jnp.where(low_end, 0.0, -slope * jnp.where(right, exp_a, exp_b))
    high_slope = jnp.where(high_end, 0.0, slope * jnp.where(right, exp_b, exp_a))
    center_grad = -(low_slope + high_slope) / sigma
    sigma_grad = -(low_slope * lower + high_slope * upper) / sigma
    return bits, center_grad * (1.0 - center * center), sigma_grad * gate


def head_links():
    for p in range(2):
        for q in range(2):
            for kh in range(4):
                for kw in range(4):
                    up, left = p + UP_SHIFT[kh], q + UP_SHIFT[kw]
                    out = (2 * p + kh % 2, 2 * q + kw % 2)
                    yield out, 4 * kh + kw, 2 * (up % 2) + left % 2, up // 2, left // 2


QUARTER = 448
KINDS = {"stride": (0, 256), "block": (256, 144), "mixer": (400, 16), "codes": (416, 16), "small": (432, 16)}


def store_rows(g_ref, kind, start, value):
    base, size = KINDS[kind]
    done = 0
    while done < value.shape[0]:
        place = start + done
        count = min(size - place % size, value.shape[0] - done)
        first = base + place % size
        g_ref[place // size, first : first + count, :] = value[done : done + count]
        done += count


def with_scalar(x, scalar):
    row = lax.broadcasted_iota(jnp.int32, (64, 64), 0)
    lane = lax.broadcasted_iota(jnp.int32, (64, 64), 1)
    return jnp.concatenate([x, jnp.where((row == 0) & (lane == 0), scalar, 0.0)], 1)


def block_backward(grad_out, resid_ref, u_ref, v_ref, q_ref, w_ref, dv_ref, g_ref):
    low = grad_out.astype(BF16)
    own_q = q_ref[:, 0:128].astype(F32).T[0:64].astype(BF16)
    store_rows(g_ref, "mixer", 0, nn(own_q, low))
    mid = nt(low, w_ref[9])
    inner = gelu_slope(v_ref[...]) * mid
    store_three(dv_ref, inner)
    own = inner[:, 0:128].T[0:64].astype(BF16)
    for row in range(3):
        for col in range(3):
            tap = 3 * row + col
            store_rows(g_ref, "block", 64 * tap, nn(own, three(u_ref, row - 1, col - 1)))
    return grad_out + gelu_slope(resid_ref[...]) * same_backward(dv_ref, w_ref)


def main_body(
    meta, total_ref, vq_ref, r2_ref, u2_ref, w1_ref, own, near, far, mine, other,
    head_in, pix_in, zq_in, post_in, pre_in, codes_in, stem_in, diff_in, r1_in,
    q0_in, v0_in, u0_in, wb_in, r0_in, w0_in, a_in, x_in,
    keep_ref, send_ref,
    w_ref, head_ref, pix_ref, zq_ref, post_ref, pre_ref, codes_ref, stem_ref, diff_ref, r1_ref,
    q0_ref, v0_ref, u0_ref, wb_ref, r0_ref, w0_ref, a_ref, x_ref,
    v1_ref, q1_ref, r3_ref, u3_ref, h4_ref, a4_ref, prod_ref, q_ref, dh_ref, dv_ref,
    back_ref, late_ref, gd_ref, g_ref, sems,
):
    core = meta[3]
    pairs = [(own, w_ref.at[:, 0:64, :])]
    for part, step in ((near, 1 + 2 * core), (far, 3 - 2 * core)):
        pairs.append((part, w_ref.at[:, pl.ds(pl.multiple_of(64 * step, 64), 64), :]))
    for part, half in ((mine, core), (other, 1 - core)):
        pairs.append((part, w_ref.at[pl.ds(8 * half, 8), 128:192, :]))
    pairs += [(head_in, head_ref), (pix_in, pix_ref), (zq_in, zq_ref), (post_in, post_ref)]
    pairs += [(pre_in, pre_ref), (codes_in, codes_ref), (stem_in, stem_ref), (diff_in, diff_ref), (r1_in, r1_ref)]
    pairs += [(q0_in, q0_ref), (v0_in, v0_ref), (u0_in, u0_ref), (wb_in, wb_ref), (r0_in, r0_ref)]
    pairs += [(w0_in, w0_ref), (a_in, a_ref), (x_in, x_ref)]
    copies = copy_all(sems, pairs)
    for copy in copies:
        copy.start()
    r3 = block_forward(r2_ref[...], u2_ref, w1_ref, v1_ref, q1_ref)
    r3_ref[...] = r3
    store_three(u3_ref, gelu(r3))
    for copy in copies[0:7]:
        copy.wait()
    decode_back(
        meta, total_ref, pix_ref, r3_ref, u3_ref, head_ref, r2_ref, u2_ref, v1_ref, q1_ref, w1_ref,
        gd_ref, w_ref, h4_ref, a4_ref, prod_ref, q_ref, dh_ref, dv_ref, zq_ref, post_ref, back_ref, copies[7:9],
    )
    for copy in copies[9:]:
        copy.wait()
    encode_back(
        meta, total_ref, vq_ref, back_ref, diff_ref, codes_ref, r1_ref, pre_ref, stem_ref, x_ref, a_ref,
        r0_ref, u0_ref, v0_ref, q0_ref, wb_ref, w0_ref, gd_ref, keep_ref, send_ref, dv_ref, u3_ref, g_ref, late_ref,
    )


def decode_back(
    meta, total_ref, pix_ref, r3_ref, u3_ref, head_ref, r2_ref, u2_ref, v1_ref, q1_ref, w1_ref,
    g_ref, w_ref, h4_ref, a4_ref, prod_ref, q_ref, dh_ref, dv_ref, zq_ref, post_ref, back_ref, waits,
):
    tensor, high, wide = meta[0], meta[1], meta[2]
    head = head_ref[...].astype(F32).T.astype(BF16)
    for p in range(2):
        for q in range(2):
            phase = 2 * p + q
            total = None
            for kh in (p, p + 2):
                for kw in (q, q + 2):
                    term = nt(three(u3_ref, UP_SHIFT[kh], UP_SHIFT[kw]), w_ref[4 * kh + kw])
                    total = term if total is None else total + term
            h4_ref[phase] = total
            act = gelu(total).astype(BF16)
            a4_ref[phase] = act
            prod_ref[:, phase * CELLS : (phase + 1) * CELLS] = nt(head, act)
    outs = {}
    for out, tap, phase, up, left in head_links():
        term = moved_plane(
            prod_ref[8 * tap : 8 * tap + 8, phase * CELLS : (phase + 1) * CELLS], up, left
        )
        outs[out] = term if out not in outs else outs[out] + term
    sub = lax.broadcasted_iota(jnp.int32, (8, CELLS), 0)
    rows, cols = lane_grid((8, CELLS))
    keep = (rows < high) & (cols < wide) & (sub % 4 != 3)
    first = sub < 4
    scale = -1.0 / (math.log(2.0) * 48.0 * total_ref[0, 0])
    grads = {}
    bits = None
    for pair in range(8):
        row, col = pair // 2, 2 * (pair % 2)
        one, other = outs[row, col], outs[row, col + 1]
        centers = jnp.where(first, one, pltpu.roll(other, 4, 0))
        scales = jnp.where(first, pltpu.roll(one, 4, 0), other)
        part, center_grad, scale_grad = likelihood(centers, scales, pix_ref[pair], keep, scale)
        bits = part if bits is None else bits + part
        grads[row, col] = jnp.where(first, center_grad, pltpu.roll(scale_grad, 4, 0))
        grads[row, col + 1] = jnp.where(first, pltpu.roll(center_grad, 4, 0), scale_grad)
    bits = -jnp.sum(bits) / math.log(2.0)
    found = {}
    for out, tap, phase, up, left in head_links():
        found[tap, phase] = moved_plane(grads[out], -up, -left)
    for phase in range(4):
        for tap in range(0, 16, 2):
            q_ref[8 * tap : 8 * tap + 16, phase * CELLS : (phase + 1) * CELLS] = jnp.concatenate(
                [found[tap, phase], found[tap + 1, phase]], 0
            ).astype(BF16)
    head_grad = None
    for phase in range(4):
        spread = q_ref[:, phase * CELLS : (phase + 1) * CELLS]
        term = nn(spread, a4_ref[phase, :, 0:64])
        head_grad = term if head_grad is None else head_grad + term
        slope = gelu_slope(h4_ref[phase]) * nn(spread.T, head)
        store_two(dh_ref, phase, slope)
        own = slope[:, 0:128].T[0:64].astype(BF16)
        for kh in (phase // 2, phase // 2 + 2):
            for kw in (phase % 2, phase % 2 + 2):
                tap = 4 * kh + kw
                store_rows(g_ref, "stride", 64 * tap, nn(own, three(u3_ref, UP_SHIFT[kh], UP_SHIFT[kw])))
    total = None
    for kh in range(4):
        for kw in range(4):
            phase = 2 * (kh % 2) + kw % 2
            term = nn(two(dh_ref, phase, -UP_SHIFT[kh], -UP_SHIFT[kw]), w_ref[4 * kh + kw])
            total = term if total is None else total + term
    grad = gelu_slope(r3_ref[...]) * total
    grad = block_backward(grad, r2_ref, u2_ref, v1_ref, q1_ref, w1_ref, dv_ref, g_ref)
    for copy in waits:
        copy.wait()
    low = grad.astype(BF16)
    post_grad = nn(zq_ref[...].astype(F32).T.astype(BF16), own_lanes(grad, tensor).astype(BF16))
    small = jnp.concatenate([post_grad, head_grad[0:64], head_grad[64:128]], 1)
    store_rows(g_ref, "small", 0, with_scalar(small, bits))
    store_rows(g_ref, "codes", 0, jnp.zeros((64, C), F32))
    back_ref[...] = nn(low, post_ref[...])


def encode_back(
    meta, total_ref, vq_ref, back_ref, diff_ref, codes_ref, r1_ref, pre_ref, stem_ref, x_ref, a_ref,
    r0_ref, u_ref, v_ref, q_ref, wb_ref, w_ref, gd_ref, keep_ref, send_ref, dv_ref, dr_ref, g_ref, late_ref,
):
    tensor, high, wide = meta[0], meta[1], meta[2]
    cell = lax.broadcasted_iota(jnp.int32, (CELLS, E), 0)
    inside = (cell // SIDE < high) & (cell % SIDE < wide)
    scaled = jnp.where(inside, diff_ref[...] / (64.0 * total_ref[0, 0]), 0.0)
    dz = (back_ref[...] + 2.0 * beta_commit * scaled).astype(BF16)
    hot = one_hot_codes(codes_ref)
    found = nt(jnp.concatenate(split_three((-2.0 * scaled).T), 0), hot)
    codes = (found[0:64] + found[64:128]) + found[128:192]
    store_rows(g_ref, "codes", 0, codes[:, 0:256])
    late_ref[...] = codes[:, 256:512]
    resid = r1_ref[...]
    act = own_lanes(gelu(resid), tensor)
    pre_grad = nn(act.T.astype(BF16), dz)
    grad = gelu_slope(resid) * nt(dz, pre_ref[...])
    grad = block_backward(grad, r0_ref, u_ref, v_ref, q_ref, wb_ref, dv_ref, g_ref)
    store_three(dr_ref, grad)
    own = own_lanes(grad, tensor).T.astype(BF16)
    for kh in range(4):
        for kw in range(4):
            tap = 4 * kh + kw
            phase = 2 * DOWN_PARITY[kh] + DOWN_PARITY[kw]
            term = nn(own, two(a_ref, phase, DOWN_SHIFT[kh], DOWN_SHIFT[kw]))
            store_rows(g_ref, "stride", 64 * tap, term)
    stem_grad = None
    for phase in range(4):
        total = None
        for kh in range(4):
            for kw in range(4):
                if 2 * DOWN_PARITY[kh] + DOWN_PARITY[kw] == phase:
                    term = nn(three(dr_ref, -DOWN_SHIFT[kh], -DOWN_SHIFT[kw]), w_ref[4 * kh + kw])
                    total = term if total is None else total + term
        patch = x_ref[:, phase * CELLS : (phase + 1) * CELLS]
        before = nt(patch.T, stem_ref[pl.ds(pl.multiple_of(64 * tensor, 64), 64), :])
        slope = (gelu_slope(before) * own_lanes(total, tensor)).astype(BF16)
        term = nn(patch, slope)
        stem_grad = term if stem_grad is None else stem_grad + term
    small = jnp.concatenate([pre_grad, stem_grad[0:64], stem_grad[64:128]], 1)
    store_rows(g_ref, "small", 0, with_scalar(small, vq_ref[0, 0]))
    base = KINDS["codes"][0]

    @pl.when(meta[3] == 0)
    def _():
        keep_ref[...] = g_ref[...]
        send_ref[...] = gd_ref[...]
        for part in range(4):
            send_ref[part, base : base + 16, :] = late_ref[16 * part : 16 * part + 16, :]

    @pl.when(meta[3] == 1)
    def _():
        keep_ref[...] = gd_ref[...]
        send_ref[...] = g_ref[...]
        for part in range(4):
            keep_ref[part, base : base + 16, :] = late_ref[16 * part : 16 * part + 16, :]


def add_cores_body(meta, keep_ref, other_ref, *outs):
    for k, out in enumerate(outs):
        part = (meta[4] + k) % 4
        out[...] = keep_ref[part] + other_ref[part]


def join_body(meta, own, other1, other2, other3, half_ref, square_ref):
    row = lax.broadcasted_iota(jnp.int32, (QUARTER, C), 0)
    lane = lax.broadcasted_iota(jnp.int32, (QUARTER, C), 1)
    codes, small = KINDS["codes"][0], KINDS["small"][0]
    share = jnp.where((row >= codes) & (row < small), 0.25, 1.0)
    share = jnp.where((row >= small) & (lane >= 192), 0.0, share)
    total = jnp.zeros((QUARTER, C), F32)
    for k, part in enumerate((own, other1, other2, other3)):
        value = part[...]
        half_ref[(meta[4] + k) % 4] = value
        total = total + value * value
    square_ref[...] = jnp.full((8, 128), jnp.sum(total * share), F32)


def order_body(meta, half_ref, other_ref, stride_ref, block_ref, mix_ref, codes_ref, small_ref):
    def place(first, second):
        for side, ref in enumerate((first, second)):
            for part in range(4):
                for kind, out in (("stride", stride_ref), ("block", block_ref), ("mixer", mix_ref), ("small", small_ref)):
                    base, size = KINDS[kind]
                    out[side, size * part : size * part + size, :] = ref[part, base : base + size, :]
                base, size = KINDS["codes"]
                codes_ref[16 * part : 16 * part + 16, 256 * side : 256 * side + 256] = ref[part, base : base + size, :]

    @pl.when(meta[3] == 0)
    def _():
        place(half_ref, other_ref)

    @pl.when(meta[3] == 1)
    def _():
        place(other_ref, half_ref)


SMEM = pl.BlockSpec(memory_space=pltpu.SMEM)
VMEM = pl.BlockSpec(memory_space=pltpu.VMEM)


def run_kernel(name, body, scalars, arrays, outs, scratch=(), limit=6, sems=0, slab=None, near=True):
    anywhere = pl.BlockSpec(memory_space=pl.ANY)
    shapes, out_specs, specs, given = [], [], [SMEM] * len(scalars), list(scalars)
    for out in outs:
        if out is None:
            shapes.append(pltpu.SMEM((1, 1), F32))
            out_specs.append(SMEM)
        elif out[0] == "far":
            shapes.append(pltpu.HBM(*out[1:]))
            out_specs.append(anywhere)
        else:
            shapes.append(pltpu.VMEM(*out))
            out_specs.append(VMEM)
    for array in arrays:
        if isinstance(array, tuple):
            given.append(array[1])
            specs.append(anywhere)
        else:
            given.append(pltpu.with_memory_space_constraint(array, pltpu.VMEM) if near else array)
            specs.append(VMEM)
    if slab is not None:
        specs[len(scalars)] = pl.BlockSpec((None, *arrays[0].shape[1:]), lambda i: (slab,) + (0,) * (arrays[0].ndim - 1))
    return pl.pallas_call(
        body,
        grid=() if slab is None else (1,),
        out_shape=shapes,
        in_specs=specs,
        out_specs=out_specs,
        scratch_shapes=[pltpu.VMEM(*s) for s in scratch] + ([pltpu.SemaphoreType.DMA((sems,))] if sems else []),
        compiler_params=pltpu.CompilerParams(vmem_limit_bytes=limit * 2**20),
        name=name,
    )(*given)


THREE = ((3, PADDED, C), BF16)
EIGHT = ((8, PADDED, C), BF16)
WIDE = ((CELLS, C), F32)
WIDE_LOW = ((CELLS, C), BF16)
TEN = ((10, C, C), BF16)
THIN = ((CELLS, E), F32)
THIN_LOW = ((CELLS, E), BF16)


def far(*arrays):
    return tuple(("far", array) for array in arrays)


def far_out(*shapes):
    return tuple(("far", *shape) for shape in shapes)


SIXTEEN = ((16, C, C), BF16)


def adam(weight, moment, second, grad, rate):
    m_new = beta_one * moment + (1.0 - beta_one) * grad
    v_new = beta_two * second + (1.0 - beta_two) * grad * grad
    m_hat = m_new / (1.0 - beta_one**STEP)
    v_hat = v_new / (1.0 - beta_two**STEP)
    return (
        weight - rate * (m_hat / (jnp.sqrt(v_hat) + adam_eps) + decay_rate * weight),
        m_new,
        v_new,
    )


BOTH = ("dp", "tensor")


def send(value, target):
    pairs = []
    for x in range(4):
        for z in range(4):
            for core in range(2):
                for y in range(4):
                    to = target(x, z, core, y)
                    pairs.append(
                        (
                            ((x * 4 + z) * 2 + core) * 4 + y,
                            (((to[0] % 4) * 4 + to[1] % 4) * 2 + to[2]) * 4 + to[3] % 4,
                        )
                    )
    return lax.ppermute(value, BOTH, pairs)


def swap_cores(value):
    return send(value, lambda x, z, core, y: (x, z, 1 - core, y))


def along_first(value, k):
    return send(value, lambda x, z, core, y: (x + k, z, core, y) if core == 0 else (x, z + k, core, y))


def along_second(value, k):
    return send(value, lambda x, z, core, y: (x, z + k, core, y) if core == 0 else (x + k, z, core, y))


def along_tensor(value, k):
    return send(value, lambda x, z, core, y: (x, z, core, y + k))


def from_one_side(local):
    return send(local, lambda x, z, core, y: (x, z, core, y - 1 if core == 0 else y + 1))


def from_all(local, near, core, step, count):
    part = lax.dynamic_slice_in_dim(near, core * step, count, 0)
    mine = from_one_side(part)
    return [local, near, swap_cores(near), mine, swap_cores(mine)]


def after(value, *others):
    return lax.optimization_barrier((value, *others))[0]


def on_device(
    pixels,
    image_sizes,
    code_indices,
    stem_kernel,
    stride_kernels,
    block_kernels,
    block_mixers,
    pre_project,
    post_project,
    codebook,
    head_kernel,
    *moments,
):
    firsts, seconds = moments[:8], moments[8:]
    params = (
        stem_kernel,
        stride_kernels,
        block_kernels,
        block_mixers,
        pre_project,
        post_project,
        codebook,
        head_kernel,
    )
    tensor, index = lax.axis_index("tensor"), lax.axis_index("dp")
    core = index % 2
    place = jnp.where(core == 0, index // 8, (index // 2) % 4)
    quarters = image_sizes[0] // 4
    cells = (quarters[0] * quarters[1]).astype(F32)
    total = jnp.full((8, 128), cells, F32)
    total = total + swap_cores(total)
    for step in (1, 3):
        total = total + send(total, lambda x, z, core, y, k=step: (x ^ k, z, core, y))
    for step in (1, 3):
        total = total + send(total, lambda x, z, core, y, k=step: (x, z ^ k, core, y))
    meta = jnp.stack([tensor, quarters[0], quarters[1], core, place]).astype(jnp.int32)

    stride_rows = stride_kernels.reshape(2, 1024, C)
    stem_rows = stem_kernel.transpose(0, 2, 1, 3).reshape(48, 64)
    head_rows = head_kernel.transpose(0, 3, 1, 2).reshape(96, 64)
    (first,) = run_kernel(
        "pack_stride0", pack_stride0_body, (meta,), (stride_rows, stem_rows, head_rows, pre_project, post_project),
        (((1120, C), BF16),), near=False, slab=0, limit=8,
    )
    near0 = from_one_side(first)
    stride_rows, block_rows, mix_rows, _ = lax.optimization_barrier(
        (stride_kernels.reshape(2, 16, 64, C), block_kernels.reshape(2, 9, 64, C), block_mixers, first)
    )
    second, third = run_kernel(
        "pack_rest", pack_rest_body, (meta,), (stride_rows, block_rows, mix_rows),
        (((20, 64, C), BF16), ((16, 64, C), BF16)), near=False, slab=1, limit=8,
    )
    code_row = code_indices.reshape(1, CELLS)
    image = after(pixels.reshape(384, 128), second)
    pix, xt, entries = run_kernel(
        "patches", patch_body, (meta,), (image, code_row, codebook.T),
        (*far_out(((8, 8, CELLS), F32)), ((128, 4 * CELLS), BF16), *far_out(THIN)),
        (((8, 8, CELLS), F32), THIN), limit=10, sems=2, near=False,
    )
    near0 = after(near0, xt)
    stride0 = from_all(first, near0, core, 512, 608)
    near1 = from_one_side(after(second, near0))
    near1 = after(near1, stride0[3])
    blocks = from_all(second, near1, core, 10, 10)
    near2 = from_one_side(after(third, near1))
    small = (((C, 128), BF16), ((C, 128), BF16), ((C, E), BF16), ((C, E), BF16))
    r0, u0, av, xt, w0, stem, head, pre, post = run_kernel(
        "front", front_body, (meta,), (xt, *stride0),
        (WIDE, THREE, *far_out(EIGHT, ((128, 4 * CELLS), BF16), SIXTEEN, *small)),
        (EIGHT, SIXTEEN, *small), limit=14, sems=10,
    )
    near2 = after(near2, r0)
    stride1 = from_all(third, near2, core, 8, 8)
    r2, u2, wb1, vq, r0, u0, wb0, v0, q0, r1, diff, zq = run_kernel(
        "encode", encode_body, (meta,), (r0, u0, *blocks, *far(pre, post, entries)),
        (WIDE, THREE, TEN, None, *far_out(WIDE, THREE, TEN, WIDE, WIDE_LOW, WIDE, THIN, THIN_LOW)),
        (TEN, WIDE, WIDE_LOW, WIDE, THIN, THIN_LOW, ((C, E), BF16), ((C, E), BF16), THIN), limit=14, sems=11,
    )
    half = ((4, QUARTER, C), F32)
    lanes = ((128, 4 * CELLS), BF16)
    keep, other = run_kernel(
        "main", main_body, (meta, total, vq),
        (r2, u2, wb1, *far(*stride1, head, pix, zq, post, pre, code_row, stem, diff, r1, q0, v0, u0, wb0, r0, w0, av, xt)),
        (half, half),
        (
            SIXTEEN, ((C, 128), BF16), ((8, 8, CELLS), F32), THIN_LOW, ((C, E), BF16), ((C, E), BF16),
            ((1, CELLS), jnp.int32), ((C, 128), BF16), THIN, WIDE, WIDE_LOW, WIDE, THREE, TEN, WIDE, SIXTEEN, EIGHT, lanes,
            WIDE, WIDE_LOW, WIDE, THREE, ((4, CELLS, C), F32), ((4, CELLS, C), BF16), ((128, 4 * CELLS), F32), lanes,
            EIGHT, THREE, THIN, ((64, C), F32), half, half,
        ),
        limit=52, sems=22,
    )

    quarter = ((QUARTER, C), F32)
    parts = run_kernel("add_cores", add_cores_body, (meta,), (keep, swap_cores(other)), (quarter,) * 4)
    found = [along_first(parts[k], k) for k in (1, 2, 3)]
    grad = (parts[0] + found[1]) + (found[0] + found[2])
    found = [along_second(grad, k) for k in (1, 2, 3)]
    grad = (grad + found[1]) + (found[0] + found[2])
    found = [along_first(grad, -k) for k in (1, 2, 3)]
    own_half, square = run_kernel("join", join_body, (meta,), (grad, *found), (half, ((8, 128), F32)))
    other_half = swap_cores(own_half)
    found = [along_tensor(square, k) for k in (1, 2, 3)]
    square = (square + found[1]) + (found[0] + found[2])
    square = square + swap_cores(square)
    norm = jnp.sqrt(square[0, 0])
    factor = jnp.minimum(1.0, clip_norm / (norm + 1e-06))
    stride, block, mixer, codes, smalls = run_kernel(
        "order", order_body, (meta,), (own_half, other_half),
        (((2, 1024, C), F32), ((2, 576, C), F32), ((2, 64, C), F32), ((64, 512), F32), ((2, 64, C), F32)),
    )
    stem_grad = jnp.concatenate([smalls[0, :, 64:128], smalls[0, :, 128:192]], 0)
    stem_grad = stem_grad.reshape(4, 4, 8, 64)[:, :, 0:3]
    head_grad = jnp.concatenate([smalls[1, :, 64:128], smalls[1, :, 128:192]], 0)
    head_grad = head_grad.reshape(4, 4, 2, 4, 64)[:, :, :, 0:3].reshape(4, 4, 6, 64).transpose(0, 1, 3, 2)
    grads = (
        stem_grad,
        stride.reshape(2, 4, 4, 64, C),
        block.reshape(2, 3, 3, 64, C),
        mixer,
        smalls[0, :, 0:64],
        smalls[1, :, 0:64],
        codes.T,
        head_grad,
    )
    rates = (
        48.0 ** (-0.5),
        (16.0 * C) ** (-0.5),
        (9.0 * C) ** (-0.5),
        C ** (-0.5),
        C ** (-0.5),
        E ** (-0.5),
        0.6,
        (4.0 * C) ** (-0.5),
    )
    news = [adam(params[i], firsts[i], seconds[i], factor * grads[i], rates[i]) for i in range(8)]
    loss_terms = jnp.stack(
        [smalls[1, 0, 192], 48.0 * total[0, 0], smalls[0, 0, 192], 64.0 * total[0, 0]]
    )
    return (loss_terms, norm, *(n[0] for n in news), *(n[1] for n in news), *(n[2] for n in news))


def solution(mesh):
    in_specs = (
        P("dp", None, None, None),
        P("dp", None),
        P("dp", None, None),
        P(None, None, None, "tensor"),
        P(None, None, None, "tensor", None),
        P(None, None, None, "tensor", None),
        P(None, "tensor", None),
        P("tensor", None),
        P(None, "tensor"),
        P(),
        P(None, None, "tensor", None),
        P(None, None, None, "tensor"),
        P(None, None, None, "tensor", None),
        P(None, None, None, "tensor", None),
        P(None, "tensor", None),
        P("tensor", None),
        P(None, "tensor"),
        P(),
        P(None, None, "tensor", None),
        P(None, None, None, "tensor"),
        P(None, None, None, "tensor", None),
        P(None, None, None, "tensor", None),
        P(None, "tensor", None),
        P("tensor", None),
        P(None, "tensor"),
        P(),
        P(None, None, "tensor", None),
    )
    out_specs = (
        P(),
        P(),
        P(None, None, None, "tensor"),
        P(None, None, None, "tensor", None),
        P(None, None, None, "tensor", None),
        P(None, "tensor", None),
        P("tensor", None),
        P(None, "tensor"),
        P(),
        P(None, None, "tensor", None),
        P(None, None, None, "tensor"),
        P(None, None, None, "tensor", None),
        P(None, None, None, "tensor", None),
        P(None, "tensor", None),
        P("tensor", None),
        P(None, "tensor"),
        P(),
        P(None, None, "tensor", None),
        P(None, None, None, "tensor"),
        P(None, None, None, "tensor", None),
        P(None, None, None, "tensor", None),
        P(None, "tensor", None),
        P("tensor", None),
        P(None, "tensor"),
        P(),
        P(None, None, "tensor", None),
    )
    return jax.shard_map(
        on_device, mesh=mesh, in_specs=in_specs, out_specs=out_specs, check_vma=False
    )
```

```python
import math

import jax
import jax.numpy as jnp
from jax import lax
from jax.experimental import pallas as pl
from jax.experimental.pallas import tpu as pltpu
from jax.sharding import PartitionSpec as P

C = 256
E = 64
STEP = 10
SIDE = 32
CELLS = SIDE * SIDE
PADDED = CELLS + 2 * SIDE

beta_commit = 0.25
clip_norm = 0.002
beta_one = 0.9
beta_two = 0.999
adam_eps = 1e-08
decay_rate = 0.01
half_bin = 1.0 / 255.0
root_half = 0.7071067811865476
gelu_root = 0.7978845608028654
gelu_cube = 0.044715

F32 = jnp.float32
BF16 = jnp.bfloat16

UP_SHIFT = (-1, 0, 0, 1)
DOWN_PARITY = (1, 0, 1, 0)
DOWN_SHIFT = (-1, 0, 0, 1)


def here():
    index = lax.axis_index("dp")
    core = index % 2
    return lax.axis_index("tensor"), core, jnp.where(core == 0, index // 8, (index // 2) % 4)


def nn(left, right):
    return lax.dot_general(left, right, (((1,), (0,)), ((), ())), preferred_element_type=F32)


def nt(left, right):
    return lax.dot_general(left, right, (((1,), (1,)), ((), ())), preferred_element_type=F32)


def gelu(x):
    return x * (0.5 * (1.0 + jnp.tanh(gelu_root * (x + gelu_cube * (x * x * x)))))


def gelu_both(x):
    square = x * x
    t = jnp.tanh(x * (gelu_root + gelu_root * gelu_cube * square))
    share = 0.5 + 0.5 * t
    bend = 0.5 * gelu_root + 1.5 * gelu_root * gelu_cube * square
    return x * share, share + x * (1.0 - t * t) * bend


def columns(shape):
    return lax.broadcasted_iota(jnp.int32, shape, 0) % SIDE


def left_of(x):
    return jnp.where(columns(x.shape) == 0, 0.0, pltpu.roll(x, 1, 0))


def right_of(x):
    return jnp.where(columns(x.shape) == SIDE - 1, 0.0, pltpu.roll(x, x.shape[0] - 1, 0))


def clear_edges(ref, index):
    edge = jnp.zeros((SIDE, C), BF16)
    ref[index, 0:SIDE, :] = edge
    ref[index, PADDED - SIDE : PADDED, :] = edge


def store_three(ref, x):
    for index in range(3):
        clear_edges(ref, index)
    ref[0, SIDE : SIDE + CELLS, :] = left_of(x).astype(BF16)
    ref[1, SIDE : SIDE + CELLS, :] = x.astype(BF16)
    ref[2, SIDE : SIDE + CELLS, :] = right_of(x).astype(BF16)


def store_two(ref, phase, x):
    clear_edges(ref, 2 * phase)
    clear_edges(ref, 2 * phase + 1)
    moved = right_of(x) if phase % 2 == 0 else left_of(x)
    ref[2 * phase, SIDE : SIDE + CELLS, :] = x.astype(BF16)
    ref[2 * phase + 1, SIDE : SIDE + CELLS, :] = moved.astype(BF16)


def window(ref, index, shift):
    return ref[index, (shift + 1) * SIDE : (shift + 1) * SIDE + CELLS, :]


def three(ref, row_shift, col_shift):
    return window(ref, col_shift + 1, row_shift)


def two(ref, phase, row_shift, col_shift):
    return window(ref, 2 * phase + (0 if col_shift == 0 else 1), row_shift)


def own_lanes(x, tensor):
    half = jnp.where(tensor >= 2, x[:, 128:256], x[:, 0:128])
    return jnp.where(tensor % 2 == 1, pltpu.roll(half, 64, 1), half)[:, 0:64]


def lane_grid(shape):
    lane = lax.broadcasted_iota(jnp.int32, shape, 1)
    return lane // SIDE, lane % SIDE


def moved_plane(x, row_shift, col_shift):
    if row_shift == 0 and col_shift == 0:
        return x
    y = pltpu.roll(x, (-(SIDE * row_shift + col_shift)) % CELLS, 1)
    rows, cols = lane_grid(x.shape)
    keep = None
    for index, shift in ((rows, row_shift), (cols, col_shift)):
        if shift != 0:
            ok = (index < SIDE - 1) if shift == 1 else (index > 0)
            keep = ok if keep is None else (keep & ok)
    return jnp.where(keep, y, 0.0)


def same_forward(source, weight_ref, first):
    total = None
    for row in range(3):
        for col in range(3):
            term = nt(three(source, row - 1, col - 1), weight_ref[first + 3 * row + col])
            total = term if total is None else total + term
    return total


def same_backward(source, weight_ref, first):
    total = None
    for row in range(3):
        for col in range(3):
            term = nn(three(source, 1 - row, 1 - col), weight_ref[first + 3 * row + col])
            total = term if total is None else total + term
    return total


def down_forward(source, weight_ref):
    total = None
    for row in range(4):
        for col in range(4):
            phase = 2 * DOWN_PARITY[row] + DOWN_PARITY[col]
            term = nt(two(source, phase, DOWN_SHIFT[row], DOWN_SHIFT[col]), weight_ref[4 * row + col])
            total = term if total is None else total + term
    return total


def split_three(x):
    first = x.astype(BF16)
    rest = x - first.astype(F32)
    second = rest.astype(BF16)
    return first, second, (rest - second.astype(F32)).astype(BF16)


def one_hot_codes(codes_ref):
    return (
        (lax.broadcasted_iota(jnp.int32, (512, CELLS), 0) == codes_ref[...]).astype(F32).astype(BF16)
    )


def patch_body(
    sizes, image_in, codes_in, book_in, pix_out, x_out, entries_out,
    image_ref, codes_ref, book_ref, pix_ref, x_ref, entries_ref, sems,
):
    high, wide = sizes[0, 0] // 4, sizes[0, 1] // 4
    copies = copy_all(
        sems,
        [
            (image_in, image_ref), (codes_in, codes_ref), (book_in, book_ref),
            (pix_ref, pix_out), (entries_ref, entries_out), (x_ref, x_out),
        ],
    )
    start_all(copies[0:3])
    wait_all(copies[0:3])
    book = jnp.concatenate(split_three(book_ref[...]), 0)
    found = nn(book, one_hot_codes(codes_ref))
    entries_ref[...] = ((found[0:64] + found[64:128]) + found[128:192]).T
    copies[4].start()
    image = image_ref[...].astype(F32).astype(BF16)
    lane = lax.broadcasted_iota(jnp.int32, (128, CELLS), 1)
    source = lax.broadcasted_iota(jnp.int32, (128, CELLS), 0)
    row = lax.broadcasted_iota(jnp.int32, (384, CELLS), 0)
    own_row = (row // 4) % SIDE == lax.broadcasted_iota(jnp.int32, (384, CELLS), 1) // SIDE
    slot = lax.broadcasted_iota(jnp.int32, (32, 384), 0)
    line = lax.broadcasted_iota(jnp.int32, (32, 384), 1)
    pick = ((line % 4 == slot // 8) & (line // 128 == slot % 8)).astype(F32).astype(BF16)
    planes = {}
    for col in range(4):
        spread = (source == 4 * (lane % SIDE) + col).astype(F32).astype(BF16)
        lined = jnp.where(own_row, nn(image, spread), 0.0).astype(BF16)
        found = nn(pick, lined)
        for r in range(4):
            planes[r, col] = found[8 * r : 8 * r + 8]
    for r in range(4):
        for half in range(2):
            pix_ref[2 * r + half] = planes[r, 2 * half] + pltpu.roll(planes[r, 2 * half + 1], 4, 0)
    copies[3].start()
    rows, cols = lane_grid((8, CELLS))
    channel = lax.broadcasted_iota(jnp.int32, (8, CELLS), 0)
    inside = (rows < high) & (cols < wide) & (channel < 3)
    planes = {key: jnp.where(inside, value / 127.5 - 1.0, 0.0) for key, value in planes.items()}
    moved = {}
    for r in range(-1, 5):
        for c in range(-1, 5):
            moved[r, c] = moved_plane(planes[r % 4, c % 4], r // 4, c // 4)
    for p in range(2):
        for q in range(2):
            for kh in range(4):
                for kw in range(0, 4, 2):
                    r, c = 2 * p + kh - 1, 2 * q + kw - 1
                    tap = 4 * kh + kw
                    x_ref[8 * tap : 8 * tap + 16, (2 * p + q) * CELLS : (2 * p + q + 1) * CELLS] = (
                        jnp.concatenate([moved[r, c], moved[r, c + 1]], 0).astype(BF16)
                    )
    copies[5].start()
    wait_all(copies[3:])


def copy_all(sems, pairs):
    return [pltpu.make_async_copy(source, target, sems.at[i]) for i, (source, target) in enumerate(pairs)]


def start_all(copies):
    for copy in copies:
        copy.start()


def wait_all(copies):
    for copy in copies:
        copy.wait()


def count_body(sizes, count_ref):
    count_ref[...] = jnp.full((8, 128), (sizes[0, 0] // 4) * (sizes[0, 1] // 4), jnp.int32).astype(F32)


def pack_first_body(
    stride_in, stem_in, head_in, pre_in, post_in, out, part_out,
    stride_ref, stem_ref, head_ref, pre_ref, post_ref, out_ref, sems,
):
    _, core, _ = here()
    copies = copy_all(
        sems,
        [
            (stem_in, stem_ref), (head_in, head_ref), (pre_in, pre_ref), (post_in, post_ref),
            (stride_in.at[0, 0:8], stride_ref.at[0:8]), (stride_in.at[0, 8:16], stride_ref.at[8:16]),
            (out_ref.at[8:10], out.at[8:10]), (out_ref.at[0:8], out.at[0:8]), (out_ref.at[10:18], out.at[10:18]),
            (out_ref.at[pl.ds(8 * core, 10)], part_out),
        ],
    )
    start_all(copies[0:6])
    wait_all(copies[0:4])

    def ordered(ref, per):
        rows = jnp.concatenate([ref[kh, c] for kh in range(4) for c in range(per)], 0)
        count = 16 * per
        slot = lax.broadcasted_iota(jnp.int32, (128, count), 0)
        line = lax.broadcasted_iota(jnp.int32, (128, count), 1)
        channel = slot % 8
        if per == 6:
            channel = jnp.where(channel % 4 == 3, per, channel - channel // 4)
        wanted = (slot // 32) * 4 * per + channel * 4 + (slot // 8) % 4
        pick = ((line == wanted) & (channel < per)).astype(F32).astype(BF16)
        return nn(pick, rows.astype(BF16)).T

    out_ref[8] = jnp.concatenate([ordered(stem_ref, 3), ordered(head_ref, 6)], 1).astype(BF16)
    thin = jnp.concatenate([pre_ref[...], post_ref[...].T], 1)
    out_ref[9] = jnp.concatenate([thin, thin], 1).astype(BF16)
    copies[6].start()
    for k in range(2):
        copies[4 + k].wait()
        out_ref[10 * k : 10 * k + 8] = stride_ref[8 * k : 8 * k + 8].astype(BF16)
        copies[7 + k].start()
    copies[9].start()
    wait_all(copies[6:])


def pack_rest_body(stride_in, block_in, mix_in, out, stride_ref, block_ref, mix_ref, out_ref, sems):
    copies = copy_all(
        sems,
        [
            (block_in, block_ref), (mix_in, mix_ref), (stride_in.at[1], stride_ref), (out_ref, out),
        ],
    )
    start_all(copies[0:3])
    wait_all(copies[0:3])
    for b in range(2):
        out_ref[18 * b : 18 * b + 9] = block_ref[b].astype(BF16)
        out_ref[18 * b + 9] = mix_ref[b].astype(BF16)
        out_ref[18 * b + 10 : 18 * b + 18] = stride_ref[8 * b : 8 * b + 8].astype(BF16)
    start_all(copies[3:])
    wait_all(copies[3:])


def gather_pairs(ref, parts, tensor, core, rotated, low, high, half_low):
    def rows(step):
        if rotated and isinstance(step, int):
            return pl.ds(64 * step, 64)
        return pl.ds(pl.multiple_of((64 * step if rotated else ((tensor + step) % 4) * 64), 64), 64)

    count = ref.shape[0] // 2
    pairs = []
    for part, step in zip(parts[0:3], (0, 1 + 2 * core, 3 - 2 * core), strict=True):
        for k, start in enumerate((low, high)):
            pairs.append((part.at[start : start + count], ref.at[count * k : count * k + count, rows(step), :]))
    for part, half in ((parts[3], core), (parts[4], 1 - core)):
        source = part.at[pl.ds(half_low(half), count)]
        pairs.append((source, ref.at[pl.ds(count * half, count), rows(2), :]))
    return pairs


def block_forward(resid, u_ref, w_ref, first, v_ref, q_ref):
    value, v_ref[...] = gelu_both(same_forward(u_ref, w_ref, first))
    act = value.astype(BF16)
    q_ref[...] = act
    return resid + nn(act, w_ref[first + 9])


def front_body(
    x_in, own, near, far, mine, other,
    r_ref, u_ref, slope_out, a_out, w_out, stem_out, head_out, pre_out, post_out, patch_out,
    x_ref, small_ref, slope_ref, a_ref, w_ref, stem_ref, head_ref, pre_ref, post_ref, patch_ref, sems,
):
    tensor, core, _ = here()
    small = [part.at[8:10] for part in (own, near, far)] + [mine.at[pl.ds(8 * (1 - core), 2)]]
    pairs = [(x_in, x_ref)] + [(part, small_ref.at[k]) for k, part in enumerate(small)]
    pairs += gather_pairs(w_ref, (own, near, far, mine, other), tensor, core, False, 0, 10, lambda half: 2 * half)
    copies = copy_all(sems, pairs)
    start_all(copies)
    outs = [(stem_ref, stem_out), (head_ref, head_out), (pre_ref, pre_out), (post_ref, post_out), (w_ref, w_out)]
    outs += [(a_ref.at[2 * p : 2 * p + 2], a_out.at[2 * p : 2 * p + 2]) for p in range(4)]
    outs += [(patch_ref, patch_out), (slope_ref, slope_out)]
    writes = [
        pltpu.make_async_copy(source, target, sems.at[len(copies) + i]) for i, (source, target) in enumerate(outs)
    ]
    wait_all(copies[0:5])
    for k, step in enumerate((0, 1 + 2 * core, 3 - 2 * core, 2)):
        rows = pl.ds(pl.multiple_of(((tensor + step) % 4) * 64, 64), 64)
        turned = 64 * step if isinstance(step, int) else pl.multiple_of(64 * step, 64)
        stem_ref[rows, :] = small_ref[k, 0, :, 0:128]
        head_ref[pl.ds(turned, 64), :] = small_ref[k, 0, :, 128:256]
        pre_ref[rows, :] = small_ref[k, 1, :, 0:64]
        post_ref[rows, :] = small_ref[k, 1, :, 64:128]
    start_all(writes[0:4])
    for phase in range(4):
        patch = x_ref[:, phase * CELLS : (phase + 1) * CELLS].T
        patch_ref[phase * CELLS : (phase + 1) * CELLS, :] = patch
        store_two(a_ref, phase, gelu(nt(patch, stem_ref[...])))
        writes[5 + phase].start()
    writes[9].start()
    wait_all(copies[5:])
    writes[4].start()
    resid = down_forward(a_ref, w_ref)
    r_ref[...] = resid
    value, slope_ref[...] = gelu_both(resid)
    writes[10].start()
    store_three(u_ref, value)
    wait_all(writes)


def valid_cells(sizes):
    cell = lax.broadcasted_iota(jnp.int32, (CELLS, E), 0)
    return (cell // SIDE < sizes[0, 0] // 4) & (cell % SIDE < sizes[0, 1] // 4)


def poly(x, coefs):
    total = jnp.full_like(x, coefs[0])
    for c in coefs[1:]:
        total = total * x + c
    return total


ERFC_LOW = (
    2.326819970068386e-2, -1.387039388740657e-1, 3.687424674597105e-1, -5.824733027278666e-1,
    6.210004621745983e-1, -4.944515323274145e-1, 3.404879937665872e-1, -2.741127028184656e-1,
    5.638259427386472e-1,
)
ERFC_HIGH = (
    -1.047766399936249e1, 1.297719955372516e1, -7.495518717768503e0, 2.921019019210786e0,
    -1.015265279202700e0, 4.218463358204948e-1, -2.820767439740514e-1, 5.641895067754075e-1,
)
ERF_NEAR = (
    7.853861353153693e-5, -8.010193625184903e-4, 5.188327685732524e-3, -2.685381193529856e-2,
    1.128358514861418e-1, -3.761262582423300e-1, 1.128379165726710e0,
)


def erfc(x):
    size = jnp.abs(x)
    square = x * x
    far_exp = jnp.exp(-square)
    recip = 1.0 / jnp.maximum(size, 0.5)
    y = recip * recip
    far = far_exp * recip * jnp.where(size < 2.0, poly(y, ERFC_LOW), poly(y, ERFC_HIGH))
    far = jnp.where(x < 0, 2.0 - far, far)
    near = 1.0 - x * poly(square, ERF_NEAR)
    return jnp.where(size > 1.0, far, near), far_exp


def likelihood(center_out, scale_out, pix, keep, scale):
    target = pix / 127.5 - 1.0
    center = jnp.tanh(center_out)
    decay = jnp.exp(-jnp.abs(scale_out))
    sigma = 0.25 + (jnp.maximum(scale_out, 0.0) + jnp.log(1.0 + decay))
    gate = jnp.where(scale_out >= 0, 1.0, decay) / (1.0 + decay)
    low_end, high_end = pix == 0.0, pix == 255.0
    lower = jnp.where(low_end, -40.0, (target - half_bin - center) / sigma)
    upper = jnp.where(high_end, 40.0, (target + half_bin - center) / sigma)
    right = lower + upper > 0
    tail_a, exp_a = erfc(jnp.where(right, lower, -upper) * root_half)
    tail_b, exp_b = erfc(jnp.where(right, upper, -lower) * root_half)
    mass = 0.5 * (tail_a - tail_b)
    bits = jnp.where(keep, jnp.log(mass), 0.0)
    density = 1.0 / math.sqrt(2.0 * math.pi)
    slope = jnp.where(keep, scale * density / mass, 0.0)
    low_slope = jnp.where(low_end, 0.0, -slope * jnp.where(right, exp_a, exp_b))
    high_slope = jnp.where(high_end, 0.0, slope * jnp.where(right, exp_b, exp_a))
    center_grad = -(low_slope + high_slope) / sigma
    sigma_grad = -(low_slope * lower + high_slope * upper) / sigma
    return bits, center_grad * (1.0 - center * center), sigma_grad * gate


def head_links():
    for p in range(2):
        for q in range(2):
            for kh in range(4):
                for kw in range(4):
                    up, left = p + UP_SHIFT[kh], q + UP_SHIFT[kw]
                    out = (2 * p + kh % 2, 2 * q + kw % 2)
                    yield out, 4 * kh + kw, 2 * (up % 2) + left % 2, up // 2, left // 2


QUARTER = 448
KINDS = {"stride": (0, 256), "block": (256, 144), "mixer": (400, 16), "codes": (416, 16), "small": (432, 16)}


def store_rows(g_ref, kind, start, value):
    base, size = KINDS[kind]
    done = 0
    while done < value.shape[0]:
        place = start + done
        count = min(size - place % size, value.shape[0] - done)
        first = base + place % size
        g_ref[place // size, first : first + count, :] = value[done : done + count]
        done += count


def with_scalar(x, scalar):
    row = lax.broadcasted_iota(jnp.int32, (64, 64), 0)
    lane = lax.broadcasted_iota(jnp.int32, (64, 64), 1)
    return jnp.concatenate([x, jnp.where((row == 0) & (lane == 0), scalar, 0.0)], 1)


def block_backward(grad_out, resid_ref, u_ref, v_ref, q_ref, w_ref, first, dv_ref, g_ref):
    low = grad_out.astype(BF16)
    own_q = q_ref[:, 0:128].astype(F32).T[0:64].astype(BF16)
    store_rows(g_ref, "mixer", 0, nn(own_q, low))
    mid = nt(low, w_ref[first + 9])
    inner = v_ref[...] * mid
    store_three(dv_ref, inner)
    own = inner[:, 0:128].T[0:64].astype(BF16)
    for row in range(3):
        for col in range(3):
            tap = 3 * row + col
            store_rows(g_ref, "block", 64 * tap, nn(own, three(u_ref, row - 1, col - 1)))
    return grad_out + resid_ref[...] * same_backward(dv_ref, w_ref, first)


def forward_blocks(
    sizes, r0_ref, u0_ref, w_ref, pre_ref, post_ref, entries_ref,
    v0_ref, q0_ref, r1_ref, act_ref, diff_ref, zq_ref, r2_ref, u2_ref, v1_ref, q1_ref, r3_ref, u3_ref, waits,
):
    resid = block_forward(r0_ref[...], u0_ref, w_ref, 0, v0_ref, q0_ref)
    value, r1_ref[...] = gelu_both(resid)
    act = value.astype(BF16)
    act_ref[...] = act
    wait_all(waits)
    latent = nn(act, pre_ref[...])
    entries = entries_ref[...]
    diff = latent - entries
    diff_ref[...] = diff
    code = (latent + (entries - latent)).astype(BF16)
    zq_ref[...] = code
    resid = nt(code, post_ref[...])
    value, r2_ref[...] = gelu_both(resid)
    store_three(u2_ref, value)
    resid = block_forward(resid, u2_ref, w_ref, 10, v1_ref, q1_ref)
    value, r3_ref[...] = gelu_both(resid)
    store_three(u3_ref, value)
    return (1.0 + beta_commit) * jnp.sum(jnp.where(valid_cells(sizes), diff * diff, 0.0))


def main_body(
    sizes, total_ref, r0_ref, u0_ref, own, near, far, mine, other,
    pre_in, post_in, entries_in, head_in, pix_in, codes_in, stem_in, r0s_in, w0_in, a_in, x_in, patch_in,
    keep_ref, send_ref,
    wb_ref, w_ref, pre_ref, post_ref, entries_ref, head_ref, pix_ref, codes_ref, stem_ref, r0s_ref, w0_ref, a_ref, x_ref, patch_ref,
    v0_ref, q0_ref, r1_ref, act_ref, diff_ref, zq_ref, r2_ref, u2_ref, v1_ref, q1_ref, r3_ref, u3_ref,
    h4_ref, a4_ref, prod_ref, q_ref, dh_ref, dv_ref, back_ref, late_ref, gd_ref, g_ref, sems,
):
    tensor, core, _ = here()
    parts = (own, near, far, mine, other)
    pairs = gather_pairs(wb_ref, parts, tensor, core, True, 0, 18, lambda half: 0)
    pairs += [(pre_in, pre_ref), (post_in, post_ref), (entries_in, entries_ref)]
    pairs += gather_pairs(w_ref, parts, tensor, core, True, 10, 28, lambda half: 10)
    pairs += [(head_in, head_ref), (pix_in, pix_ref), (codes_in, codes_ref), (stem_in, stem_ref)]
    pairs += [(r0s_in, r0s_ref), (w0_in, w0_ref), (a_in, a_ref), (x_in, x_ref), (patch_in, patch_ref)]
    copies = copy_all(sems, pairs)
    start_all(copies)
    wait_all(copies[0:8])
    vq = forward_blocks(
        sizes, r0_ref, u0_ref, wb_ref, pre_ref, post_ref, entries_ref,
        v0_ref, q0_ref, r1_ref, act_ref, diff_ref, zq_ref, r2_ref, u2_ref, v1_ref, q1_ref, r3_ref, u3_ref, copies[8:11],
    )
    wait_all(copies[11:19])
    decode_back(
        sizes, total_ref, pix_ref, r3_ref, u3_ref, head_ref, r2_ref, u2_ref, v1_ref, q1_ref, wb_ref,
        gd_ref, w_ref, h4_ref, a4_ref, prod_ref, q_ref, dh_ref, dv_ref, zq_ref, post_ref, back_ref, copies[19:21],
    )
    wait_all(copies[21:])
    encode_back(
        sizes, total_ref, vq, back_ref, diff_ref, codes_ref, r1_ref, act_ref, pre_ref, stem_ref, x_ref, patch_ref, a_ref,
        r0s_ref, u0_ref, v0_ref, q0_ref, wb_ref, w0_ref, gd_ref, keep_ref, send_ref, dv_ref, dh_ref, g_ref, late_ref,
    )


def decode_back(
    sizes, total_ref, pix_ref, r3_ref, u3_ref, head_ref, r2_ref, u2_ref, v1_ref, q1_ref, w1_ref,
    g_ref, w_ref, h4_ref, a4_ref, prod_ref, q_ref, dh_ref, dv_ref, zq_ref, post_ref, back_ref, early,
):
    tensor, _, _ = here()
    high, wide = sizes[0, 0] // 4, sizes[0, 1] // 4
    wait_all(early)
    head = head_ref[...].astype(F32).T.astype(BF16)
    for p in range(2):
        for q in range(2):
            phase = 2 * p + q
            total = None
            for kh in (p, p + 2):
                for kw in (q, q + 2):
                    term = nt(three(u3_ref, UP_SHIFT[kh], UP_SHIFT[kw]), w_ref[4 * kh + kw])
                    total = term if total is None else total + term
            value, h4_ref[phase] = gelu_both(total)
            act = value.astype(BF16)
            a4_ref[phase] = act
            prod_ref[:, phase * CELLS : (phase + 1) * CELLS] = nt(head, act)
    outs = {}
    for out, tap, phase, up, left in head_links():
        term = moved_plane(
            prod_ref[8 * tap : 8 * tap + 8, phase * CELLS : (phase + 1) * CELLS], up, left
        )
        outs[out] = term if out not in outs else outs[out] + term
    sub = lax.broadcasted_iota(jnp.int32, (8, CELLS), 0)
    rows, cols = lane_grid((8, CELLS))
    keep = (rows < high) & (cols < wide) & (sub % 4 != 3)
    first = sub < 4
    scale = -1.0 / (math.log(2.0) * 48.0 * total_ref[0, 0])
    grads = {}
    bits = None
    for pair in range(8):
        row, col = pair // 2, 2 * (pair % 2)
        one, other = outs[row, col], outs[row, col + 1]
        centers = jnp.where(first, one, pltpu.roll(other, 4, 0))
        scales = jnp.where(first, pltpu.roll(one, 4, 0), other)
        part, center_grad, scale_grad = likelihood(centers, scales, pix_ref[pair], keep, scale)
        bits = part if bits is None else bits + part
        grads[row, col] = jnp.where(first, center_grad, pltpu.roll(scale_grad, 4, 0))
        grads[row, col + 1] = jnp.where(first, pltpu.roll(center_grad, 4, 0), scale_grad)
    bits = -jnp.sum(bits) / math.log(2.0)
    found = {}
    for out, tap, phase, up, left in head_links():
        found[tap, phase] = moved_plane(grads[out], -up, -left)
    for phase in range(4):
        for tap in range(0, 16, 2):
            q_ref[8 * tap : 8 * tap + 16, phase * CELLS : (phase + 1) * CELLS] = jnp.concatenate(
                [found[tap, phase], found[tap + 1, phase]], 0
            ).astype(BF16)
    head_grad = None
    for phase in range(4):
        spread = q_ref[:, phase * CELLS : (phase + 1) * CELLS]
        term = nn(spread, a4_ref[phase, :, 0:64])
        head_grad = term if head_grad is None else head_grad + term
        slope = h4_ref[phase] * nn(spread.T, head)
        store_two(dh_ref, phase, slope)
        own = slope[:, 0:128].T[0:64].astype(BF16)
        for kh in (phase // 2, phase // 2 + 2):
            for kw in (phase % 2, phase % 2 + 2):
                tap = 4 * kh + kw
                store_rows(g_ref, "stride", 64 * tap, nn(own, three(u3_ref, UP_SHIFT[kh], UP_SHIFT[kw])))
    total = None
    for kh in range(4):
        for kw in range(4):
            phase = 2 * (kh % 2) + kw % 2
            term = nn(two(dh_ref, phase, -UP_SHIFT[kh], -UP_SHIFT[kw]), w_ref[4 * kh + kw])
            total = term if total is None else total + term
    grad = r3_ref[...] * total
    grad = block_backward(grad, r2_ref, u2_ref, v1_ref, q1_ref, w1_ref, 10, dv_ref, g_ref)
    low = grad.astype(BF16)
    post_grad = nn(zq_ref[...].astype(F32).T.astype(BF16), own_lanes(grad, tensor).astype(BF16))
    small = jnp.concatenate([post_grad, head_grad[0:64], head_grad[64:128]], 1)
    store_rows(g_ref, "small", 0, with_scalar(small, bits))
    store_rows(g_ref, "codes", 0, jnp.zeros((64, C), F32))
    back_ref[...] = nn(low, post_ref[...])


def encode_back(
    sizes, total_ref, vq, back_ref, diff_ref, codes_ref, r1_ref, act_ref, pre_ref, stem_ref, x_ref, patch_ref, a_ref,
    r0_ref, u_ref, v_ref, q_ref, wb_ref, w_ref, gd_ref, keep_ref, send_ref, dv_ref, dr_ref, g_ref, late_ref,
):
    tensor, core, _ = here()
    scaled = jnp.where(valid_cells(sizes), diff_ref[...] / (64.0 * total_ref[0, 0]), 0.0)
    dz = (back_ref[...] + 2.0 * beta_commit * scaled).astype(BF16)
    hot = one_hot_codes(codes_ref)
    found = nt(jnp.concatenate(split_three((-2.0 * scaled).T), 0), hot)
    codes = (found[0:64] + found[64:128]) + found[128:192]
    store_rows(g_ref, "codes", 0, codes[:, 0:256])
    late_ref[...] = codes[:, 256:512]
    act = own_lanes(act_ref[...].astype(F32), tensor)
    pre_grad = nn(act.T.astype(BF16), dz)
    grad = r1_ref[...] * nt(dz, pre_ref[...])
    grad = block_backward(grad, r0_ref, u_ref, v_ref, q_ref, wb_ref, 0, dv_ref, g_ref)
    store_three(dr_ref, grad)
    own = own_lanes(grad, tensor).T.astype(BF16)
    for kh in range(4):
        for kw in range(4):
            tap = 4 * kh + kw
            phase = 2 * DOWN_PARITY[kh] + DOWN_PARITY[kw]
            term = nn(own, two(a_ref, phase, DOWN_SHIFT[kh], DOWN_SHIFT[kw]))
            store_rows(g_ref, "stride", 64 * tap, term)
    line = lax.broadcasted_iota(jnp.int32, (C, C), 0)
    lane = lax.broadcasted_iota(jnp.int32, (C, C), 1)
    shifts = [(up, left) for up in (-1, 0, 1) for left in (-1, 0, 1)]
    before = total = None
    stem = stem_ref[pl.ds(pl.multiple_of(64 * tensor, 64), 64), :].astype(F32).T.astype(BF16)
    for phase in range(4):
        place = (lane[0:64] == line[0:64] + 64 * phase).astype(F32).astype(BF16)
        wide = nn(stem, place).astype(BF16)
        term = nn(patch_ref[phase * CELLS : (phase + 1) * CELLS, :], wide)
        before = term if before is None else before + term
    picks = [
        ((lane == line - 64 * tensor + 64 * phase) & (lane // 64 == phase)).astype(F32).astype(BF16) for phase in range(4)
    ]
    for up, left in shifts:
        weight = None
        for kh in range(4):
            for kw in range(4):
                if (-DOWN_SHIFT[kh], -DOWN_SHIFT[kw]) == (up, left):
                    term = nn(w_ref[4 * kh + kw], picks[2 * DOWN_PARITY[kh] + DOWN_PARITY[kw]])
                    weight = term if weight is None else weight + term
        term = nn(three(dr_ref, up, left), weight.astype(BF16))
        total = term if total is None else total + term
    slope = (gelu_both(before)[1] * total).astype(BF16)
    stem_grad = None
    for phase in range(4):
        term = nn(x_ref[:, phase * CELLS : (phase + 1) * CELLS], slope)[:, 64 * phase : 64 * phase + 64]
        stem_grad = term if stem_grad is None else stem_grad + term
    small = jnp.concatenate([pre_grad, stem_grad[0:64], stem_grad[64:128]], 1)
    store_rows(g_ref, "small", 0, with_scalar(small, vq))
    base = KINDS["codes"][0]

    @pl.when(core == 0)
    def _():
        keep_ref[...] = g_ref[...]
        send_ref[...] = gd_ref[...]
        for part in range(4):
            send_ref[part, base : base + 16, :] = late_ref[16 * part : 16 * part + 16, :]

    @pl.when(core == 1)
    def _():
        keep_ref[...] = gd_ref[...]
        send_ref[...] = g_ref[...]
        for part in range(4):
            keep_ref[part, base : base + 16, :] = late_ref[16 * part : 16 * part + 16, :]


def split_scalar(x):
    side = x[:, 128:256]
    lane = lax.broadcasted_iota(jnp.int32, side.shape, 1)
    whole = jnp.where(lane == 64, side + (pltpu.roll(side, 127, 1) + pltpu.roll(side, 126, 1)), 0.0)
    one, two_on, three_on = (part.astype(F32) for part in split_three(whole))
    side = jnp.where(lane < 64, side, one + (pltpu.roll(two_on, 1, 1) + pltpu.roll(three_on, 2, 1)))
    return jnp.concatenate([x[:, 0:128], side], 1)


def add_cores_body(keep_ref, other_ref, own_ref, *outs):
    _, _, place = here()
    own_ref[...] = keep_ref[place] + other_ref[place]
    last = KINDS["small"][0]
    for k, out in enumerate(outs):
        part = (place + 1 + k) % 4
        out[0:last, :] = (keep_ref[part, 0:last] + other_ref[part, 0:last]).astype(BF16)
        out[last:QUARTER, :] = split_scalar(keep_ref[part, last:QUARTER] + other_ref[part, last:QUARTER]).astype(BF16)


def four(own, one, two_on, three_on):
    return (own[...].astype(F32) + two_on[...].astype(F32)) + (one[...].astype(F32) + three_on[...].astype(F32))


def add_first_body(own, one, two_on, three_on, out):
    value = four(own, one, two_on, three_on)
    last = KINDS["small"][0]
    out[0:last, :] = value[0:last].astype(BF16)
    out[last:QUARTER, :] = split_scalar(value[last:QUARTER]).astype(BF16)


def add_second_body(own, one, two_on, three_on, out):
    out[...] = four(own, one, two_on, three_on)


def join_body(own, one, two_on, three_on, half_ref, square_ref):
    _, _, place = here()
    row = lax.broadcasted_iota(jnp.int32, (QUARTER, C), 0)
    lane = lax.broadcasted_iota(jnp.int32, (QUARTER, C), 1)
    codes, small = KINDS["codes"][0], KINDS["small"][0]
    share = jnp.where((row >= codes) & (row < small), 0.25, 1.0)
    share = jnp.where((row >= small) & (lane >= 192), 0.0, share)
    total = jnp.zeros((QUARTER, C), F32)
    for k, part in enumerate((own, one, two_on, three_on)):
        value = part[...]
        half_ref[(place + k) % 4] = value
        total = total + value * value
    square_ref[...] = jnp.full((8, 128), jnp.sum(total * share), F32)


def adam(weight, moment, second, grad, rate):
    m_new = beta_one * moment + (1.0 - beta_one) * grad
    v_new = beta_two * second + (1.0 - beta_two) * grad * grad
    m_hat = m_new / (1.0 - beta_one**STEP)
    v_hat = v_new / (1.0 - beta_two**STEP)
    return (
        weight - rate * (m_hat / (jnp.sqrt(v_hat) + adam_eps) + decay_rate * weight),
        m_new,
        v_new,
    )


RATES = (
    48.0 ** (-0.5),
    (16.0 * C) ** (-0.5),
    (9.0 * C) ** (-0.5),
    C ** (-0.5),
    C ** (-0.5),
    E ** (-0.5),
    0.6,
    (4.0 * C) ** (-0.5),
)


def adam_body(half_ref, other_ref, square_ref, total_ref, *refs):
    _, core, _ = here()
    given, outs, loss_ref, norm_ref = refs[0:24], refs[24:48], refs[48], refs[49]
    results, small_ref, sems = refs[50:74], refs[74], refs[75]
    norm = jnp.sqrt(square_ref[...])
    factor = jnp.minimum(1.0, clip_norm / (norm + 1e-06))[0:1, 0:1]
    norm_ref[0, 0] = jnp.max(norm)

    def rows_of(side, part, kind):
        base, size = KINDS[kind]
        mine, theirs = half_ref[part, base : base + size, :], other_ref[part, base : base + size, :]
        return jnp.where(core == side, mine.astype(F32), theirs.astype(F32))

    def update(weight, index, grad):
        values = [given[3 * weight + i][index] for i in range(3)]
        for i, value in enumerate(adam(*values, factor * grad, RATES[weight])):
            results[3 * weight + i][index] = value

    copies = []

    def finish(weight, index=None):
        for i in range(3):
            source, target = results[3 * weight + i], outs[3 * weight + i]
            if index is not None:
                source, target = source.at[index], target.at[index]
            copies.append(pltpu.make_async_copy(source, target, sems.at[len(copies)]))
            copies[-1].start()

    for side in range(2):
        for part in range(4):
            for weight, kind in ((1, "stride"), (2, "block"), (3, "mixer")):
                size = KINDS[kind][1]
                index = (side, pl.ds(size * part, size), slice(None))
                update(weight, index, rows_of(side, part, kind))
                if weight < 3:
                    finish(weight, index)
            update(6, (pl.ds(16 * part, 16), pl.ds(256 * side, 256)), rows_of(side, part, "codes"))
            small_ref[side, 16 * part : 16 * part + 16, :] = rows_of(side, part, "small")
    finish(3)
    finish(6)
    update(4, (slice(None), slice(None)), small_ref[0, :, 0:64])
    update(5, (slice(None), slice(None)), small_ref[1, :, 0:64])
    finish(4)
    finish(5)
    for weight, side, channels in ((0, 0, 3), (7, 1, 6)):
        turned = small_ref[side, :, 64:192]
        for kh in range(4):
            block = turned[32 * (kh % 2) : 32 * (kh % 2) + 32, 64 * (kh // 2) : 64 * (kh // 2) + 64]
            for c in range(channels):
                slot = c + (c // 3 if channels == 6 else 0)
                lines = jnp.concatenate([block[8 * kw + slot : 8 * kw + slot + 1] for kw in range(4)], 0)
                update(weight, (kh, c), lines)
        finish(weight)
    first = (lax.broadcasted_iota(jnp.int32, (16, 64), 0) == 0) & (lax.broadcasted_iota(jnp.int32, (16, 64), 1) < 3)
    for slot, side, share in ((0, 1, 48.0), (2, 0, 64.0)):
        loss_ref[0, slot] = jnp.sum(jnp.where(first, small_ref[side, 0:16, 192:256], 0.0))
        loss_ref[0, slot + 1] = share * total_ref[0, 0]
    wait_all(copies)


SMEM = pl.BlockSpec(memory_space=pltpu.SMEM)
VMEM = pl.BlockSpec(memory_space=pltpu.VMEM)


def run_kernel(name, body, scalars, arrays, outs, scratch=(), limit=6, sems=0, micros=1):
    anywhere = pl.BlockSpec(memory_space=pl.ANY)
    shapes, out_specs, specs, given = [], [], [SMEM] * len(scalars), list(scalars)
    for out in outs:
        if isinstance(out, int):
            shapes.append(pltpu.SMEM((1, out), F32))
            out_specs.append(SMEM)
        elif out[0] == "far":
            shapes.append(pltpu.HBM(*out[1:]))
            out_specs.append(anywhere)
        else:
            shapes.append(pltpu.VMEM(*out))
            out_specs.append(VMEM)
    for array in arrays:
        if isinstance(array, tuple):
            place, array = array
            given.append(pltpu.with_memory_space_constraint(array, pltpu.HBM) if place == "far" else array)
            specs.append(anywhere)
        else:
            given.append(pltpu.with_memory_space_constraint(array, pltpu.VMEM))
            specs.append(VMEM)
    return pl.pallas_call(
        body,
        out_shape=shapes,
        in_specs=specs,
        out_specs=out_specs,
        scratch_shapes=[pltpu.VMEM(*s) for s in scratch] + ([pltpu.SemaphoreType.DMA((sems,))] if sems else []),
        compiler_params=pltpu.CompilerParams(vmem_limit_bytes=limit * 2**20),
        cost_estimate=pl.CostEstimate(flops=int(micros * 1.1e9), bytes_accessed=0, transcendentals=0),
        name=name,
    )(*given)


THREE = ((3, PADDED, C), BF16)
EIGHT = ((8, PADDED, C), BF16)
WIDE = ((CELLS, C), F32)
WIDE_LOW = ((CELLS, C), BF16)
TWENTY = ((20, C, C), BF16)
THIN = ((CELLS, E), F32)
THIN_LOW = ((CELLS, E), BF16)
PATCH = ((4 * CELLS, 128), BF16)


def far(*arrays):
    return tuple(("far", array) for array in arrays)


def received(parts):
    return (("far", parts[0]), *(("any", part) for part in parts[1:]))


def far_out(*shapes):
    return tuple(("far", *shape) for shape in shapes)


SIXTEEN = ((16, C, C), BF16)


BOTH = ("dp", "tensor")


def send(value, target):
    pairs = []
    for x in range(4):
        for z in range(4):
            for core in range(2):
                for y in range(4):
                    to = target(x, z, core, y)
                    pairs.append(
                        (
                            ((x * 4 + z) * 2 + core) * 4 + y,
                            (((to[0] % 4) * 4 + to[1] % 4) * 2 + to[2]) * 4 + to[3] % 4,
                        )
                    )
    return lax.ppermute(value, BOTH, pairs)


def swap_cores(value):
    return send(value, lambda x, z, core, y: (x, z, 1 - core, y))


def along_first(value, k):
    return send(value, lambda x, z, core, y: (x + k, z, core, y) if core == 0 else (x, z + k, core, y))


def along_second(value, k):
    return send(value, lambda x, z, core, y: (x, z + k, core, y) if core == 0 else (x + k, z, core, y))


def along_tensor(value, k):
    return send(value, lambda x, z, core, y: (x, z, core, y + k))


def from_one_side(local):
    return send(local, lambda x, z, core, y: (x, z, core, y - 1 if core == 0 else y + 1))


def from_two(whole, part):
    return from_one_side(whole), along_tensor(part, 2)


def after(value, *others):
    return lax.optimization_barrier((value, *others))[0]


def on_device(
    pixels,
    image_sizes,
    code_indices,
    stem_kernel,
    stride_kernels,
    block_kernels,
    block_mixers,
    pre_project,
    post_project,
    codebook,
    head_kernel,
    *moments,
):
    def add_along(value, step, along_x):
        return value + send(value, lambda x, z, core, y: (x ^ step, z, core, y) if along_x else (x, z ^ step, core, y))

    image_sizes = pltpu.with_memory_space_constraint(image_sizes, pltpu.HBM)
    stem_rows = stem_kernel.transpose(0, 2, 1, 3)
    head_rows = head_kernel.transpose(0, 3, 1, 2)
    stride_rows = stride_kernels.reshape(2, 16, 64, C)
    block_rows = block_kernels.reshape(2, 9, 64, C)
    small = (((E, E), F32), ((E, E), F32))
    taps = lambda count: ((count, 64, C), BF16)
    (count,) = run_kernel("count", count_body, (image_sizes,), (), (((8, 128), F32),))
    count = add_along(count, 1, True)
    first, first_part = run_kernel(
        "pack_first", pack_first_body, (), far(stride_rows, stem_rows, head_rows, pre_project, post_project),
        far_out(taps(18), taps(10)),
        (((16, 64, C), F32), ((4, 3, 4, 64), F32), ((4, 6, 4, 64), F32), *small, taps(18)), limit=8, sems=10, micros=3,
    )
    near0, mine0 = from_two(first, first_part)
    (second,) = run_kernel(
        "pack_rest", pack_rest_body, (), far(stride_rows, block_rows, after(block_mixers, first, count)),
        far_out(taps(36)),
        (((16, 64, C), F32), ((2, 9, 64, C), F32), ((2, 64, C), F32), taps(36)), limit=10, sems=4, micros=3,
    )
    count = add_along(count, 3, True)
    code_row = code_indices.reshape(1, CELLS)
    image = after(pixels.reshape(384, 128), second, count)
    planes, lanes = ((8, 8, CELLS), F32), ((128, 4 * CELLS), BF16)
    pix, xt, entries = run_kernel(
        "patches", patch_body, (image_sizes,), far(image, code_row, codebook.T), far_out(planes, lanes, THIN),
        (((384, 128), jnp.int32), ((1, CELLS), jnp.int32), ((E, 512), F32), planes, lanes, THIN), limit=12, sems=6, micros=20,
    )
    count = add_along(count, 1, False)
    near1 = from_one_side(second)
    near0, mine0, xt, count = lax.optimization_barrier((near0, mine0, xt, count))
    stride0 = (first, near0, swap_cores(near0), mine0, swap_cores(mine0))
    count = add_along(count, 3, False)
    count = count + swap_cores(count)
    small = (((C, 128), BF16), ((C, 128), BF16), ((C, E), BF16), ((C, E), BF16))
    r0, u0, slope0, av, w0, stem, head, pre, post, patch = run_kernel(
        "front", front_body, (), (*far(after(xt, count)), *received(stride0)), (WIDE, THREE, *far_out(WIDE, EIGHT, SIXTEEN, *small, PATCH)),
        (lanes, ((4, 2, 64, C), BF16), WIDE, EIGHT, SIXTEEN, *small, PATCH), limit=20, sems=25, micros=0.1,
    )
    near1, r0 = lax.optimization_barrier((near1, r0))
    mine1 = from_one_side(lax.dynamic_slice_in_dim(near1, 18 * (lax.axis_index("dp") % 2), 18, 0))
    rest = (second, near1, swap_cores(near1), mine1, swap_cores(mine1))
    half = ((4, QUARTER, C), F32)
    keep, other = run_kernel(
        "main", main_body, (image_sizes, count),
        (r0, u0, *received(rest), *far(pre, post, entries, head, pix, code_row, stem, slope0, w0, av, xt, patch)),
        (half, half),
        (
            TWENTY, SIXTEEN, ((C, E), BF16), ((C, E), BF16), THIN, ((C, 128), BF16), planes, ((1, CELLS), jnp.int32),
            ((C, 128), BF16), WIDE, SIXTEEN, EIGHT, lanes, PATCH,
            WIDE, WIDE_LOW, WIDE, WIDE_LOW, THIN, THIN_LOW, WIDE, THREE, WIDE, WIDE_LOW, WIDE, THREE,
            ((4, CELLS, C), F32), ((4, CELLS, C), BF16), ((128, 4 * CELLS), F32), lanes,
            EIGHT, THREE, THIN, ((64, C), F32), half, half,
        ),
        limit=53, sems=28, micros=40,
    )

    quarter, quarter_low = ((QUARTER, C), F32), ((QUARTER, C), BF16)
    parts = run_kernel("add_cores", add_cores_body, (), (keep, swap_cores(other)), (quarter, *(quarter_low,) * 3))
    found = [along_first(parts[k], k) for k in (1, 2, 3)]
    (grad,) = run_kernel("add_first", add_first_body, (), (parts[0], *found), (quarter_low,))
    found = [along_second(grad, k) for k in (1, 2, 3)]
    (grad,) = run_kernel("add_second", add_second_body, (), (grad, *found), (quarter,))
    found = [along_first(grad, -k) for k in (1, 2, 3)]

    own_half, square = run_kernel("join", join_body, (), (grad, *found), (half, ((8, 128), F32)))
    other_half = swap_cores(own_half)
    found = [along_tensor(square, k) for k in (1, 2, 3)]
    square = (square + found[1]) + (found[0] + found[2])
    square = square + swap_cores(square)

    def viewed(stem, stride, block, mixer, pre, post, codes, head):
        return (
            stem.transpose(0, 2, 1, 3), stride.reshape(2, 1024, C), block.reshape(2, 576, C), mixer,
            pre, post, codes.T, head.transpose(0, 3, 1, 2),
        )

    sets = [
        viewed(
            stem_kernel, stride_kernels, block_kernels, block_mixers, pre_project, post_project, codebook, head_kernel
        ),
        viewed(*moments[:8]),
        viewed(*moments[8:]),
    ]
    given = [sets[i][weight] for weight in range(8) for i in range(3)]
    shapes = [(x.shape, x.dtype) for x in given]
    *news, loss_terms, norm = run_kernel(
        "adam", adam_body, (), (own_half, other_half, square, count, *given),
        (*far_out(*shapes), 4, 1), (*shapes, ((2, 64, C), F32)), limit=24, sems=66, micros=7,
    )

    def restored(stem, stride, block, mixer, pre, post, codes, head):
        return (
            stem.transpose(0, 2, 1, 3), stride.reshape(2, 4, 4, 64, C), block.reshape(2, 3, 3, 64, C), mixer,
            pre, post, codes.T, head.transpose(0, 2, 3, 1),
        )

    return (
        loss_terms.reshape(4),
        norm.reshape(()),
        *restored(*news[0::3]),
        *restored(*news[1::3]),
        *restored(*news[2::3]),
    )


def solution(mesh):
    in_specs = (
        P("dp", None, None, None),
        P("dp", None),
        P("dp", None, None),
        P(None, None, None, "tensor"),
        P(None, None, None, "tensor", None),
        P(None, None, None, "tensor", None),
        P(None, "tensor", None),
        P("tensor", None),
        P(None, "tensor"),
        P(),
        P(None, None, "tensor", None),
        P(None, None, None, "tensor"),
        P(None, None, None, "tensor", None),
        P(None, None, None, "tensor", None),
        P(None, "tensor", None),
        P("tensor", None),
        P(None, "tensor"),
        P(),
        P(None, None, "tensor", None),
        P(None, None, None, "tensor"),
        P(None, None, None, "tensor", None),
        P(None, None, None, "tensor", None),
        P(None, "tensor", None),
        P("tensor", None),
        P(None, "tensor"),
        P(),
        P(None, None, "tensor", None),
    )
    out_specs = (
        P(),
        P(),
        P(None, None, None, "tensor"),
        P(None, None, None, "tensor", None),
        P(None, None, None, "tensor", None),
        P(None, "tensor", None),
        P("tensor", None),
        P(None, "tensor"),
        P(),
        P(None, None, "tensor", None),
        P(None, None, None, "tensor"),
        P(None, None, None, "tensor", None),
        P(None, None, None, "tensor", None),
        P(None, "tensor", None),
        P("tensor", None),
        P(None, "tensor"),
        P(),
        P(None, None, "tensor", None),
        P(None, None, None, "tensor"),
        P(None, None, None, "tensor", None),
        P(None, None, None, "tensor", None),
        P(None, "tensor", None),
        P("tensor", None),
        P(None, "tensor"),
        P(),
        P(None, None, "tensor", None),
    )
    return jax.shard_map(
        on_device, mesh=mesh, in_specs=in_specs, out_specs=out_specs, check_vma=False
    )
```

```python
import math

import jax
import jax.numpy as jnp
from jax import lax
from jax.experimental import pallas as pl
from jax.experimental.pallas import tpu as pltpu
from jax.sharding import PartitionSpec as P

C = 256
E = 64
STEP = 10
SIDE = 32
CELLS = SIDE * SIDE
PADDED = CELLS + 2 * SIDE

beta_commit = 0.25
clip_norm = 0.002
beta_one = 0.9
beta_two = 0.999
adam_eps = 1e-08
decay_rate = 0.01
half_bin = 1.0 / 255.0
root_half = 0.7071067811865476
gelu_root = 0.7978845608028654
gelu_cube = 0.044715

F32 = jnp.float32
BF16 = jnp.bfloat16

UP_SHIFT = (-1, 0, 0, 1)
DOWN_PARITY = (1, 0, 1, 0)
DOWN_SHIFT = (-1, 0, 0, 1)


def here():
    index = lax.axis_index("dp")
    core = index % 2
    return lax.axis_index("tensor"), core, jnp.where(core == 0, index // 8, (index // 2) % 4)


def nn(left, right):
    return lax.dot_general(left, right, (((1,), (0,)), ((), ())), preferred_element_type=F32)


def nt(left, right):
    return lax.dot_general(left, right, (((1,), (1,)), ((), ())), preferred_element_type=F32)


def gelu(x):
    return x * (0.5 * (1.0 + jnp.tanh(gelu_root * (x + gelu_cube * (x * x * x)))))


def gelu_both(x):
    square = x * x
    t = jnp.tanh(x * (gelu_root + gelu_root * gelu_cube * square))
    share = 0.5 + 0.5 * t
    bend = 0.5 * gelu_root + 1.5 * gelu_root * gelu_cube * square
    return x * share, share + x * (1.0 - t * t) * bend


def columns(shape):
    return lax.broadcasted_iota(jnp.int32, shape, 0) % SIDE


def left_of(x):
    return jnp.where(columns(x.shape) == 0, 0.0, pltpu.roll(x, 1, 0))


def right_of(x):
    return jnp.where(columns(x.shape) == SIDE - 1, 0.0, pltpu.roll(x, x.shape[0] - 1, 0))


def clear_edges(ref, index):
    edge = jnp.zeros((SIDE, C), BF16)
    ref[index, 0:SIDE, :] = edge
    ref[index, PADDED - SIDE : PADDED, :] = edge


def store_three(ref, x):
    for index in range(3):
        clear_edges(ref, index)
    ref[0, SIDE : SIDE + CELLS, :] = left_of(x).astype(BF16)
    ref[1, SIDE : SIDE + CELLS, :] = x.astype(BF16)
    ref[2, SIDE : SIDE + CELLS, :] = right_of(x).astype(BF16)


def store_two(ref, phase, x):
    clear_edges(ref, 2 * phase)
    clear_edges(ref, 2 * phase + 1)
    moved = right_of(x) if phase % 2 == 0 else left_of(x)
    ref[2 * phase, SIDE : SIDE + CELLS, :] = x.astype(BF16)
    ref[2 * phase + 1, SIDE : SIDE + CELLS, :] = moved.astype(BF16)


def window(ref, index, shift):
    return ref[index, (shift + 1) * SIDE : (shift + 1) * SIDE + CELLS, :]


def three(ref, row_shift, col_shift):
    return window(ref, col_shift + 1, row_shift)


def two(ref, phase, row_shift, col_shift):
    return window(ref, 2 * phase + (0 if col_shift == 0 else 1), row_shift)


def own_lanes(x, tensor):
    half = jnp.where(tensor >= 2, x[:, 128:256], x[:, 0:128])
    return jnp.where(tensor % 2 == 1, pltpu.roll(half, 64, 1), half)[:, 0:64]


def lane_grid(shape):
    lane = lax.broadcasted_iota(jnp.int32, shape, 1)
    return lane // SIDE, lane % SIDE


def moved_plane(x, row_shift, col_shift):
    if row_shift == 0 and col_shift == 0:
        return x
    y = pltpu.roll(x, (-(SIDE * row_shift + col_shift)) % CELLS, 1)
    rows, cols = lane_grid(x.shape)
    keep = None
    for index, shift in ((rows, row_shift), (cols, col_shift)):
        if shift != 0:
            ok = (index < SIDE - 1) if shift == 1 else (index > 0)
            keep = ok if keep is None else (keep & ok)
    return jnp.where(keep, y, 0.0)


def same_forward(source, weight_ref, first):
    total = None
    for row in range(3):
        for col in range(3):
            term = nt(three(source, row - 1, col - 1), weight_ref[first + 3 * row + col])
            total = term if total is None else total + term
    return total


def same_backward(source, weight_ref, first):
    total = None
    for row in range(3):
        for col in range(3):
            term = nn(three(source, 1 - row, 1 - col), weight_ref[first + 3 * row + col])
            total = term if total is None else total + term
    return total


def down_forward(source, weight_ref):
    total = None
    for row in range(4):
        for col in range(4):
            phase = 2 * DOWN_PARITY[row] + DOWN_PARITY[col]
            term = nt(two(source, phase, DOWN_SHIFT[row], DOWN_SHIFT[col]), weight_ref[4 * row + col])
            total = term if total is None else total + term
    return total


def split_three(x):
    first = x.astype(BF16)
    rest = x - first.astype(F32)
    second = rest.astype(BF16)
    return first, second, (rest - second.astype(F32)).astype(BF16)


def one_hot_codes(codes_ref):
    return (
        (lax.broadcasted_iota(jnp.int32, (512, CELLS), 0) == codes_ref[...]).astype(F32).astype(BF16)
    )


def patch_body(
    sizes, image_in, codes_in, book_in, pix_out, x_out, entries_out,
    image_ref, codes_ref, book_ref, pix_ref, x_ref, entries_ref, sems,
):
    high, wide = sizes[0, 0] // 4, sizes[0, 1] // 4
    copies = copy_all(
        sems,
        [
            (image_in, image_ref), (codes_in, codes_ref), (book_in, book_ref),
            (pix_ref, pix_out), (entries_ref, entries_out), (x_ref, x_out),
        ],
    )
    start_all(copies[0:3])
    wait_all(copies[0:3])
    book = jnp.concatenate(split_three(book_ref[...]), 0)
    found = nn(book, one_hot_codes(codes_ref))
    entries_ref[...] = ((found[0:64] + found[64:128]) + found[128:192]).T
    copies[4].start()
    image = image_ref[...].astype(F32).astype(BF16)
    lane = lax.broadcasted_iota(jnp.int32, (128, CELLS), 1)
    source = lax.broadcasted_iota(jnp.int32, (128, CELLS), 0)
    row = lax.broadcasted_iota(jnp.int32, (384, CELLS), 0)
    own_row = (row // 4) % SIDE == lax.broadcasted_iota(jnp.int32, (384, CELLS), 1) // SIDE
    slot = lax.broadcasted_iota(jnp.int32, (32, 384), 0)
    line = lax.broadcasted_iota(jnp.int32, (32, 384), 1)
    pick = ((line % 4 == slot // 8) & (line // 128 == slot % 8)).astype(F32).astype(BF16)
    planes = {}
    for col in range(4):
        spread = (source == 4 * (lane % SIDE) + col).astype(F32).astype(BF16)
        lined = jnp.where(own_row, nn(image, spread), 0.0).astype(BF16)
        found = nn(pick, lined)
        for r in range(4):
            planes[r, col] = found[8 * r : 8 * r + 8]
    for r in range(4):
        for half in range(2):
            pix_ref[2 * r + half] = planes[r, 2 * half] + pltpu.roll(planes[r, 2 * half + 1], 4, 0)
    copies[3].start()
    rows, cols = lane_grid((8, CELLS))
    channel = lax.broadcasted_iota(jnp.int32, (8, CELLS), 0)
    inside = (rows < high) & (cols < wide) & (channel < 3)
    planes = {key: jnp.where(inside, value / 127.5 - 1.0, 0.0) for key, value in planes.items()}
    moved = {}
    for r in range(-1, 5):
        for c in range(-1, 5):
            moved[r, c] = moved_plane(planes[r % 4, c % 4], r // 4, c // 4)
    for p in range(2):
        for q in range(2):
            for kh in range(4):
                for kw in range(0, 4, 2):
                    r, c = 2 * p + kh - 1, 2 * q + kw - 1
                    tap = 4 * kh + kw
                    x_ref[8 * tap : 8 * tap + 16, (2 * p + q) * CELLS : (2 * p + q + 1) * CELLS] = (
                        jnp.concatenate([moved[r, c], moved[r, c + 1]], 0).astype(BF16)
                    )
    copies[5].start()
    wait_all(copies[3:])


def copy_all(sems, pairs):
    return [pltpu.make_async_copy(source, target, sems.at[i]) for i, (source, target) in enumerate(pairs)]


def start_all(copies):
    for copy in copies:
        copy.start()


def wait_all(copies):
    for copy in copies:
        copy.wait()


def count_body(sizes, count_ref):
    count_ref[...] = jnp.full((8, 128), (sizes[0, 0] // 4) * (sizes[0, 1] // 4), jnp.int32).astype(F32)


def pack_first_body(
    stride_in, stem_in, head_in, pre_in, post_in, out,
    stride_ref, stem_ref, head_ref, pre_ref, post_ref, out_ref, sems,
):
    copies = copy_all(
        sems,
        [
            (stem_in, stem_ref), (head_in, head_ref), (pre_in, pre_ref), (post_in, post_ref),
            (stride_in.at[0, 0:8], stride_ref.at[0:8]), (stride_in.at[0, 8:16], stride_ref.at[8:16]),
            (out_ref.at[8:10], out.at[8:10]), (out_ref.at[0:8], out.at[0:8]), (out_ref.at[10:18], out.at[10:18]),
        ],
    )
    start_all(copies[0:6])
    wait_all(copies[0:4])

    def ordered(ref, per):
        rows = jnp.concatenate([ref[kh, c] for kh in range(4) for c in range(per)], 0)
        count = 16 * per
        slot = lax.broadcasted_iota(jnp.int32, (128, count), 0)
        line = lax.broadcasted_iota(jnp.int32, (128, count), 1)
        channel = slot % 8
        if per == 6:
            channel = jnp.where(channel % 4 == 3, per, channel - channel // 4)
        wanted = (slot // 32) * 4 * per + channel * 4 + (slot // 8) % 4
        pick = ((line == wanted) & (channel < per)).astype(F32).astype(BF16)
        return nn(pick, rows.astype(BF16)).T

    out_ref[8] = jnp.concatenate([ordered(stem_ref, 3), ordered(head_ref, 6)], 1).astype(BF16)
    thin = jnp.concatenate([pre_ref[...], post_ref[...].T], 1)
    out_ref[9] = jnp.concatenate([thin, thin], 1).astype(BF16)
    copies[6].start()
    for k in range(2):
        copies[4 + k].wait()
        out_ref[10 * k : 10 * k + 8] = stride_ref[8 * k : 8 * k + 8].astype(BF16)
        copies[7 + k].start()
    wait_all(copies[6:])


def pack_rest_body(stride_in, block_in, mix_in, out, stride_ref, block_ref, mix_ref, out_ref, sems):
    copies = copy_all(
        sems,
        [
            (block_in, block_ref), (mix_in, mix_ref), (stride_in.at[1], stride_ref), (out_ref, out),
        ],
    )
    start_all(copies[0:3])
    wait_all(copies[0:3])
    for b in range(2):
        out_ref[18 * b : 18 * b + 9] = block_ref[b].astype(BF16)
        out_ref[18 * b + 9] = mix_ref[b].astype(BF16)
        out_ref[18 * b + 10 : 18 * b + 18] = stride_ref[8 * b : 8 * b + 8].astype(BF16)
    start_all(copies[3:])
    wait_all(copies[3:])


def gather_pairs(ref, parts, tensor, core, rotated, low, high, half_low):
    def rows(step):
        if rotated and isinstance(step, int):
            return pl.ds(64 * step, 64)
        return pl.ds(pl.multiple_of((64 * step if rotated else ((tensor + step) % 4) * 64), 64), 64)

    count = ref.shape[0] // 2
    pairs = []
    for part, step in zip(parts[0:3], (0, 1 + 2 * core, 3 - 2 * core), strict=True):
        for k, start in enumerate((low, high)):
            pairs.append((part.at[start : start + count], ref.at[count * k : count * k + count, rows(step), :]))
    for part, half in ((parts[3], core), (parts[4], 1 - core)):
        source = part.at[pl.ds(half_low(half), count)]
        pairs.append((source, ref.at[pl.ds(count * half, count), rows(2), :]))
    return pairs


def block_forward(resid, u_ref, w_ref, first, v_ref, q_ref):
    value, v_ref[...] = gelu_both(same_forward(u_ref, w_ref, first))
    act = value.astype(BF16)
    q_ref[...] = act
    return resid + nn(act, w_ref[first + 9])


def front_body(
    x_in, own, near, far, mine, other,
    r_ref, u_ref, slope_out, a_out, w_out, stem_out, head_out, pre_out, post_out, patch_out,
    x_ref, small_ref, slope_ref, a_ref, w_ref, stem_ref, head_ref, pre_ref, post_ref, patch_ref, sems,
):
    tensor, core, _ = here()
    small = [part.at[8:10] for part in (own, near, far)] + [mine.at[pl.ds(8 * (1 - core), 2)]]
    pairs = [(x_in, x_ref)] + [(part, small_ref.at[k]) for k, part in enumerate(small)]
    pairs += gather_pairs(w_ref, (own, near, far, mine, other), tensor, core, False, 0, 10, lambda half: 2 * half)
    copies = copy_all(sems, pairs)
    start_all(copies)
    outs = [(stem_ref, stem_out), (head_ref, head_out), (pre_ref, pre_out), (post_ref, post_out), (w_ref, w_out)]
    outs += [(a_ref.at[2 * p : 2 * p + 2], a_out.at[2 * p : 2 * p + 2]) for p in range(4)]
    outs += [(patch_ref, patch_out), (slope_ref, slope_out)]
    writes = [
        pltpu.make_async_copy(source, target, sems.at[len(copies) + i]) for i, (source, target) in enumerate(outs)
    ]
    wait_all(copies[0:5])
    for k, step in enumerate((0, 1 + 2 * core, 3 - 2 * core, 2)):
        rows = pl.ds(pl.multiple_of(((tensor + step) % 4) * 64, 64), 64)
        turned = 64 * step if isinstance(step, int) else pl.multiple_of(64 * step, 64)
        stem_ref[rows, :] = small_ref[k, 0, :, 0:128]
        head_ref[pl.ds(turned, 64), :] = small_ref[k, 0, :, 128:256]
        pre_ref[rows, :] = small_ref[k, 1, :, 0:64]
        post_ref[rows, :] = small_ref[k, 1, :, 64:128]
    start_all(writes[0:4])
    for phase in range(4):
        patch = x_ref[:, phase * CELLS : (phase + 1) * CELLS].T
        patch_ref[phase * CELLS : (phase + 1) * CELLS, :] = patch
        store_two(a_ref, phase, gelu(nt(patch, stem_ref[...])))
        writes[5 + phase].start()
    writes[9].start()
    wait_all(copies[5:])
    writes[4].start()
    resid = down_forward(a_ref, w_ref)
    r_ref[...] = resid
    value, slope_ref[...] = gelu_both(resid)
    writes[10].start()
    store_three(u_ref, value)
    wait_all(writes)


def valid_cells(sizes):
    cell = lax.broadcasted_iota(jnp.int32, (CELLS, E), 0)
    return (cell // SIDE < sizes[0, 0] // 4) & (cell % SIDE < sizes[0, 1] // 4)


def poly(x, coefs):
    total = jnp.full_like(x, coefs[0])
    for c in coefs[1:]:
        total = total * x + c
    return total


ERFC_LOW = (
    2.326819970068386e-2, -1.387039388740657e-1, 3.687424674597105e-1, -5.824733027278666e-1,
    6.210004621745983e-1, -4.944515323274145e-1, 3.404879937665872e-1, -2.741127028184656e-1,
    5.638259427386472e-1,
)
ERFC_HIGH = (
    -1.047766399936249e1, 1.297719955372516e1, -7.495518717768503e0, 2.921019019210786e0,
    -1.015265279202700e0, 4.218463358204948e-1, -2.820767439740514e-1, 5.641895067754075e-1,
)
ERF_NEAR = (
    7.853861353153693e-5, -8.010193625184903e-4, 5.188327685732524e-3, -2.685381193529856e-2,
    1.128358514861418e-1, -3.761262582423300e-1, 1.128379165726710e0,
)


def erfc(x):
    size = jnp.abs(x)
    square = x * x
    far_exp = jnp.exp(-square)
    recip = 1.0 / jnp.maximum(size, 0.5)
    y = recip * recip
    far = far_exp * recip * jnp.where(size < 2.0, poly(y, ERFC_LOW), poly(y, ERFC_HIGH))
    far = jnp.where(x < 0, 2.0 - far, far)
    near = 1.0 - x * poly(square, ERF_NEAR)
    return jnp.where(size > 1.0, far, near), far_exp


def likelihood(center_out, scale_out, pix, keep, scale):
    target = pix / 127.5 - 1.0
    center = jnp.tanh(center_out)
    decay = jnp.exp(-jnp.abs(scale_out))
    sigma = 0.25 + (jnp.maximum(scale_out, 0.0) + jnp.log(1.0 + decay))
    gate = jnp.where(scale_out >= 0, 1.0, decay) / (1.0 + decay)
    low_end, high_end = pix == 0.0, pix == 255.0
    lower = jnp.where(low_end, -40.0, (target - half_bin - center) / sigma)
    upper = jnp.where(high_end, 40.0, (target + half_bin - center) / sigma)
    right = lower + upper > 0
    tail_a, exp_a = erfc(jnp.where(right, lower, -upper) * root_half)
    tail_b, exp_b = erfc(jnp.where(right, upper, -lower) * root_half)
    mass = 0.5 * (tail_a - tail_b)
    bits = jnp.where(keep, jnp.log(mass), 0.0)
    density = 1.0 / math.sqrt(2.0 * math.pi)
    slope = jnp.where(keep, scale * density / mass, 0.0)
    low_slope = jnp.where(low_end, 0.0, -slope * jnp.where(right, exp_a, exp_b))
    high_slope = jnp.where(high_end, 0.0, slope * jnp.where(right, exp_b, exp_a))
    center_grad = -(low_slope + high_slope) / sigma
    sigma_grad = -(low_slope * lower + high_slope * upper) / sigma
    return bits, center_grad * (1.0 - center * center), sigma_grad * gate


def head_links():
    for p in range(2):
        for q in range(2):
            for kh in range(4):
                for kw in range(4):
                    up, left = p + UP_SHIFT[kh], q + UP_SHIFT[kw]
                    out = (2 * p + kh % 2, 2 * q + kw % 2)
                    yield out, 4 * kh + kw, 2 * (up % 2) + left % 2, up // 2, left // 2


QUARTER = 448
KINDS = {"stride": (0, 256), "block": (256, 144), "mixer": (400, 16), "codes": (416, 16), "small": (432, 16)}


def store_rows(g_ref, kind, start, value):
    base, size = KINDS[kind]
    done = 0
    while done < value.shape[0]:
        place = start + done
        count = min(size - place % size, value.shape[0] - done)
        first = base + place % size
        g_ref[place // size, first : first + count, :] = value[done : done + count]
        done += count


def with_scalar(x, scalar):
    row = lax.broadcasted_iota(jnp.int32, (64, 64), 0)
    lane = lax.broadcasted_iota(jnp.int32, (64, 64), 1)
    return jnp.concatenate([x, jnp.where((row == 0) & (lane == 0), scalar, 0.0)], 1)


def block_backward(grad_out, resid_ref, u_ref, v_ref, q_ref, w_ref, first, dv_ref, g_ref):
    low = grad_out.astype(BF16)
    own_q = q_ref[:, 0:128].astype(F32).T[0:64].astype(BF16)
    store_rows(g_ref, "mixer", 0, nn(own_q, low))
    mid = nt(low, w_ref[first + 9])
    inner = v_ref[...] * mid
    store_three(dv_ref, inner)
    own = inner[:, 0:128].T[0:64].astype(BF16)
    for row in range(3):
        for col in range(3):
            tap = 3 * row + col
            store_rows(g_ref, "block", 64 * tap, nn(own, three(u_ref, row - 1, col - 1)))
    return grad_out + resid_ref[...] * same_backward(dv_ref, w_ref, first)


def forward_blocks(
    sizes, r0_ref, u0_ref, w_ref, pre_ref, post_ref, entries_ref,
    v0_ref, q0_ref, r1_ref, act_ref, diff_ref, zq_ref, r2_ref, u2_ref, v1_ref, q1_ref, r3_ref, u3_ref, waits,
):
    resid = block_forward(r0_ref[...], u0_ref, w_ref, 0, v0_ref, q0_ref)
    value, r1_ref[...] = gelu_both(resid)
    act = value.astype(BF16)
    act_ref[...] = act
    wait_all(waits)
    latent = nn(act, pre_ref[...])
    entries = entries_ref[...]
    diff = latent - entries
    diff_ref[...] = diff
    code = (latent + (entries - latent)).astype(BF16)
    zq_ref[...] = code
    resid = nt(code, post_ref[...])
    value, r2_ref[...] = gelu_both(resid)
    store_three(u2_ref, value)
    resid = block_forward(resid, u2_ref, w_ref, 10, v1_ref, q1_ref)
    value, r3_ref[...] = gelu_both(resid)
    store_three(u3_ref, value)
    return (1.0 + beta_commit) * jnp.sum(jnp.where(valid_cells(sizes), diff * diff, 0.0))


def main_body(
    sizes, total_ref, r0_ref, u0_ref, own, near, far, mine, other,
    pre_in, post_in, entries_in, head_in, pix_in, codes_in, stem_in, r0s_in, w0_in, a_in, x_in, patch_in,
    keep_ref, send_ref,
    wb_ref, w_ref, pre_ref, post_ref, entries_ref, head_ref, pix_ref, codes_ref, stem_ref, r0s_ref, w0_ref, a_ref, x_ref, patch_ref,
    v0_ref, q0_ref, r1_ref, act_ref, diff_ref, zq_ref, r2_ref, u2_ref, v1_ref, q1_ref, r3_ref, u3_ref,
    h4_ref, a4_ref, prod_ref, q_ref, dh_ref, dv_ref, back_ref, late_ref, gd_ref, g_ref, sems,
):
    tensor, core, _ = here()
    parts = (own, near, far, mine, other)
    pairs = gather_pairs(wb_ref, parts, tensor, core, True, 0, 18, lambda half: 0)
    pairs += [(pre_in, pre_ref), (post_in, post_ref), (entries_in, entries_ref)]
    pairs += gather_pairs(w_ref, parts, tensor, core, True, 10, 28, lambda half: 10)
    pairs += [(head_in, head_ref), (pix_in, pix_ref), (codes_in, codes_ref), (stem_in, stem_ref)]
    pairs += [(r0s_in, r0s_ref), (w0_in, w0_ref), (a_in, a_ref), (x_in, x_ref), (patch_in, patch_ref)]
    copies = copy_all(sems, pairs)
    start_all(copies[0:8])
    wait_all(copies[0:8])
    start_all(copies[8:])
    vq = forward_blocks(
        sizes, r0_ref, u0_ref, wb_ref, pre_ref, post_ref, entries_ref,
        v0_ref, q0_ref, r1_ref, act_ref, diff_ref, zq_ref, r2_ref, u2_ref, v1_ref, q1_ref, r3_ref, u3_ref, copies[8:11],
    )
    wait_all(copies[11:19])
    decode_back(
        sizes, total_ref, pix_ref, r3_ref, u3_ref, head_ref, r2_ref, u2_ref, v1_ref, q1_ref, wb_ref,
        gd_ref, w_ref, h4_ref, a4_ref, prod_ref, q_ref, dh_ref, dv_ref, zq_ref, post_ref, back_ref, copies[19:21],
    )
    wait_all(copies[21:])
    encode_back(
        sizes, total_ref, vq, back_ref, diff_ref, codes_ref, r1_ref, act_ref, pre_ref, stem_ref, x_ref, patch_ref, a_ref,
        r0s_ref, u0_ref, v0_ref, q0_ref, wb_ref, w0_ref, gd_ref, keep_ref, send_ref, dv_ref, dh_ref, g_ref, late_ref,
    )


def decode_back(
    sizes, total_ref, pix_ref, r3_ref, u3_ref, head_ref, r2_ref, u2_ref, v1_ref, q1_ref, w1_ref,
    g_ref, w_ref, h4_ref, a4_ref, prod_ref, q_ref, dh_ref, dv_ref, zq_ref, post_ref, back_ref, early,
):
    tensor, _, _ = here()
    high, wide = sizes[0, 0] // 4, sizes[0, 1] // 4
    wait_all(early)
    head = head_ref[...].astype(F32).T.astype(BF16)
    for p in range(2):
        for q in range(2):
            phase = 2 * p + q
            total = None
            for kh in (p, p + 2):
                for kw in (q, q + 2):
                    term = nt(three(u3_ref, UP_SHIFT[kh], UP_SHIFT[kw]), w_ref[4 * kh + kw])
                    total = term if total is None else total + term
            value, h4_ref[phase] = gelu_both(total)
            act = value.astype(BF16)
            a4_ref[phase] = act
            prod_ref[:, phase * CELLS : (phase + 1) * CELLS] = nt(head, act)
    outs = {}
    for out, tap, phase, up, left in head_links():
        term = moved_plane(
            prod_ref[8 * tap : 8 * tap + 8, phase * CELLS : (phase + 1) * CELLS], up, left
        )
        outs[out] = term if out not in outs else outs[out] + term
    sub = lax.broadcasted_iota(jnp.int32, (8, CELLS), 0)
    rows, cols = lane_grid((8, CELLS))
    keep = (rows < high) & (cols < wide) & (sub % 4 != 3)
    first = sub < 4
    scale = -1.0 / (math.log(2.0) * 48.0 * total_ref[0, 0])
    grads = {}
    bits = None
    for pair in range(8):
        row, col = pair // 2, 2 * (pair % 2)
        one, other = outs[row, col], outs[row, col + 1]
        centers = jnp.where(first, one, pltpu.roll(other, 4, 0))
        scales = jnp.where(first, pltpu.roll(one, 4, 0), other)
        part, center_grad, scale_grad = likelihood(centers, scales, pix_ref[pair], keep, scale)
        bits = part if bits is None else bits + part
        grads[row, col] = jnp.where(first, center_grad, pltpu.roll(scale_grad, 4, 0))
        grads[row, col + 1] = jnp.where(first, pltpu.roll(center_grad, 4, 0), scale_grad)
    bits = -jnp.sum(bits) / math.log(2.0)
    found = {}
    for out, tap, phase, up, left in head_links():
        found[tap, phase] = moved_plane(grads[out], -up, -left)
    for phase in range(4):
        for tap in range(0, 16, 2):
            q_ref[8 * tap : 8 * tap + 16, phase * CELLS : (phase + 1) * CELLS] = jnp.concatenate(
                [found[tap, phase], found[tap + 1, phase]], 0
            ).astype(BF16)
    head_grad = None
    for phase in range(4):
        spread = q_ref[:, phase * CELLS : (phase + 1) * CELLS]
        term = nn(spread, a4_ref[phase, :, 0:64])
        head_grad = term if head_grad is None else head_grad + term
        slope = h4_ref[phase] * nn(spread.T, head)
        store_two(dh_ref, phase, slope)
        own = slope[:, 0:128].T[0:64].astype(BF16)
        for kh in (phase // 2, phase // 2 + 2):
            for kw in (phase % 2, phase % 2 + 2):
                tap = 4 * kh + kw
                store_rows(g_ref, "stride", 64 * tap, nn(own, three(u3_ref, UP_SHIFT[kh], UP_SHIFT[kw])))
    total = None
    for kh in range(4):
        for kw in range(4):
            phase = 2 * (kh % 2) + kw % 2
            term = nn(two(dh_ref, phase, -UP_SHIFT[kh], -UP_SHIFT[kw]), w_ref[4 * kh + kw])
            total = term if total is None else total + term
    grad = r3_ref[...] * total
    grad = block_backward(grad, r2_ref, u2_ref, v1_ref, q1_ref, w1_ref, 10, dv_ref, g_ref)
    low = grad.astype(BF16)
    post_grad = nn(zq_ref[...].astype(F32).T.astype(BF16), own_lanes(grad, tensor).astype(BF16))
    small = jnp.concatenate([post_grad, head_grad[0:64], head_grad[64:128]], 1)
    store_rows(g_ref, "small", 0, with_scalar(small, bits))
    back_ref[...] = nn(low, post_ref[...])


def encode_back(
    sizes, total_ref, vq, back_ref, diff_ref, codes_ref, r1_ref, act_ref, pre_ref, stem_ref, x_ref, patch_ref, a_ref,
    r0_ref, u_ref, v_ref, q_ref, wb_ref, w_ref, gd_ref, keep_ref, send_ref, dv_ref, dr_ref, g_ref, late_ref,
):
    tensor, core, _ = here()
    scaled = jnp.where(valid_cells(sizes), diff_ref[...] / (64.0 * total_ref[0, 0]), 0.0)
    dz = (back_ref[...] + 2.0 * beta_commit * scaled).astype(BF16)
    hot = one_hot_codes(codes_ref)
    found = nt(jnp.concatenate(split_three((-2.0 * scaled).T), 0), hot)
    codes = (found[0:64] + found[64:128]) + found[128:192]
    store_rows(g_ref, "codes", 0, codes[:, 0:256])
    late_ref[...] = codes[:, 256:512]
    act = own_lanes(act_ref[...].astype(F32), tensor)
    pre_grad = nn(act.T.astype(BF16), dz)
    grad = r1_ref[...] * nt(dz, pre_ref[...])
    grad = block_backward(grad, r0_ref, u_ref, v_ref, q_ref, wb_ref, 0, dv_ref, g_ref)
    store_three(dr_ref, grad)
    own = own_lanes(grad, tensor).T.astype(BF16)
    for kh in range(4):
        for kw in range(4):
            tap = 4 * kh + kw
            phase = 2 * DOWN_PARITY[kh] + DOWN_PARITY[kw]
            term = nn(own, two(a_ref, phase, DOWN_SHIFT[kh], DOWN_SHIFT[kw]))
            store_rows(g_ref, "stride", 64 * tap, term)
    line = lax.broadcasted_iota(jnp.int32, (C, C), 0)
    lane = lax.broadcasted_iota(jnp.int32, (C, C), 1)
    shifts = [(up, left) for up in (-1, 0, 1) for left in (-1, 0, 1)]
    before = total = None
    stem = stem_ref[pl.ds(pl.multiple_of(64 * tensor, 64), 64), :].astype(F32).T.astype(BF16)
    for phase in range(4):
        place = (lane[0:64] == line[0:64] + 64 * phase).astype(F32).astype(BF16)
        wide = nn(stem, place).astype(BF16)
        term = nn(patch_ref[phase * CELLS : (phase + 1) * CELLS, :], wide)
        before = term if before is None else before + term
    picks = [
        ((lane == line - 64 * tensor + 64 * phase) & (lane // 64 == phase)).astype(F32).astype(BF16) for phase in range(4)
    ]
    for up, left in shifts:
        weight = None
        for kh in range(4):
            for kw in range(4):
                if (-DOWN_SHIFT[kh], -DOWN_SHIFT[kw]) == (up, left):
                    term = nn(w_ref[4 * kh + kw], picks[2 * DOWN_PARITY[kh] + DOWN_PARITY[kw]])
                    weight = term if weight is None else weight + term
        term = nn(three(dr_ref, up, left), weight.astype(BF16))
        total = term if total is None else total + term
    slope = (gelu_both(before)[1] * total).astype(BF16)
    stem_grad = None
    for phase in range(4):
        term = nn(x_ref[:, phase * CELLS : (phase + 1) * CELLS], slope)[:, 64 * phase : 64 * phase + 64]
        stem_grad = term if stem_grad is None else stem_grad + term
    small = jnp.concatenate([pre_grad, stem_grad[0:64], stem_grad[64:128]], 1)
    store_rows(g_ref, "small", 0, with_scalar(small, vq))
    base = KINDS["codes"][0]
    for part in range(4):
        gd_ref[part, base : base + 16, :] = late_ref[16 * part : 16 * part + 16, :]

    @pl.when(core == 0)
    def _():
        keep_ref[...] = g_ref[...]
        for part in range(4):
            put_sent(send_ref.at[part], gd_ref[part])

    @pl.when(core == 1)
    def _():
        keep_ref[...] = gd_ref[...]
        for part in range(4):
            put_sent(send_ref.at[part], g_ref[part])


SENT = QUARTER + 32
SMALL_ROWS = KINDS["small"][0]


def put_sent(out, value):
    out[0:SMALL_ROWS, :] = value[0:SMALL_ROWS].astype(BF16)
    for k, part in enumerate(split_three(value[SMALL_ROWS:QUARTER])):
        out[SMALL_ROWS + 16 * k : SMALL_ROWS + 16 * k + 16, :] = part


def small_of(ref):
    parts = [ref[SMALL_ROWS + 16 * k : SMALL_ROWS + 16 * k + 16, :].astype(F32) for k in range(3)]
    return (parts[0] + parts[1]) + parts[2]


def whole(ref):
    return jnp.concatenate([ref[0:SMALL_ROWS, :].astype(F32), small_of(ref)], 0)


def add_cores_body(keep_ref, other_ref, own_ref, *outs):
    _, _, place = here()
    own_ref[...] = keep_ref[place] + whole(other_ref.at[place])
    for k, out in enumerate(outs):
        part = (place + 1 + k) % 4
        put_sent(out, keep_ref[part] + whole(other_ref.at[part]))


def four(own, one, two_on, three_on):
    return (own + whole(two_on)) + (whole(one) + whole(three_on))


def add_first_body(own, one, two_on, three_on, out):
    put_sent(out, four(own[...], one, two_on, three_on))


def add_second_body(own, one, two_on, three_on, out):
    put_sent(out, four(whole(own), one, two_on, three_on))


def join_body(own, one, two_on, three_on, half_ref, square_ref):
    _, _, place = here()
    row = lax.broadcasted_iota(jnp.int32, (QUARTER, C), 0)
    lane = lax.broadcasted_iota(jnp.int32, (QUARTER, C), 1)
    share = jnp.where((row >= KINDS["codes"][0]) & (row < SMALL_ROWS), 0.25, 1.0)
    share = jnp.where((row >= SMALL_ROWS) & (lane >= 192), 0.0, share)
    total = jnp.zeros((QUARTER, C), F32)
    for k, part in enumerate((own, one, two_on, three_on)):
        half_ref[(place + k) % 4] = part[...]
        value = whole(part)
        total = total + value * value
    square_ref[...] = jnp.full((8, 128), jnp.sum(total * share), F32)


def adam(weight, moment, second, grad, rate):
    m_new = beta_one * moment + (1.0 - beta_one) * grad
    v_new = beta_two * second + ((1.0 - beta_two) * grad) * grad
    change = (rate / (1.0 - beta_one**STEP)) * m_new
    size = jnp.sqrt((1.0 / (1.0 - beta_two**STEP)) * v_new) + adam_eps
    return (1.0 - rate * decay_rate) * weight - change / size, m_new, v_new


RATES = (
    48.0 ** (-0.5),
    (16.0 * C) ** (-0.5),
    (9.0 * C) ** (-0.5),
    C ** (-0.5),
    C ** (-0.5),
    E ** (-0.5),
    0.6,
    (4.0 * C) ** (-0.5),
)


def adam_body(half_ref, other_ref, square_ref, total_ref, *refs):
    _, core, _ = here()
    given, outs, loss_ref, norm_ref = refs[0:24], refs[24:48], refs[48], refs[49]
    results, small_ref, sems = refs[50:74], refs[74], refs[75]
    norm = jnp.sqrt(square_ref[...])
    factor = jnp.minimum(1.0, clip_norm / (norm + 1e-06))[0:1, 0:1]
    norm_ref[0, 0] = jnp.max(norm)

    def rows_of(side, part, kind):
        if kind == "small":
            return jnp.where(core == side, small_of(half_ref.at[part]), small_of(other_ref.at[part]))
        base, size = KINDS[kind]
        mine, theirs = half_ref[part, base : base + size, :], other_ref[part, base : base + size, :]
        return jnp.where(core == side, mine.astype(F32), theirs.astype(F32))

    def update(weight, index, grad):
        values = [given[3 * weight + i][index] for i in range(3)]
        for i, value in enumerate(adam(*values, factor * grad, RATES[weight])):
            results[3 * weight + i][index] = value

    copies = []

    def finish(weight, index=None):
        for i in range(3):
            source, target = results[3 * weight + i], outs[3 * weight + i]
            if index is not None:
                source, target = source.at[index], target.at[index]
            copies.append(pltpu.make_async_copy(source, target, sems.at[len(copies)]))
            copies[-1].start()

    for side in range(2):
        for part in range(4):
            small_ref[side, 16 * part : 16 * part + 16, :] = rows_of(side, part, "small")
            update(3, (side, pl.ds(16 * part, 16), slice(None)), rows_of(side, part, "mixer"))
            update(6, (pl.ds(16 * part, 16), pl.ds(256 * side, 256)), rows_of(side, part, "codes"))
    finish(3)
    finish(6)
    for weight, side, channels in ((0, 0, 3), (7, 1, 6)):
        spread = small_ref[side, :, 64:192]
        for kh in range(4):
            block = spread[32 * (kh % 2) : 32 * (kh % 2) + 32, 64 * (kh // 2) : 64 * (kh // 2) + 64]
            for c in range(channels):
                slot = c + (c // 3 if channels == 6 else 0)
                lines = jnp.concatenate([block[8 * kw + slot : 8 * kw + slot + 1] for kw in range(4)], 0)
                update(weight, (kh, c), lines)
        finish(weight)
    for weight, side in ((4, 0), (5, 1)):
        update(weight, (slice(None), slice(None)), small_ref[side, :, 0:64])
        finish(weight)
    for weight, kind in ((1, "stride"), (2, "block")):
        size = KINDS[kind][1]
        for side in range(2):
            for part in range(4):
                index = (side, pl.ds(size * part, size), slice(None))
                update(weight, index, rows_of(side, part, kind))
                finish(weight, index)
    first = (lax.broadcasted_iota(jnp.int32, (16, 64), 0) == 0) & (lax.broadcasted_iota(jnp.int32, (16, 64), 1) == 0)
    for slot, side, share in ((0, 1, 48.0), (2, 0, 64.0)):
        loss_ref[0, slot] = jnp.sum(jnp.where(first, small_ref[side, 0:16, 192:256], 0.0))
        loss_ref[0, slot + 1] = share * total_ref[0, 0]
    wait_all(copies)


SMEM = pl.BlockSpec(memory_space=pltpu.SMEM)
VMEM = pl.BlockSpec(memory_space=pltpu.VMEM)


def run_kernel(name, body, scalars, arrays, outs, scratch=(), limit=6, sems=0, micros=1):
    anywhere = pl.BlockSpec(memory_space=pl.ANY)
    shapes, out_specs, specs, given = [], [], [SMEM] * len(scalars), list(scalars)
    for out in outs:
        if isinstance(out, int):
            shapes.append(pltpu.SMEM((1, out), F32))
            out_specs.append(SMEM)
        elif out[0] == "far":
            shapes.append(pltpu.HBM(*out[1:]))
            out_specs.append(anywhere)
        else:
            shapes.append(pltpu.VMEM(*out))
            out_specs.append(VMEM)
    for array in arrays:
        if isinstance(array, tuple):
            place, array = array
            given.append(pltpu.with_memory_space_constraint(array, pltpu.HBM) if place == "far" else array)
            specs.append(anywhere)
        else:
            given.append(pltpu.with_memory_space_constraint(array, pltpu.VMEM))
            specs.append(VMEM)
    return pl.pallas_call(
        body,
        out_shape=shapes,
        in_specs=specs,
        out_specs=out_specs,
        scratch_shapes=[pltpu.VMEM(*s) for s in scratch] + ([pltpu.SemaphoreType.DMA((sems,))] if sems else []),
        compiler_params=pltpu.CompilerParams(vmem_limit_bytes=limit * 2**20),
        cost_estimate=pl.CostEstimate(flops=int(micros * 1.1e9), bytes_accessed=0, transcendentals=0),
        name=name,
    )(*given)


THREE = ((3, PADDED, C), BF16)
EIGHT = ((8, PADDED, C), BF16)
WIDE = ((CELLS, C), F32)
WIDE_LOW = ((CELLS, C), BF16)
TWENTY = ((20, C, C), BF16)
THIN = ((CELLS, E), F32)
THIN_LOW = ((CELLS, E), BF16)
PATCH = ((4 * CELLS, 128), BF16)


def far(*arrays):
    return tuple(("far", array) for array in arrays)


def received(parts):
    return (("far", parts[0]), *(("any", part) for part in parts[1:]))


def far_out(*shapes):
    return tuple(("far", *shape) for shape in shapes)


SIXTEEN = ((16, C, C), BF16)


BOTH = ("dp", "tensor")


def send(value, target):
    pairs = []
    for x in range(4):
        for z in range(4):
            for core in range(2):
                for y in range(4):
                    to = target(x, z, core, y)
                    pairs.append(
                        (
                            ((x * 4 + z) * 2 + core) * 4 + y,
                            (((to[0] % 4) * 4 + to[1] % 4) * 2 + to[2]) * 4 + to[3] % 4,
                        )
                    )
    return lax.ppermute(value, BOTH, pairs)


def swap_cores(value):
    return send(value, lambda x, z, core, y: (x, z, 1 - core, y))


def along_first(value, k):
    return send(value, lambda x, z, core, y: (x + k, z, core, y) if core == 0 else (x, z + k, core, y))


def along_second(value, k):
    return send(value, lambda x, z, core, y: (x, z + k, core, y) if core == 0 else (x + k, z, core, y))


def three_others(along, *values, back=False):
    found = {}
    for k in (1, 3, 2):
        found[k] = along(values[k - 1] if len(values) > 1 else values[0], -k if back else k)
    return [found[k] for k in (1, 2, 3)]


def along_tensor(value, k):
    return send(value, lambda x, z, core, y: (x, z, core, y + k))


def from_one_side(local):
    return send(local, lambda x, z, core, y: (x, z, core, y - 1 if core == 0 else y + 1))


def after(value, *others):
    return lax.optimization_barrier((value, *others))[0]


def on_device(
    pixels,
    image_sizes,
    code_indices,
    stem_kernel,
    stride_kernels,
    block_kernels,
    block_mixers,
    pre_project,
    post_project,
    codebook,
    head_kernel,
    *moments,
):
    def add_along(value, step, along_x):
        return value + send(value, lambda x, z, core, y: (x ^ step, z, core, y) if along_x else (x, z ^ step, core, y))

    image_sizes = pltpu.with_memory_space_constraint(image_sizes, pltpu.HBM)
    stem_rows = stem_kernel.transpose(0, 2, 1, 3)
    head_rows = head_kernel.transpose(0, 3, 1, 2)
    stride_rows = stride_kernels.reshape(2, 16, 64, C)
    block_rows = block_kernels.reshape(2, 9, 64, C)
    small = (((E, E), F32), ((E, E), F32))
    taps = lambda count: ((count, 64, C), BF16)
    core = lax.axis_index("dp") % 2

    def passed_on(near, step, taps):
        return from_one_side(lax.dynamic_slice_in_dim(near, core * step, taps, 0))

    (first,) = run_kernel(
        "pack_first", pack_first_body, (), far(stride_rows, stem_rows, head_rows, pre_project, post_project),
        far_out(taps(18)),
        (((16, 64, C), F32), ((4, 3, 4, 64), F32), ((4, 6, 4, 64), F32), *small, taps(18)), limit=8, sems=9, micros=3,
    )
    near0 = from_one_side(first)
    (count,) = run_kernel("count", count_body, (after(image_sizes, first),), (), (((8, 128), F32),))
    (second,) = run_kernel(
        "pack_rest", pack_rest_body, (), far(stride_rows, block_rows, after(block_mixers, first)),
        far_out(taps(36)),
        (((16, 64, C), F32), ((2, 9, 64, C), F32), ((2, 64, C), F32), taps(36)), limit=10, sems=4, micros=3,
    )
    near1 = from_one_side(second)
    count = add_along(count, 1, True)
    code_row = code_indices.reshape(1, CELLS)
    image = after(pixels.reshape(384, 128), second, count)
    planes, lanes = ((8, 8, CELLS), F32), ((128, 4 * CELLS), BF16)
    pix, xt, entries = run_kernel(
        "patches", patch_body, (image_sizes,), far(image, code_row, codebook.T), far_out(planes, lanes, THIN),
        (((384, 128), jnp.int32), ((1, CELLS), jnp.int32), ((E, 512), F32), planes, lanes, THIN), limit=12, sems=6, micros=20,
    )
    count = add_along(count, 3, True)
    near0, xt, count = lax.optimization_barrier((near0, xt, count))
    mine0 = passed_on(near0, 8, 10)
    stride0 = (first, near0, swap_cores(near0))
    count = add_along(count, 1, False)
    mine0, count = lax.optimization_barrier((mine0, count))
    stride0 += (mine0, swap_cores(mine0))
    near1, xt, count, *stride0 = lax.optimization_barrier((near1, xt, count, *stride0))
    mine1 = passed_on(near1, 18, 18)
    count = add_along(count, 3, False)
    small = (((C, 128), BF16), ((C, 128), BF16), ((C, E), BF16), ((C, E), BF16))
    r0, u0, slope0, av, w0, stem, head, pre, post, patch = run_kernel(
        "front", front_body, (), (*far(xt), *received(stride0)), (WIDE, THREE, *far_out(WIDE, EIGHT, SIXTEEN, *small, PATCH)),
        (lanes, ((4, 2, 64, C), BF16), WIDE, EIGHT, SIXTEEN, *small, PATCH), limit=20, sems=25, micros=12,
    )
    mine1, post, count = lax.optimization_barrier((mine1, post, count))
    count = count + swap_cores(count)
    rest = (second, near1, swap_cores(near1), mine1, swap_cores(mine1))
    half, sent_half = ((4, QUARTER, C), F32), ((4, SENT, C), BF16)
    keep, other = run_kernel(
        "main", main_body, (image_sizes, count),
        (r0, u0, *received(rest), *far(pre, post, entries, head, pix, code_row, stem, slope0, w0, av, xt, patch)),
        (half, sent_half),
        (
            TWENTY, SIXTEEN, ((C, E), BF16), ((C, E), BF16), THIN, ((C, 128), BF16), planes, ((1, CELLS), jnp.int32),
            ((C, 128), BF16), WIDE, SIXTEEN, EIGHT, lanes, PATCH,
            WIDE, WIDE_LOW, WIDE, WIDE_LOW, THIN, THIN_LOW, WIDE, THREE, WIDE, WIDE_LOW, WIDE, THREE,
            ((4, CELLS, C), F32), ((4, CELLS, C), BF16), ((128, 4 * CELLS), F32), lanes,
            EIGHT, THREE, THIN, ((64, C), F32), half, half,
        ),
        limit=53, sems=28, micros=40,
    )

    quarter, sent = ((QUARTER, C), F32), ((SENT, C), BF16)
    parts = run_kernel("add_cores", add_cores_body, (), (keep, swap_cores(other)), (quarter, *(sent,) * 3))
    found = three_others(along_first, *parts[1:])
    (grad,) = run_kernel("add_first", add_first_body, (), (parts[0], *found), (sent,))
    found = three_others(along_second, grad)
    (grad,) = run_kernel("add_second", add_second_body, (), (grad, *found), (sent,))
    found = three_others(along_first, grad, back=True)

    own_half, square = run_kernel("join", join_body, (), (grad, *found), (sent_half, ((8, 128), F32)))
    other_half = swap_cores(own_half)
    found = three_others(along_tensor, square)
    square = (square + found[1]) + (found[0] + found[2])
    square = square + swap_cores(square)

    def viewed(stem, stride, block, mixer, pre, post, codes, head):
        return (
            stem.transpose(0, 2, 1, 3), stride.reshape(2, 1024, C), block.reshape(2, 576, C), mixer,
            pre, post, codes.T, head.transpose(0, 3, 1, 2),
        )

    sets = [
        viewed(
            stem_kernel, stride_kernels, block_kernels, block_mixers, pre_project, post_project, codebook, head_kernel
        ),
        viewed(*moments[:8]),
        viewed(*moments[8:]),
    ]
    given = [sets[i][weight] for weight in range(8) for i in range(3)]
    shapes = [(x.shape, x.dtype) for x in given]
    *news, loss_terms, norm = run_kernel(
        "adam", adam_body, (), (own_half, other_half, square, count, *given),
        (*far_out(*shapes), 4, 1), (*shapes, ((2, 64, C), F32)), limit=24, sems=66, micros=7,
    )

    def restored(stem, stride, block, mixer, pre, post, codes, head):
        return (
            stem.transpose(0, 2, 1, 3), stride.reshape(2, 4, 4, 64, C), block.reshape(2, 3, 3, 64, C), mixer,
            pre, post, codes.T, head.transpose(0, 2, 3, 1),
        )

    return (
        loss_terms.reshape(4),
        norm.reshape(()),
        *restored(*news[0::3]),
        *restored(*news[1::3]),
        *restored(*news[2::3]),
    )


def solution(mesh):
    in_specs = (
        P("dp", None, None, None),
        P("dp", None),
        P("dp", None, None),
        P(None, None, None, "tensor"),
        P(None, None, None, "tensor", None),
        P(None, None, None, "tensor", None),
        P(None, "tensor", None),
        P("tensor", None),
        P(None, "tensor"),
        P(),
        P(None, None, "tensor", None),
        P(None, None, None, "tensor"),
        P(None, None, None, "tensor", None),
        P(None, None, None, "tensor", None),
        P(None, "tensor", None),
        P("tensor", None),
        P(None, "tensor"),
        P(),
        P(None, None, "tensor", None),
        P(None, None, None, "tensor"),
        P(None, None, None, "tensor", None),
        P(None, None, None, "tensor", None),
        P(None, "tensor", None),
        P("tensor", None),
        P(None, "tensor"),
        P(),
        P(None, None, "tensor", None),
    )
    out_specs = (
        P(),
        P(),
        P(None, None, None, "tensor"),
        P(None, None, None, "tensor", None),
        P(None, None, None, "tensor", None),
        P(None, "tensor", None),
        P("tensor", None),
        P(None, "tensor"),
        P(),
        P(None, None, "tensor", None),
        P(None, None, None, "tensor"),
        P(None, None, None, "tensor", None),
        P(None, None, None, "tensor", None),
        P(None, "tensor", None),
        P("tensor", None),
        P(None, "tensor"),
        P(),
        P(None, None, "tensor", None),
        P(None, None, None, "tensor"),
        P(None, None, None, "tensor", None),
        P(None, None, None, "tensor", None),
        P(None, "tensor", None),
        P("tensor", None),
        P(None, "tensor"),
        P(),
        P(None, None, "tensor", None),
    )
    return jax.shard_map(
        on_device, mesh=mesh, in_specs=in_specs, out_specs=out_specs, check_vma=False
    )
```

```python
import math

import jax
import jax.numpy as jnp
from jax import lax
from jax.experimental import pallas as pl
from jax.experimental.pallas import tpu as pltpu
from jax.sharding import PartitionSpec as P

C = 256
E = 64
STEP = 10
SIDE = 32
CELLS = SIDE * SIDE
PADDED = CELLS + 2 * SIDE

beta_commit = 0.25
clip_norm = 0.002
beta_one = 0.9
beta_two = 0.999
adam_eps = 1e-08
decay_rate = 0.01
half_bin = 1.0 / 255.0
root_half = 0.7071067811865476
gelu_root = 0.7978845608028654
gelu_cube = 0.044715

F32 = jnp.float32
BF16 = jnp.bfloat16

UP_SHIFT = (-1, 0, 0, 1)
DOWN_PARITY = (1, 0, 1, 0)
DOWN_SHIFT = (-1, 0, 0, 1)


def here():
    index = lax.axis_index("dp")
    core = index % 2
    return lax.axis_index("tensor"), core, jnp.where(core == 0, index // 8, (index // 2) % 4)


def nn(left, right):
    return lax.dot_general(left, right, (((1,), (0,)), ((), ())), preferred_element_type=F32)


def nt(left, right):
    return lax.dot_general(left, right, (((1,), (1,)), ((), ())), preferred_element_type=F32)


def gelu(x):
    return x * (0.5 * (1.0 + jnp.tanh(gelu_root * (x + gelu_cube * (x * x * x)))))


def gelu_both(x):
    square = x * x
    t = jnp.tanh(x * (gelu_root + gelu_root * gelu_cube * square))
    share = 0.5 + 0.5 * t
    bend = 0.5 * gelu_root + 1.5 * gelu_root * gelu_cube * square
    return x * share, share + x * (1.0 - t * t) * bend


def columns(shape):
    return lax.broadcasted_iota(jnp.int32, shape, 0) % SIDE


def left_of(x):
    return jnp.where(columns(x.shape) == 0, 0.0, pltpu.roll(x, 1, 0))


def right_of(x):
    return jnp.where(columns(x.shape) == SIDE - 1, 0.0, pltpu.roll(x, x.shape[0] - 1, 0))


def clear_edges(ref, index):
    edge = jnp.zeros((SIDE, C), BF16)
    ref[index, 0:SIDE, :] = edge
    ref[index, PADDED - SIDE : PADDED, :] = edge


def store_three(ref, x):
    for index in range(3):
        clear_edges(ref, index)
    ref[0, SIDE : SIDE + CELLS, :] = left_of(x).astype(BF16)
    ref[1, SIDE : SIDE + CELLS, :] = x.astype(BF16)
    ref[2, SIDE : SIDE + CELLS, :] = right_of(x).astype(BF16)


def store_two(ref, phase, x):
    clear_edges(ref, 2 * phase)
    clear_edges(ref, 2 * phase + 1)
    moved = right_of(x) if phase % 2 == 0 else left_of(x)
    ref[2 * phase, SIDE : SIDE + CELLS, :] = x.astype(BF16)
    ref[2 * phase + 1, SIDE : SIDE + CELLS, :] = moved.astype(BF16)


def window(ref, index, shift):
    return ref[index, (shift + 1) * SIDE : (shift + 1) * SIDE + CELLS, :]


def three(ref, row_shift, col_shift):
    return window(ref, col_shift + 1, row_shift)


def two(ref, phase, row_shift, col_shift):
    return window(ref, 2 * phase + (0 if col_shift == 0 else 1), row_shift)


def own_lanes(x, tensor):
    half = jnp.where(tensor >= 2, x[:, 128:256], x[:, 0:128])
    return jnp.where(tensor % 2 == 1, pltpu.roll(half, 64, 1), half)[:, 0:64]


def lane_grid(shape):
    lane = lax.broadcasted_iota(jnp.int32, shape, 1)
    return lane // SIDE, lane % SIDE


def moved_plane(x, row_shift, col_shift):
    if row_shift == 0 and col_shift == 0:
        return x
    y = pltpu.roll(x, (-(SIDE * row_shift + col_shift)) % CELLS, 1)
    rows, cols = lane_grid(x.shape)
    keep = None
    for index, shift in ((rows, row_shift), (cols, col_shift)):
        if shift != 0:
            ok = (index < SIDE - 1) if shift == 1 else (index > 0)
            keep = ok if keep is None else (keep & ok)
    return jnp.where(keep, y, 0.0)


def same_forward(source, weight_ref, first):
    total = None
    for row in range(3):
        for col in range(3):
            term = nt(three(source, row - 1, col - 1), weight_ref[first + 3 * row + col])
            total = term if total is None else total + term
    return total


def same_backward(source, weight_ref, first):
    total = None
    for row in range(3):
        for col in range(3):
            term = nn(three(source, 1 - row, 1 - col), weight_ref[first + 3 * row + col])
            total = term if total is None else total + term
    return total


def down_forward(source, weight_ref):
    total = None
    for row in range(4):
        for col in range(4):
            phase = 2 * DOWN_PARITY[row] + DOWN_PARITY[col]
            term = nt(two(source, phase, DOWN_SHIFT[row], DOWN_SHIFT[col]), weight_ref[4 * row + col])
            total = term if total is None else total + term
    return total


def split_three(x):
    first = x.astype(BF16)
    rest = x - first.astype(F32)
    second = rest.astype(BF16)
    return first, second, (rest - second.astype(F32)).astype(BF16)


def one_hot_codes(codes_ref):
    return (
        (lax.broadcasted_iota(jnp.int32, (512, CELLS), 0) == codes_ref[...]).astype(F32).astype(BF16)
    )


def patch_body(
    sizes, image_in, codes_in, book_in, pix_out, x_out, entries_out,
    image_ref, codes_ref, book_ref, pix_ref, x_ref, entries_ref, sems,
):
    high, wide = sizes[0, 0] // 4, sizes[0, 1] // 4
    copies = copy_all(
        sems,
        [
            (image_in, image_ref), (codes_in, codes_ref), (book_in, book_ref),
            (pix_ref, pix_out), (entries_ref, entries_out), (x_ref, x_out),
        ],
    )
    start_all(copies[0:3])
    wait_all(copies[0:3])
    book = jnp.concatenate(split_three(book_ref[...]), 0)
    found = nn(book, one_hot_codes(codes_ref))
    entries_ref[...] = ((found[0:64] + found[64:128]) + found[128:192]).T
    copies[4].start()
    image = image_ref[...].astype(F32).astype(BF16)
    lane = lax.broadcasted_iota(jnp.int32, (128, CELLS), 1)
    source = lax.broadcasted_iota(jnp.int32, (128, CELLS), 0)
    row = lax.broadcasted_iota(jnp.int32, (384, CELLS), 0)
    own_row = (row // 4) % SIDE == lax.broadcasted_iota(jnp.int32, (384, CELLS), 1) // SIDE
    slot = lax.broadcasted_iota(jnp.int32, (32, 384), 0)
    line = lax.broadcasted_iota(jnp.int32, (32, 384), 1)
    pick = ((line % 4 == slot // 8) & (line // 128 == slot % 8)).astype(F32).astype(BF16)
    planes = {}
    for col in range(4):
        spread = (source == 4 * (lane % SIDE) + col).astype(F32).astype(BF16)
        lined = jnp.where(own_row, nn(image, spread), 0.0).astype(BF16)
        found = nn(pick, lined)
        for r in range(4):
            planes[r, col] = found[8 * r : 8 * r + 8]
    for r in range(4):
        for half in range(2):
            pix_ref[2 * r + half] = planes[r, 2 * half] + pltpu.roll(planes[r, 2 * half + 1], 4, 0)
    copies[3].start()
    rows, cols = lane_grid((8, CELLS))
    channel = lax.broadcasted_iota(jnp.int32, (8, CELLS), 0)
    inside = (rows < high) & (cols < wide) & (channel < 3)
    planes = {key: jnp.where(inside, value / 127.5 - 1.0, 0.0) for key, value in planes.items()}
    moved = {}
    for r in range(-1, 5):
        for c in range(-1, 5):
            moved[r, c] = moved_plane(planes[r % 4, c % 4], r // 4, c // 4)
    for p in range(2):
        for q in range(2):
            for kh in range(4):
                for kw in range(0, 4, 2):
                    r, c = 2 * p + kh - 1, 2 * q + kw - 1
                    tap = 4 * kh + kw
                    x_ref[8 * tap : 8 * tap + 16, (2 * p + q) * CELLS : (2 * p + q + 1) * CELLS] = (
                        jnp.concatenate([moved[r, c], moved[r, c + 1]], 0).astype(BF16)
                    )
    copies[5].start()
    wait_all(copies[3:])


def copy_all(sems, pairs):
    return [pltpu.make_async_copy(source, target, sems.at[i]) for i, (source, target) in enumerate(pairs)]


def start_all(copies):
    for copy in copies:
        copy.start()


def wait_all(copies):
    for copy in copies:
        copy.wait()


def count_body(sizes, count_ref):
    count_ref[...] = jnp.full((8, 128), (sizes[0, 0] // 4) * (sizes[0, 1] // 4), jnp.int32).astype(F32)


def pack_first_body(
    stride_in, stem_in, head_in, pre_in, post_in, out_ref,
    stride_ref, stem_ref, head_ref, pre_ref, post_ref, sems,
):
    copies = copy_all(
        sems,
        [
            (stem_in, stem_ref), (head_in, head_ref), (pre_in, pre_ref), (post_in, post_ref),
            (stride_in.at[0, 0:8], stride_ref.at[0:8]), (stride_in.at[0, 8:16], stride_ref.at[8:16]),
        ],
    )
    start_all(copies[0:6])
    wait_all(copies[0:4])

    def ordered(ref, per):
        rows = jnp.concatenate([ref[kh, c] for kh in range(4) for c in range(per)], 0)
        count = 16 * per
        slot = lax.broadcasted_iota(jnp.int32, (128, count), 0)
        line = lax.broadcasted_iota(jnp.int32, (128, count), 1)
        channel = slot % 8
        if per == 6:
            channel = jnp.where(channel % 4 == 3, per, channel - channel // 4)
        wanted = (slot // 32) * 4 * per + channel * 4 + (slot // 8) % 4
        pick = ((line == wanted) & (channel < per)).astype(F32).astype(BF16)
        return nn(pick, rows.astype(BF16)).T

    out_ref[8] = jnp.concatenate([ordered(stem_ref, 3), ordered(head_ref, 6)], 1).astype(BF16)
    thin = jnp.concatenate([pre_ref[...], post_ref[...].T], 1)
    out_ref[9] = jnp.concatenate([thin, thin], 1).astype(BF16)
    for k in range(2):
        copies[4 + k].wait()
        out_ref[10 * k : 10 * k + 8] = stride_ref[8 * k : 8 * k + 8].astype(BF16)


def pack_rest_body(stride_in, block_in, mix_in, out, stride_ref, block_ref, mix_ref, out_ref, sems):
    copies = copy_all(
        sems,
        [
            (block_in, block_ref), (mix_in, mix_ref), (stride_in.at[1], stride_ref), (out_ref, out),
        ],
    )
    start_all(copies[0:3])
    wait_all(copies[0:3])
    for b in range(2):
        out_ref[18 * b : 18 * b + 9] = block_ref[b].astype(BF16)
        out_ref[18 * b + 9] = mix_ref[b].astype(BF16)
        out_ref[18 * b + 10 : 18 * b + 18] = stride_ref[8 * b : 8 * b + 8].astype(BF16)
    start_all(copies[3:])
    wait_all(copies[3:])


def gather_pairs(ref, parts, tensor, core, rotated, low, high, half_low):
    def rows(step):
        if rotated and isinstance(step, int):
            return pl.ds(64 * step, 64)
        return pl.ds(pl.multiple_of((64 * step if rotated else ((tensor + step) % 4) * 64), 64), 64)

    count = ref.shape[0] // 2
    pairs = []
    for part, step in zip(parts[0:3], (0, 1 + 2 * core, 3 - 2 * core), strict=True):
        for k, start in enumerate((low, high)):
            pairs.append((part.at[start : start + count], ref.at[count * k : count * k + count, rows(step), :]))
    for part, half in ((parts[3], core), (parts[4], 1 - core)):
        source = part.at[pl.ds(half_low(half), count)]
        pairs.append((source, ref.at[pl.ds(count * half, count), rows(2), :]))
    return pairs


def block_forward(resid, u_ref, w_ref, first, v_ref, q_ref):
    value, v_ref[...] = gelu_both(same_forward(u_ref, w_ref, first))
    act = value.astype(BF16)
    q_ref[...] = act
    return resid + nn(act, w_ref[first + 9])


def front_body(
    x_in, own, near, far, mine, other,
    r_ref, u_ref, slope_out, a_out, w_out, stem_out, head_out, pre_out, post_out, patch_out,
    x_ref, small_ref, slope_ref, a_ref, w_ref, stem_ref, head_ref, pre_ref, post_ref, patch_ref, sems,
):
    tensor, core, _ = here()
    small = [part.at[8:10] for part in (own, near, far)] + [mine.at[pl.ds(8 * (1 - core), 2)]]
    pairs = [(x_in, x_ref)] + [(part, small_ref.at[k]) for k, part in enumerate(small)]
    pairs += gather_pairs(w_ref, (own, near, far, mine, other), tensor, core, False, 0, 10, lambda half: 2 * half)
    copies = copy_all(sems, pairs)
    start_all(copies)
    outs = [(stem_ref, stem_out), (head_ref, head_out), (pre_ref, pre_out), (post_ref, post_out), (w_ref, w_out)]
    outs += [(a_ref.at[2 * p : 2 * p + 2], a_out.at[2 * p : 2 * p + 2]) for p in range(4)]
    outs += [(patch_ref, patch_out), (slope_ref, slope_out)]
    writes = [
        pltpu.make_async_copy(source, target, sems.at[len(copies) + i]) for i, (source, target) in enumerate(outs)
    ]
    wait_all(copies[0:5])
    for k, step in enumerate((0, 1 + 2 * core, 3 - 2 * core, 2)):
        rows = pl.ds(pl.multiple_of(((tensor + step) % 4) * 64, 64), 64)
        turned = 64 * step if isinstance(step, int) else pl.multiple_of(64 * step, 64)
        stem_ref[rows, :] = small_ref[k, 0, :, 0:128]
        head_ref[pl.ds(turned, 64), :] = small_ref[k, 0, :, 128:256]
        pre_ref[rows, :] = small_ref[k, 1, :, 0:64]
        post_ref[rows, :] = small_ref[k, 1, :, 64:128]
    start_all(writes[0:4])
    for phase in range(4):
        patch = x_ref[:, phase * CELLS : (phase + 1) * CELLS].T
        patch_ref[phase * CELLS : (phase + 1) * CELLS, :] = patch
        store_two(a_ref, phase, gelu(nt(patch, stem_ref[...])))
        writes[5 + phase].start()
    writes[9].start()
    wait_all(copies[5:])
    writes[4].start()
    resid = down_forward(a_ref, w_ref)
    r_ref[...] = resid
    value, slope_ref[...] = gelu_both(resid)
    writes[10].start()
    store_three(u_ref, value)
    wait_all(writes)


def valid_cells(sizes):
    cell = lax.broadcasted_iota(jnp.int32, (CELLS, E), 0)
    return (cell // SIDE < sizes[0, 0] // 4) & (cell % SIDE < sizes[0, 1] // 4)


def poly(x, coefs):
    total = jnp.full_like(x, coefs[0])
    for c in coefs[1:]:
        total = total * x + c
    return total


ERFC_LOW = (
    2.326819970068386e-2, -1.387039388740657e-1, 3.687424674597105e-1, -5.824733027278666e-1,
    6.210004621745983e-1, -4.944515323274145e-1, 3.404879937665872e-1, -2.741127028184656e-1,
    5.638259427386472e-1,
)
ERFC_HIGH = (
    -1.047766399936249e1, 1.297719955372516e1, -7.495518717768503e0, 2.921019019210786e0,
    -1.015265279202700e0, 4.218463358204948e-1, -2.820767439740514e-1, 5.641895067754075e-1,
)
ERF_NEAR = (
    7.853861353153693e-5, -8.010193625184903e-4, 5.188327685732524e-3, -2.685381193529856e-2,
    1.128358514861418e-1, -3.761262582423300e-1, 1.128379165726710e0,
)


def erfc(x):
    size = jnp.abs(x)
    square = x * x
    far_exp = jnp.exp(-square)
    recip = 1.0 / jnp.maximum(size, 0.5)
    y = recip * recip
    far = far_exp * recip * jnp.where(size < 2.0, poly(y, ERFC_LOW), poly(y, ERFC_HIGH))
    far = jnp.where(x < 0, 2.0 - far, far)
    near = 1.0 - x * poly(square, ERF_NEAR)
    return jnp.where(size > 1.0, far, near), far_exp


def likelihood(center_out, scale_out, pix, keep, scale):
    target = pix / 127.5 - 1.0
    center = jnp.tanh(center_out)
    decay = jnp.exp(-jnp.abs(scale_out))
    sigma = 0.25 + (jnp.maximum(scale_out, 0.0) + jnp.log(1.0 + decay))
    gate = jnp.where(scale_out >= 0, 1.0, decay) / (1.0 + decay)
    low_end, high_end = pix == 0.0, pix == 255.0
    lower = jnp.where(low_end, -40.0, (target - half_bin - center) / sigma)
    upper = jnp.where(high_end, 40.0, (target + half_bin - center) / sigma)
    right = lower + upper > 0
    tail_a, exp_a = erfc(jnp.where(right, lower, -upper) * root_half)
    tail_b, exp_b = erfc(jnp.where(right, upper, -lower) * root_half)
    mass = 0.5 * (tail_a - tail_b)
    bits = jnp.where(keep, jnp.log(mass), 0.0)
    density = 1.0 / math.sqrt(2.0 * math.pi)
    slope = jnp.where(keep, scale * density / mass, 0.0)
    low_slope = jnp.where(low_end, 0.0, -slope * jnp.where(right, exp_a, exp_b))
    high_slope = jnp.where(high_end, 0.0, slope * jnp.where(right, exp_b, exp_a))
    center_grad = -(low_slope + high_slope) / sigma
    sigma_grad = -(low_slope * lower + high_slope * upper) / sigma
    return bits, center_grad * (1.0 - center * center), sigma_grad * gate


def head_links():
    for p in range(2):
        for q in range(2):
            for kh in range(4):
                for kw in range(4):
                    up, left = p + UP_SHIFT[kh], q + UP_SHIFT[kw]
                    out = (2 * p + kh % 2, 2 * q + kw % 2)
                    yield out, 4 * kh + kw, 2 * (up % 2) + left % 2, up // 2, left // 2


QUARTER = 448
KINDS = {"stride": (0, 256), "block": (256, 144), "mixer": (400, 16), "codes": (416, 16), "small": (432, 16)}


def store_rows(g_ref, kind, start, value):
    base, size = KINDS[kind]
    done = 0
    while done < value.shape[0]:
        place = start + done
        count = min(size - place % size, value.shape[0] - done)
        first = base + place % size
        g_ref[place // size, first : first + count, :] = value[done : done + count]
        done += count


def with_scalar(x, scalar):
    row = lax.broadcasted_iota(jnp.int32, (64, 64), 0)
    lane = lax.broadcasted_iota(jnp.int32, (64, 64), 1)
    return jnp.concatenate([x, jnp.where((row == 0) & (lane == 0), scalar, 0.0)], 1)


def block_backward(grad_out, resid_ref, u_ref, v_ref, q_ref, w_ref, first, dv_ref, g_ref):
    low = grad_out.astype(BF16)
    own_q = q_ref[:, 0:128].astype(F32).T[0:64].astype(BF16)
    store_rows(g_ref, "mixer", 0, nn(own_q, low))
    mid = nt(low, w_ref[first + 9])
    inner = v_ref[...] * mid
    store_three(dv_ref, inner)
    own = inner[:, 0:128].T[0:64].astype(BF16)
    for row in range(3):
        for col in range(3):
            tap = 3 * row + col
            store_rows(g_ref, "block", 64 * tap, nn(own, three(u_ref, row - 1, col - 1)))
    return grad_out + resid_ref[...] * same_backward(dv_ref, w_ref, first)


def forward_blocks(
    sizes, r0_ref, u0_ref, w_ref, pre_ref, post_ref, entries_ref,
    v0_ref, q0_ref, r1_ref, act_ref, diff_ref, zq_ref, r2_ref, u2_ref, v1_ref, q1_ref, r3_ref, u3_ref, waits,
):
    resid = block_forward(r0_ref[...], u0_ref, w_ref, 0, v0_ref, q0_ref)
    value, r1_ref[...] = gelu_both(resid)
    act = value.astype(BF16)
    act_ref[...] = act
    wait_all(waits)
    latent = nn(act, pre_ref[...])
    entries = entries_ref[...]
    diff = latent - entries
    diff_ref[...] = diff
    code = (latent + (entries - latent)).astype(BF16)
    zq_ref[...] = code
    resid = nt(code, post_ref[...])
    value, r2_ref[...] = gelu_both(resid)
    store_three(u2_ref, value)
    resid = block_forward(resid, u2_ref, w_ref, 10, v1_ref, q1_ref)
    value, r3_ref[...] = gelu_both(resid)
    store_three(u3_ref, value)
    return (1.0 + beta_commit) * jnp.sum(jnp.where(valid_cells(sizes), diff * diff, 0.0))


def main_body(
    sizes, total_ref, r0_ref, u0_ref, own, near, far, mine, other,
    pre_in, post_in, entries_in, head_in, pix_in, codes_in, stem_in, r0s_in, w0_in, a_in, x_in, patch_in,
    keep_ref, send_ref,
    wb_ref, w_ref, pre_ref, post_ref, entries_ref, head_ref, pix_ref, codes_ref, stem_ref, r0s_ref, w0_ref, a_ref, x_ref, patch_ref,
    v0_ref, q0_ref, r1_ref, act_ref, diff_ref, zq_ref, r2_ref, u2_ref, v1_ref, q1_ref, r3_ref, u3_ref,
    h4_ref, a4_ref, prod_ref, q_ref, dh_ref, dv_ref, back_ref, late_ref, gd_ref, g_ref, sems,
):
    tensor, core, _ = here()
    parts = (own, near, far, mine, other)
    pairs = gather_pairs(wb_ref, parts, tensor, core, True, 0, 18, lambda half: 0)
    pairs += [(pre_in, pre_ref), (post_in, post_ref), (entries_in, entries_ref)]
    pairs += gather_pairs(w_ref, parts, tensor, core, True, 10, 28, lambda half: 10)
    pairs += [(head_in, head_ref), (pix_in, pix_ref), (codes_in, codes_ref), (stem_in, stem_ref)]
    pairs += [(r0s_in, r0s_ref), (w0_in, w0_ref), (a_in, a_ref), (x_in, x_ref), (patch_in, patch_ref)]
    copies = copy_all(sems, pairs)
    start_all(copies[0:8])
    wait_all(copies[0:8])
    start_all(copies[8:])
    vq = forward_blocks(
        sizes, r0_ref, u0_ref, wb_ref, pre_ref, post_ref, entries_ref,
        v0_ref, q0_ref, r1_ref, act_ref, diff_ref, zq_ref, r2_ref, u2_ref, v1_ref, q1_ref, r3_ref, u3_ref, copies[8:11],
    )
    wait_all(copies[11:19])
    decode_back(
        sizes, total_ref, pix_ref, r3_ref, u3_ref, head_ref, r2_ref, u2_ref, v1_ref, q1_ref, wb_ref,
        gd_ref, w_ref, h4_ref, a4_ref, prod_ref, q_ref, dh_ref, dv_ref, zq_ref, post_ref, back_ref, copies[19:21],
    )
    wait_all(copies[21:])
    encode_back(
        sizes, total_ref, vq, back_ref, diff_ref, codes_ref, r1_ref, act_ref, pre_ref, stem_ref, x_ref, patch_ref, a_ref,
        r0s_ref, u0_ref, v0_ref, q0_ref, wb_ref, w0_ref, gd_ref, keep_ref, send_ref, dv_ref, dh_ref, g_ref, late_ref,
    )


def decode_back(
    sizes, total_ref, pix_ref, r3_ref, u3_ref, head_ref, r2_ref, u2_ref, v1_ref, q1_ref, w1_ref,
    g_ref, w_ref, h4_ref, a4_ref, prod_ref, q_ref, dh_ref, dv_ref, zq_ref, post_ref, back_ref, early,
):
    tensor, _, _ = here()
    high, wide = sizes[0, 0] // 4, sizes[0, 1] // 4
    wait_all(early)
    head = head_ref[...].astype(F32).T.astype(BF16)
    for p in range(2):
        for q in range(2):
            phase = 2 * p + q
            total = None
            for kh in (p, p + 2):
                for kw in (q, q + 2):
                    term = nt(three(u3_ref, UP_SHIFT[kh], UP_SHIFT[kw]), w_ref[4 * kh + kw])
                    total = term if total is None else total + term
            value, h4_ref[phase] = gelu_both(total)
            act = value.astype(BF16)
            a4_ref[phase] = act
            prod_ref[:, phase * CELLS : (phase + 1) * CELLS] = nt(head, act)
    outs = {}
    for out, tap, phase, up, left in head_links():
        term = moved_plane(
            prod_ref[8 * tap : 8 * tap + 8, phase * CELLS : (phase + 1) * CELLS], up, left
        )
        outs[out] = term if out not in outs else outs[out] + term
    sub = lax.broadcasted_iota(jnp.int32, (8, CELLS), 0)
    rows, cols = lane_grid((8, CELLS))
    keep = (rows < high) & (cols < wide) & (sub % 4 != 3)
    first = sub < 4
    scale = -1.0 / (math.log(2.0) * 48.0 * total_ref[0, 0])
    grads = {}
    bits = None
    for pair in range(8):
        row, col = pair // 2, 2 * (pair % 2)
        one, other = outs[row, col], outs[row, col + 1]
        centers = jnp.where(first, one, pltpu.roll(other, 4, 0))
        scales = jnp.where(first, pltpu.roll(one, 4, 0), other)
        part, center_grad, scale_grad = likelihood(centers, scales, pix_ref[pair], keep, scale)
        bits = part if bits is None else bits + part
        grads[row, col] = jnp.where(first, center_grad, pltpu.roll(scale_grad, 4, 0))
        grads[row, col + 1] = jnp.where(first, pltpu.roll(center_grad, 4, 0), scale_grad)
    bits = -jnp.sum(bits) / math.log(2.0)
    found = {}
    for out, tap, phase, up, left in head_links():
        found[tap, phase] = moved_plane(grads[out], -up, -left)
    for phase in range(4):
        for tap in range(0, 16, 2):
            q_ref[8 * tap : 8 * tap + 16, phase * CELLS : (phase + 1) * CELLS] = jnp.concatenate(
                [found[tap, phase], found[tap + 1, phase]], 0
            ).astype(BF16)
    head_grad = None
    for phase in range(4):
        spread = q_ref[:, phase * CELLS : (phase + 1) * CELLS]
        term = nn(spread, a4_ref[phase, :, 0:64])
        head_grad = term if head_grad is None else head_grad + term
        slope = h4_ref[phase] * nn(spread.T, head)
        store_two(dh_ref, phase, slope)
        own = slope[:, 0:128].T[0:64].astype(BF16)
        for kh in (phase // 2, phase // 2 + 2):
            for kw in (phase % 2, phase % 2 + 2):
                tap = 4 * kh + kw
                store_rows(g_ref, "stride", 64 * tap, nn(own, three(u3_ref, UP_SHIFT[kh], UP_SHIFT[kw])))
    total = None
    for kh in range(4):
        for kw in range(4):
            phase = 2 * (kh % 2) + kw % 2
            term = nn(two(dh_ref, phase, -UP_SHIFT[kh], -UP_SHIFT[kw]), w_ref[4 * kh + kw])
            total = term if total is None else total + term
    grad = r3_ref[...] * total
    grad = block_backward(grad, r2_ref, u2_ref, v1_ref, q1_ref, w1_ref, 10, dv_ref, g_ref)
    low = grad.astype(BF16)
    post_grad = nn(zq_ref[...].astype(F32).T.astype(BF16), own_lanes(grad, tensor).astype(BF16))
    small = jnp.concatenate([post_grad, head_grad[0:64], head_grad[64:128]], 1)
    store_rows(g_ref, "small", 0, with_scalar(small, bits))
    back_ref[...] = nn(low, post_ref[...])


def encode_back(
    sizes, total_ref, vq, back_ref, diff_ref, codes_ref, r1_ref, act_ref, pre_ref, stem_ref, x_ref, patch_ref, a_ref,
    r0_ref, u_ref, v_ref, q_ref, wb_ref, w_ref, gd_ref, keep_ref, send_ref, dv_ref, dr_ref, g_ref, late_ref,
):
    tensor, core, _ = here()
    scaled = jnp.where(valid_cells(sizes), diff_ref[...] / (64.0 * total_ref[0, 0]), 0.0)
    dz = (back_ref[...] + 2.0 * beta_commit * scaled).astype(BF16)
    hot = one_hot_codes(codes_ref)
    found = nt(jnp.concatenate(split_three((-2.0 * scaled).T), 0), hot)
    codes = (found[0:64] + found[64:128]) + found[128:192]
    store_rows(g_ref, "codes", 0, codes[:, 0:256])
    late_ref[...] = codes[:, 256:512]
    act = own_lanes(act_ref[...].astype(F32), tensor)
    pre_grad = nn(act.T.astype(BF16), dz)
    grad = r1_ref[...] * nt(dz, pre_ref[...])
    grad = block_backward(grad, r0_ref, u_ref, v_ref, q_ref, wb_ref, 0, dv_ref, g_ref)
    store_three(dr_ref, grad)
    own = own_lanes(grad, tensor).T.astype(BF16)
    for kh in range(4):
        for kw in range(4):
            tap = 4 * kh + kw
            phase = 2 * DOWN_PARITY[kh] + DOWN_PARITY[kw]
            term = nn(own, two(a_ref, phase, DOWN_SHIFT[kh], DOWN_SHIFT[kw]))
            store_rows(g_ref, "stride", 64 * tap, term)
    line = lax.broadcasted_iota(jnp.int32, (C, C), 0)
    lane = lax.broadcasted_iota(jnp.int32, (C, C), 1)
    shifts = [(up, left) for up in (-1, 0, 1) for left in (-1, 0, 1)]
    before = total = None
    stem = stem_ref[pl.ds(pl.multiple_of(64 * tensor, 64), 64), :].astype(F32).T.astype(BF16)
    for phase in range(4):
        place = (lane[0:64] == line[0:64] + 64 * phase).astype(F32).astype(BF16)
        wide = nn(stem, place).astype(BF16)
        term = nn(patch_ref[phase * CELLS : (phase + 1) * CELLS, :], wide)
        before = term if before is None else before + term
    picks = [
        ((lane == line - 64 * tensor + 64 * phase) & (lane // 64 == phase)).astype(F32).astype(BF16) for phase in range(4)
    ]
    for up, left in shifts:
        weight = None
        for kh in range(4):
            for kw in range(4):
                if (-DOWN_SHIFT[kh], -DOWN_SHIFT[kw]) == (up, left):
                    term = nn(w_ref[4 * kh + kw], picks[2 * DOWN_PARITY[kh] + DOWN_PARITY[kw]])
                    weight = term if weight is None else weight + term
        term = nn(three(dr_ref, up, left), weight.astype(BF16))
        total = term if total is None else total + term
    slope = (gelu_both(before)[1] * total).astype(BF16)
    stem_grad = None
    for phase in range(4):
        term = nn(x_ref[:, phase * CELLS : (phase + 1) * CELLS], slope)[:, 64 * phase : 64 * phase + 64]
        stem_grad = term if stem_grad is None else stem_grad + term
    small = jnp.concatenate([pre_grad, stem_grad[0:64], stem_grad[64:128]], 1)
    store_rows(g_ref, "small", 0, with_scalar(small, vq))
    base = KINDS["codes"][0]
    for part in range(4):
        gd_ref[part, base : base + 16, :] = late_ref[16 * part : 16 * part + 16, :]

    @pl.when(core == 0)
    def _():
        keep_ref[...] = g_ref[...]
        for part in range(4):
            put_sent(send_ref.at[part], gd_ref[part])

    @pl.when(core == 1)
    def _():
        keep_ref[...] = gd_ref[...]
        for part in range(4):
            put_sent(send_ref.at[part], g_ref[part])


SENT = QUARTER + 32
SMALL_ROWS = KINDS["small"][0]


def put_sent(out, value):
    out[0:SMALL_ROWS, :] = value[0:SMALL_ROWS].astype(BF16)
    for k, part in enumerate(split_three(value[SMALL_ROWS:QUARTER])):
        out[SMALL_ROWS + 16 * k : SMALL_ROWS + 16 * k + 16, :] = part


def small_of(ref):
    parts = [ref[SMALL_ROWS + 16 * k : SMALL_ROWS + 16 * k + 16, :].astype(F32) for k in range(3)]
    return (parts[0] + parts[1]) + parts[2]


def whole(ref):
    return jnp.concatenate([ref[0:SMALL_ROWS, :].astype(F32), small_of(ref)], 0)


def add_cores_body(keep_ref, other_ref, own_ref, *outs):
    _, _, place = here()
    own_ref[...] = keep_ref[place] + whole(other_ref.at[place])
    for k, out in enumerate(outs):
        part = (place + 1 + k) % 4
        put_sent(out, keep_ref[part] + whole(other_ref.at[part]))


def four(own, one, two_on, three_on):
    return (own + whole(two_on)) + (whole(one) + whole(three_on))


def add_first_body(own, one, three_on, two_on, out):
    put_sent(out, four(own[...], one, two_on, three_on))


def add_second_body(own, two_on, one, three_on, out):
    put_sent(out, four(whole(own), one, two_on, three_on))


def join_body(own, two_on, one, three_on, half_ref, square_ref):
    _, _, place = here()
    row = lax.broadcasted_iota(jnp.int32, (QUARTER, C), 0)
    lane = lax.broadcasted_iota(jnp.int32, (QUARTER, C), 1)
    share = jnp.where((row >= KINDS["codes"][0]) & (row < SMALL_ROWS), 0.25, 1.0)
    share = jnp.where((row >= SMALL_ROWS) & (lane >= 192), 0.0, share)
    total = jnp.zeros((QUARTER, C), F32)
    for k, part in enumerate((own, one, two_on, three_on)):
        half_ref[(place + k) % 4] = part[...]
        value = whole(part)
        total = total + value * value
    square_ref[...] = jnp.full((8, 128), jnp.sum(total * share), F32)


def adam(weight, moment, second, grad, rate):
    m_new = beta_one * moment + (1.0 - beta_one) * grad
    v_new = beta_two * second + ((1.0 - beta_two) * grad) * grad
    change = (rate / (1.0 - beta_one**STEP)) * m_new
    size = jnp.sqrt((1.0 / (1.0 - beta_two**STEP)) * v_new) + adam_eps
    return (1.0 - rate * decay_rate) * weight - change / size, m_new, v_new


RATES = (
    48.0 ** (-0.5),
    (16.0 * C) ** (-0.5),
    (9.0 * C) ** (-0.5),
    C ** (-0.5),
    C ** (-0.5),
    E ** (-0.5),
    0.6,
    (4.0 * C) ** (-0.5),
)


def adam_body(half_ref, other_ref, square_ref, total_ref, *refs):
    _, core, _ = here()
    given, outs, loss_ref, norm_ref = refs[0:24], refs[24:48], refs[48], refs[49]
    results, small_ref, sems = refs[50:74], refs[74], refs[75]
    norm = jnp.sqrt(square_ref[...])
    factor = jnp.minimum(1.0, clip_norm / (norm + 1e-06))[0:1, 0:1]
    norm_ref[0, 0] = jnp.max(norm)

    def rows_of(side, part, kind):
        if kind == "small":
            return jnp.where(core == side, small_of(half_ref.at[part]), small_of(other_ref.at[part]))
        base, size = KINDS[kind]
        mine, theirs = half_ref[part, base : base + size, :], other_ref[part, base : base + size, :]
        return jnp.where(core == side, mine.astype(F32), theirs.astype(F32))

    def update(weight, index, grad):
        values = [given[3 * weight + i][index] for i in range(3)]
        for i, value in enumerate(adam(*values, factor * grad, RATES[weight])):
            results[3 * weight + i][index] = value

    copies = []

    def finish(weight, index=None):
        for i in range(3):
            source, target = results[3 * weight + i], outs[3 * weight + i]
            if index is not None:
                source, target = source.at[index], target.at[index]
            copies.append(pltpu.make_async_copy(source, target, sems.at[len(copies)]))
            copies[-1].start()

    for side in range(2):
        for part in range(4):
            small_ref[side, 16 * part : 16 * part + 16, :] = rows_of(side, part, "small")
            update(3, (side, pl.ds(16 * part, 16), slice(None)), rows_of(side, part, "mixer"))
            update(6, (pl.ds(16 * part, 16), pl.ds(256 * side, 256)), rows_of(side, part, "codes"))
    finish(3)
    finish(6)
    for weight, side, channels in ((0, 0, 3), (7, 1, 6)):
        spread = small_ref[side, :, 64:192]
        for kh in range(4):
            block = spread[32 * (kh % 2) : 32 * (kh % 2) + 32, 64 * (kh // 2) : 64 * (kh // 2) + 64]
            for c in range(channels):
                slot = c + (c // 3 if channels == 6 else 0)
                lines = jnp.concatenate([block[8 * kw + slot : 8 * kw + slot + 1] for kw in range(4)], 0)
                update(weight, (kh, c), lines)
        finish(weight)
    for weight, side in ((4, 0), (5, 1)):
        update(weight, (slice(None), slice(None)), small_ref[side, :, 0:64])
        finish(weight)
    for weight, kind in ((1, "stride"), (2, "block")):
        size = KINDS[kind][1]
        for side in range(2):
            for part in range(4):
                index = (side, pl.ds(size * part, size), slice(None))
                update(weight, index, rows_of(side, part, kind))
                finish(weight, index)
    first = (lax.broadcasted_iota(jnp.int32, (16, 64), 0) == 0) & (lax.broadcasted_iota(jnp.int32, (16, 64), 1) == 0)
    for slot, side, share in ((0, 1, 48.0), (2, 0, 64.0)):
        loss_ref[0, slot] = jnp.sum(jnp.where(first, small_ref[side, 0:16, 192:256], 0.0))
        loss_ref[0, slot + 1] = share * total_ref[0, 0]
    wait_all(copies)


SMEM = pl.BlockSpec(memory_space=pltpu.SMEM)
VMEM = pl.BlockSpec(memory_space=pltpu.VMEM)


def run_kernel(name, body, scalars, arrays, outs, scratch=(), limit=6, sems=0, micros=1):
    anywhere = pl.BlockSpec(memory_space=pl.ANY)
    shapes, out_specs, specs, given = [], [], [SMEM] * len(scalars), list(scalars)
    for out in outs:
        if isinstance(out, int):
            shapes.append(pltpu.SMEM((1, out), F32))
            out_specs.append(SMEM)
        elif out[0] == "far":
            shapes.append(pltpu.HBM(*out[1:]))
            out_specs.append(anywhere)
        else:
            shapes.append(pltpu.VMEM(*out))
            out_specs.append(VMEM)
    for array in arrays:
        if isinstance(array, tuple):
            place, array = array
            given.append(pltpu.with_memory_space_constraint(array, pltpu.HBM) if place == "far" else array)
            specs.append(anywhere)
        else:
            given.append(pltpu.with_memory_space_constraint(array, pltpu.VMEM))
            specs.append(VMEM)
    return pl.pallas_call(
        body,
        out_shape=shapes,
        in_specs=specs,
        out_specs=out_specs,
        scratch_shapes=[pltpu.VMEM(*s) for s in scratch] + ([pltpu.SemaphoreType.DMA((sems,))] if sems else []),
        compiler_params=pltpu.CompilerParams(vmem_limit_bytes=limit * 2**20),
        cost_estimate=pl.CostEstimate(flops=int(micros * 1.1e9), bytes_accessed=0, transcendentals=0),
        name=name,
    )(*given)


THREE = ((3, PADDED, C), BF16)
EIGHT = ((8, PADDED, C), BF16)
WIDE = ((CELLS, C), F32)
WIDE_LOW = ((CELLS, C), BF16)
TWENTY = ((20, C, C), BF16)
THIN = ((CELLS, E), F32)
THIN_LOW = ((CELLS, E), BF16)
PATCH = ((4 * CELLS, 128), BF16)


def far(*arrays):
    return tuple(("far", array) for array in arrays)


def received(parts):
    return tuple(("any", part) for part in parts)


def far_out(*shapes):
    return tuple(("far", *shape) for shape in shapes)


SIXTEEN = ((16, C, C), BF16)


BOTH = ("dp", "tensor")


def send(value, target):
    pairs = []
    for x in range(4):
        for z in range(4):
            for core in range(2):
                for y in range(4):
                    to = target(x, z, core, y)
                    pairs.append(
                        (
                            ((x * 4 + z) * 2 + core) * 4 + y,
                            (((to[0] % 4) * 4 + to[1] % 4) * 2 + to[2]) * 4 + to[3] % 4,
                        )
                    )
    return lax.ppermute(value, BOTH, pairs)


def swap_cores(value):
    return send(value, lambda x, z, core, y: (x, z, 1 - core, y))


def along_first(value, k):
    return send(value, lambda x, z, core, y: (x + k, z, core, y) if core == 0 else (x, z + k, core, y))


def along_second(value, k):
    return send(value, lambda x, z, core, y: (x, z + k, core, y) if core == 0 else (x + k, z, core, y))


def three_others(along, *values, back=False):
    found = {}
    for k in (1, 3, 2):
        found[k] = along(values[k - 1] if len(values) > 1 else values[0], -k if back else k)
    return [found[k] for k in (1, 2, 3)]


def along_tensor(value, k):
    return send(value, lambda x, z, core, y: (x, z, core, y + k))


def from_one_side(local):
    return send(local, lambda x, z, core, y: (x, z, core, y - 1 if core == 0 else y + 1))


def after(value, *others):
    return lax.optimization_barrier((value, *others))[0]


def on_device(
    pixels,
    image_sizes,
    code_indices,
    stem_kernel,
    stride_kernels,
    block_kernels,
    block_mixers,
    pre_project,
    post_project,
    codebook,
    head_kernel,
    *moments,
):
    def add_along(value, step, along_x):
        return value + send(value, lambda x, z, core, y: (x ^ step, z, core, y) if along_x else (x, z ^ step, core, y))

    image_sizes = pltpu.with_memory_space_constraint(image_sizes, pltpu.HBM)
    stem_rows = stem_kernel.transpose(0, 2, 1, 3)
    head_rows = head_kernel.transpose(0, 3, 1, 2)
    stride_rows = stride_kernels.reshape(2, 16, 64, C)
    block_rows = block_kernels.reshape(2, 9, 64, C)
    small = (((E, E), F32), ((E, E), F32))
    taps = lambda count: ((count, 64, C), BF16)
    core = lax.axis_index("dp") % 2

    def half_of(near, step, taps):
        return lax.dynamic_slice_in_dim(near, core * step, taps, 0)

    (first,) = run_kernel(
        "pack_first", pack_first_body, (), far(stride_rows, stem_rows, head_rows, pre_project, post_project),
        (taps(18),),
        (((16, 64, C), F32), ((4, 3, 4, 64), F32), ((4, 6, 4, 64), F32), *small), limit=8, sems=6, micros=3,
    )
    near0 = from_one_side(first)
    (count,) = run_kernel("count", count_body, (after(image_sizes, first),), (), (((8, 128), F32),))
    (second,) = run_kernel(
        "pack_rest", pack_rest_body, (), far(stride_rows, block_rows, after(block_mixers, first)),
        far_out(taps(36)),
        (((16, 64, C), F32), ((2, 9, 64, C), F32), ((2, 64, C), F32), taps(36)), limit=10, sems=4, micros=3,
    )
    near1 = from_one_side(second)
    count = add_along(count, 1, True)
    code_row = code_indices.reshape(1, CELLS)
    image = after(pixels.reshape(384, 128), second, count)
    planes, lanes = ((8, 8, CELLS), F32), ((128, 4 * CELLS), BF16)
    pix, xt, entries = run_kernel(
        "patches", patch_body, (image_sizes,), far(image, code_row, codebook.T), far_out(planes, lanes, THIN),
        (((384, 128), jnp.int32), ((1, CELLS), jnp.int32), ((E, 512), F32), planes, lanes, THIN), limit=12, sems=6, micros=20,
    )
    count = add_along(count, 3, True)
    near0, xt, count = lax.optimization_barrier((near0, xt, count))
    mine0 = from_one_side(half_of(near0, 8, 10))
    stride0 = (first, near0, swap_cores(near0))
    count = add_along(add_along(count, 1, False), 3, False)
    count = count + swap_cores(count)
    mine0, part1, count = lax.optimization_barrier((mine0, half_of(near1, 18, 18), count))
    mine1 = from_one_side(part1)
    stride0 += (mine0, swap_cores(mine0))
    xt, *stride0 = lax.optimization_barrier((xt, *stride0))
    small = (((C, 128), BF16), ((C, 128), BF16), ((C, E), BF16), ((C, E), BF16))
    r0, u0, slope0, av, w0, stem, head, pre, post, patch = run_kernel(
        "front", front_body, (), (*far(xt), *received(stride0)), (WIDE, THREE, *far_out(WIDE, EIGHT, SIXTEEN, *small, PATCH)),
        (lanes, ((4, 2, 64, C), BF16), WIDE, EIGHT, SIXTEEN, *small, PATCH), limit=20, sems=25, micros=12,
    )
    mine1, post = lax.optimization_barrier((mine1, post))
    rest = (second, near1, swap_cores(near1), mine1, swap_cores(mine1))
    half, sent_half = ((4, QUARTER, C), F32), ((4, SENT, C), BF16)
    keep, other = run_kernel(
        "main", main_body, (image_sizes, count),
        (r0, u0, *received(rest), *far(pre, post, entries, head, pix, code_row, stem, slope0, w0, av, xt, patch)),
        (half, sent_half),
        (
            TWENTY, SIXTEEN, ((C, E), BF16), ((C, E), BF16), THIN, ((C, 128), BF16), planes, ((1, CELLS), jnp.int32),
            ((C, 128), BF16), WIDE, SIXTEEN, EIGHT, lanes, PATCH,
            WIDE, WIDE_LOW, WIDE, WIDE_LOW, THIN, THIN_LOW, WIDE, THREE, WIDE, WIDE_LOW, WIDE, THREE,
            ((4, CELLS, C), F32), ((4, CELLS, C), BF16), ((128, 4 * CELLS), F32), lanes,
            EIGHT, THREE, THIN, ((64, C), F32), half, half,
        ),
        limit=53, sems=28, micros=40,
    )

    quarter, sent = ((QUARTER, C), F32), ((SENT, C), BF16)
    parts = run_kernel("add_cores", add_cores_body, (), (keep, swap_cores(other)), (quarter, *(sent,) * 3))
    found = three_others(along_first, *parts[1:])
    (grad,) = run_kernel("add_first", add_first_body, (), (parts[0], found[0], found[2], found[1]), (sent,))
    found = three_others(along_second, grad)
    (grad,) = run_kernel("add_second", add_second_body, (), (grad, found[1], found[0], found[2]), (sent,))
    found = three_others(along_first, grad, back=True)

    own_half, square = run_kernel("join", join_body, (), (grad, found[1], found[0], found[2]), (sent_half, ((8, 128), F32)))
    other_half = swap_cores(own_half)
    found = three_others(along_tensor, square)
    square = (square + found[1]) + (found[0] + found[2])
    square = square + swap_cores(square)

    def viewed(stem, stride, block, mixer, pre, post, codes, head):
        return (
            stem.transpose(0, 2, 1, 3), stride.reshape(2, 1024, C), block.reshape(2, 576, C), mixer,
            pre, post, codes.T, head.transpose(0, 3, 1, 2),
        )

    sets = [
        viewed(
            stem_kernel, stride_kernels, block_kernels, block_mixers, pre_project, post_project, codebook, head_kernel
        ),
        viewed(*moments[:8]),
        viewed(*moments[8:]),
    ]
    given = [sets[i][weight] for weight in range(8) for i in range(3)]
    shapes = [(x.shape, x.dtype) for x in given]
    *news, loss_terms, norm = run_kernel(
        "adam", adam_body, (), (own_half, other_half, square, count, *given),
        (*far_out(*shapes), 4, 1), (*shapes, ((2, 64, C), F32)), limit=24, sems=66, micros=7,
    )

    def restored(stem, stride, block, mixer, pre, post, codes, head):
        return (
            stem.transpose(0, 2, 1, 3), stride.reshape(2, 4, 4, 64, C), block.reshape(2, 3, 3, 64, C), mixer,
            pre, post, codes.T, head.transpose(0, 2, 3, 1),
        )

    return (
        loss_terms.reshape(4),
        norm.reshape(()),
        *restored(*news[0::3]),
        *restored(*news[1::3]),
        *restored(*news[2::3]),
    )


def solution(mesh):
    in_specs = (
        P("dp", None, None, None),
        P("dp", None),
        P("dp", None, None),
        P(None, None, None, "tensor"),
        P(None, None, None, "tensor", None),
        P(None, None, None, "tensor", None),
        P(None, "tensor", None),
        P("tensor", None),
        P(None, "tensor"),
        P(),
        P(None, None, "tensor", None),
        P(None, None, None, "tensor"),
        P(None, None, None, "tensor", None),
        P(None, None, None, "tensor", None),
        P(None, "tensor", None),
        P("tensor", None),
        P(None, "tensor"),
        P(),
        P(None, None, "tensor", None),
        P(None, None, None, "tensor"),
        P(None, None, None, "tensor", None),
        P(None, None, None, "tensor", None),
        P(None, "tensor", None),
        P("tensor", None),
        P(None, "tensor"),
        P(),
        P(None, None, "tensor", None),
    )
    out_specs = (
        P(),
        P(),
        P(None, None, None, "tensor"),
        P(None, None, None, "tensor", None),
        P(None, None, None, "tensor", None),
        P(None, "tensor", None),
        P("tensor", None),
        P(None, "tensor"),
        P(),
        P(None, None, "tensor", None),
        P(None, None, None, "tensor"),
        P(None, None, None, "tensor", None),
        P(None, None, None, "tensor", None),
        P(None, "tensor", None),
        P("tensor", None),
        P(None, "tensor"),
        P(),
        P(None, None, "tensor", None),
        P(None, None, None, "tensor"),
        P(None, None, None, "tensor", None),
        P(None, None, None, "tensor", None),
        P(None, "tensor", None),
        P("tensor", None),
        P(None, "tensor"),
        P(),
        P(None, None, "tensor", None),
    )
    return jax.shard_map(
        on_device, mesh=mesh, in_specs=in_specs, out_specs=out_specs, check_vma=False
    )
```

```python
import math

import jax
import jax.numpy as jnp
from jax import lax
from jax.experimental import pallas as pl
from jax.experimental.pallas import tpu as pltpu
from jax.sharding import PartitionSpec as P

C = 256
E = 64
STEP = 10
SIDE = 32
CELLS = SIDE * SIDE
PADDED = CELLS + 2 * SIDE

beta_commit = 0.25
clip_norm = 0.002
beta_one = 0.9
beta_two = 0.999
adam_eps = 1e-08
decay_rate = 0.01
half_bin = 1.0 / 255.0
root_half = 0.7071067811865476
gelu_root = 0.7978845608028654
gelu_cube = 0.044715

F32 = jnp.float32
BF16 = jnp.bfloat16

UP_SHIFT = (-1, 0, 0, 1)
DOWN_PARITY = (1, 0, 1, 0)
DOWN_SHIFT = (-1, 0, 0, 1)


def here():
    index = lax.axis_index("dp")
    core = index % 2
    return lax.axis_index("tensor"), core, jnp.where(core == 0, index // 8, (index // 2) % 4)


def nn(left, right):
    return lax.dot_general(left, right, (((1,), (0,)), ((), ())), preferred_element_type=F32)


def nt(left, right):
    return lax.dot_general(left, right, (((1,), (1,)), ((), ())), preferred_element_type=F32)


def gelu(x):
    return x * (0.5 * (1.0 + jnp.tanh(gelu_root * (x + gelu_cube * (x * x * x)))))


def gelu_both(x):
    square = x * x
    t = jnp.tanh(x * (gelu_root + gelu_root * gelu_cube * square))
    share = 0.5 + 0.5 * t
    bend = 0.5 * gelu_root + 1.5 * gelu_root * gelu_cube * square
    return x * share, share + x * (1.0 - t * t) * bend


def columns(shape):
    return lax.broadcasted_iota(jnp.int32, shape, 0) % SIDE


def left_of(x):
    return jnp.where(columns(x.shape) == 0, 0.0, pltpu.roll(x, 1, 0))


def right_of(x):
    return jnp.where(columns(x.shape) == SIDE - 1, 0.0, pltpu.roll(x, x.shape[0] - 1, 0))


def clear_edges(ref, index):
    edge = jnp.zeros((SIDE, C), BF16)
    ref[index, 0:SIDE, :] = edge
    ref[index, PADDED - SIDE : PADDED, :] = edge


def store_three(ref, x):
    for index in range(3):
        clear_edges(ref, index)
    ref[0, SIDE : SIDE + CELLS, :] = left_of(x).astype(BF16)
    ref[1, SIDE : SIDE + CELLS, :] = x.astype(BF16)
    ref[2, SIDE : SIDE + CELLS, :] = right_of(x).astype(BF16)


def store_two(ref, phase, x):
    clear_edges(ref, 2 * phase)
    clear_edges(ref, 2 * phase + 1)
    moved = right_of(x) if phase % 2 == 0 else left_of(x)
    ref[2 * phase, SIDE : SIDE + CELLS, :] = x.astype(BF16)
    ref[2 * phase + 1, SIDE : SIDE + CELLS, :] = moved.astype(BF16)


def window(ref, index, shift):
    return ref[index, (shift + 1) * SIDE : (shift + 1) * SIDE + CELLS, :]


def three(ref, row_shift, col_shift):
    return window(ref, col_shift + 1, row_shift)


def two(ref, phase, row_shift, col_shift):
    return window(ref, 2 * phase + (0 if col_shift == 0 else 1), row_shift)


def own_lanes(x, tensor):
    half = jnp.where(tensor >= 2, x[:, 128:256], x[:, 0:128])
    return jnp.where(tensor % 2 == 1, pltpu.roll(half, 64, 1), half)[:, 0:64]


def lane_grid(shape):
    lane = lax.broadcasted_iota(jnp.int32, shape, 1)
    return lane // SIDE, lane % SIDE


def moved_plane(x, row_shift, col_shift):
    if row_shift == 0 and col_shift == 0:
        return x
    y = pltpu.roll(x, (-(SIDE * row_shift + col_shift)) % CELLS, 1)
    rows, cols = lane_grid(x.shape)
    keep = None
    for index, shift in ((rows, row_shift), (cols, col_shift)):
        if shift != 0:
            ok = (index < SIDE - 1) if shift == 1 else (index > 0)
            keep = ok if keep is None else (keep & ok)
    return jnp.where(keep, y, 0.0)


def same_forward(source, weight_ref, first):
    total = None
    for row in range(3):
        for col in range(3):
            term = nt(three(source, row - 1, col - 1), weight_ref[first + 3 * row + col])
            total = term if total is None else total + term
    return total


def same_backward(source, weight_ref, first):
    total = None
    for row in range(3):
        for col in range(3):
            term = nn(three(source, 1 - row, 1 - col), weight_ref[first + 3 * row + col])
            total = term if total is None else total + term
    return total


def down_forward(source, weight_ref):
    total = None
    for row in range(4):
        for col in range(4):
            phase = 2 * DOWN_PARITY[row] + DOWN_PARITY[col]
            term = nt(two(source, phase, DOWN_SHIFT[row], DOWN_SHIFT[col]), weight_ref[4 * row + col])
            total = term if total is None else total + term
    return total


def split_three(x):
    first = x.astype(BF16)
    rest = x - first.astype(F32)
    second = rest.astype(BF16)
    return first, second, (rest - second.astype(F32)).astype(BF16)


def one_hot_codes(codes_ref):
    return (
        (lax.broadcasted_iota(jnp.int32, (512, CELLS), 0) == codes_ref[...]).astype(F32).astype(BF16)
    )


def patch_body(
    sizes, image_in, codes_in, book_in, pix_out, x_out, entries_out,
    image_ref, codes_ref, book_ref, pix_ref, x_ref, entries_ref, sems,
):
    high, wide = sizes[0, 0] // 4, sizes[0, 1] // 4
    copies = copy_all(
        sems,
        [
            (image_in, image_ref), (codes_in, codes_ref), (book_in, book_ref),
            (pix_ref, pix_out), (entries_ref, entries_out), (x_ref, x_out),
        ],
    )
    start_all(copies[0:3])
    wait_all(copies[0:3])
    book = jnp.concatenate(split_three(book_ref[...]), 0)
    found = nn(book, one_hot_codes(codes_ref))
    entries_ref[...] = ((found[0:64] + found[64:128]) + found[128:192]).T
    copies[4].start()
    image = image_ref[...].astype(F32).astype(BF16)
    lane = lax.broadcasted_iota(jnp.int32, (128, CELLS), 1)
    source = lax.broadcasted_iota(jnp.int32, (128, CELLS), 0)
    row = lax.broadcasted_iota(jnp.int32, (384, CELLS), 0)
    own_row = (row // 4) % SIDE == lax.broadcasted_iota(jnp.int32, (384, CELLS), 1) // SIDE
    slot = lax.broadcasted_iota(jnp.int32, (32, 384), 0)
    line = lax.broadcasted_iota(jnp.int32, (32, 384), 1)
    pick = ((line % 4 == slot // 8) & (line // 128 == slot % 8)).astype(F32).astype(BF16)
    planes = {}
    for col in range(4):
        spread = (source == 4 * (lane % SIDE) + col).astype(F32).astype(BF16)
        lined = jnp.where(own_row, nn(image, spread), 0.0).astype(BF16)
        found = nn(pick, lined)
        for r in range(4):
            planes[r, col] = found[8 * r : 8 * r + 8]
    for r in range(4):
        for half in range(2):
            pix_ref[2 * r + half] = planes[r, 2 * half] + pltpu.roll(planes[r, 2 * half + 1], 4, 0)
    copies[3].start()
    rows, cols = lane_grid((8, CELLS))
    channel = lax.broadcasted_iota(jnp.int32, (8, CELLS), 0)
    inside = (rows < high) & (cols < wide) & (channel < 3)
    planes = {key: jnp.where(inside, value / 127.5 - 1.0, 0.0) for key, value in planes.items()}
    moved = {}
    for r in range(-1, 5):
        for c in range(-1, 5):
            moved[r, c] = moved_plane(planes[r % 4, c % 4], r // 4, c // 4)
    for p in range(2):
        for q in range(2):
            for kh in range(4):
                for kw in range(0, 4, 2):
                    r, c = 2 * p + kh - 1, 2 * q + kw - 1
                    tap = 4 * kh + kw
                    x_ref[8 * tap : 8 * tap + 16, (2 * p + q) * CELLS : (2 * p + q + 1) * CELLS] = (
                        jnp.concatenate([moved[r, c], moved[r, c + 1]], 0).astype(BF16)
                    )
    copies[5].start()
    wait_all(copies[3:])


def copy_all(sems, pairs):
    return [pltpu.make_async_copy(source, target, sems.at[i]) for i, (source, target) in enumerate(pairs)]


def start_all(copies):
    for copy in copies:
        copy.start()


def wait_all(copies):
    for copy in copies:
        copy.wait()


def count_body(sizes, count_ref):
    count_ref[...] = jnp.full((8, 128), (sizes[0, 0] // 4) * (sizes[0, 1] // 4), jnp.int32).astype(F32)


def pack_first_body(
    stride_in, stem_in, head_in, pre_in, post_in, out_ref,
    stride_ref, stem_ref, head_ref, pre_ref, post_ref, sems,
):
    copies = copy_all(
        sems,
        [
            (stem_in, stem_ref), (head_in, head_ref), (pre_in, pre_ref), (post_in, post_ref),
            (stride_in.at[0, 0:8], stride_ref.at[0:8]), (stride_in.at[0, 8:16], stride_ref.at[8:16]),
        ],
    )
    start_all(copies[0:6])
    wait_all(copies[0:4])

    def ordered(ref, per):
        rows = jnp.concatenate([ref[kh, c] for kh in range(4) for c in range(per)], 0)
        count = 16 * per
        slot = lax.broadcasted_iota(jnp.int32, (128, count), 0)
        line = lax.broadcasted_iota(jnp.int32, (128, count), 1)
        channel = slot % 8
        if per == 6:
            channel = jnp.where(channel % 4 == 3, per, channel - channel // 4)
        wanted = (slot // 32) * 4 * per + channel * 4 + (slot // 8) % 4
        pick = ((line == wanted) & (channel < per)).astype(F32).astype(BF16)
        return nn(pick, rows.astype(BF16)).T

    out_ref[8] = jnp.concatenate([ordered(stem_ref, 3), ordered(head_ref, 6)], 1).astype(BF16)
    thin = jnp.concatenate([pre_ref[...], post_ref[...].T], 1)
    out_ref[9] = jnp.concatenate([thin, thin], 1).astype(BF16)
    for k in range(2):
        copies[4 + k].wait()
        out_ref[10 * k : 10 * k + 8] = stride_ref[8 * k : 8 * k + 8].astype(BF16)


def pack_rest_body(stride_in, block_in, mix_in, out, stride_ref, block_ref, mix_ref, out_ref, sems):
    copies = copy_all(
        sems,
        [
            (block_in, block_ref), (mix_in, mix_ref), (stride_in.at[1], stride_ref), (out_ref, out),
        ],
    )
    start_all(copies[0:3])
    wait_all(copies[0:3])
    for b in range(2):
        out_ref[18 * b : 18 * b + 9] = block_ref[b].astype(BF16)
        out_ref[18 * b + 9] = mix_ref[b].astype(BF16)
        out_ref[18 * b + 10 : 18 * b + 18] = stride_ref[8 * b : 8 * b + 8].astype(BF16)
    start_all(copies[3:])
    wait_all(copies[3:])


def gather_pairs(ref, parts, tensor, core, rotated, low, high, half_low):
    def rows(step):
        if rotated and isinstance(step, int):
            return pl.ds(64 * step, 64)
        return pl.ds(pl.multiple_of((64 * step if rotated else ((tensor + step) % 4) * 64), 64), 64)

    count = ref.shape[0] // 2
    pairs = []
    for part, step in zip(parts[0:3], (0, 1 + 2 * core, 3 - 2 * core), strict=True):
        for k, start in enumerate((low, high)):
            pairs.append((part.at[start : start + count], ref.at[count * k : count * k + count, rows(step), :]))
    for part, half in ((parts[3], core), (parts[4], 1 - core)):
        source = part.at[pl.ds(half_low(half), count)]
        pairs.append((source, ref.at[pl.ds(count * half, count), rows(2), :]))
    return pairs


def block_forward(resid, u_ref, w_ref, first, v_ref, q_ref):
    value, v_ref[...] = gelu_both(same_forward(u_ref, w_ref, first))
    act = value.astype(BF16)
    q_ref[...] = act
    return resid + nn(act, w_ref[first + 9])


def front_body(
    x_in, own, near, far, mine, other,
    r_ref, u_ref, slope_out, a_out, w_out, stem_out, head_out, pre_out, post_out, patch_out,
    x_ref, small_ref, slope_ref, a_ref, w_ref, stem_ref, head_ref, pre_ref, post_ref, patch_ref, sems,
):
    tensor, core, _ = here()
    small = [part.at[8:10] for part in (own, near, far)] + [mine.at[pl.ds(8 * (1 - core), 2)]]
    pairs = [(x_in, x_ref)] + [(part, small_ref.at[k]) for k, part in enumerate(small)]
    pairs += gather_pairs(w_ref, (own, near, far, mine, other), tensor, core, False, 0, 10, lambda half: 2 * half)
    copies = copy_all(sems, pairs)
    start_all(copies)
    outs = [(stem_ref, stem_out), (head_ref, head_out), (pre_ref, pre_out), (post_ref, post_out), (w_ref, w_out)]
    outs += [(a_ref.at[2 * p : 2 * p + 2], a_out.at[2 * p : 2 * p + 2]) for p in range(4)]
    outs += [(patch_ref, patch_out), (slope_ref, slope_out)]
    writes = [
        pltpu.make_async_copy(source, target, sems.at[len(copies) + i]) for i, (source, target) in enumerate(outs)
    ]
    wait_all(copies[0:5])
    for k, step in enumerate((0, 1 + 2 * core, 3 - 2 * core, 2)):
        rows = pl.ds(pl.multiple_of(((tensor + step) % 4) * 64, 64), 64)
        turned = 64 * step if isinstance(step, int) else pl.multiple_of(64 * step, 64)
        stem_ref[rows, :] = small_ref[k, 0, :, 0:128]
        head_ref[pl.ds(turned, 64), :] = small_ref[k, 0, :, 128:256]
        pre_ref[rows, :] = small_ref[k, 1, :, 0:64]
        post_ref[rows, :] = small_ref[k, 1, :, 64:128]
    start_all(writes[0:4])
    for phase in range(4):
        patch = x_ref[:, phase * CELLS : (phase + 1) * CELLS].T
        patch_ref[phase * CELLS : (phase + 1) * CELLS, :] = patch
        store_two(a_ref, phase, gelu(nt(patch, stem_ref[...])))
        writes[5 + phase].start()
    writes[9].start()
    wait_all(copies[5:])
    writes[4].start()
    resid = down_forward(a_ref, w_ref)
    r_ref[...] = resid
    value, slope_ref[...] = gelu_both(resid)
    writes[10].start()
    store_three(u_ref, value)
    wait_all(writes)


def valid_cells(sizes):
    cell = lax.broadcasted_iota(jnp.int32, (CELLS, E), 0)
    return (cell // SIDE < sizes[0, 0] // 4) & (cell % SIDE < sizes[0, 1] // 4)


def poly(x, coefs):
    total = jnp.full_like(x, coefs[0])
    for c in coefs[1:]:
        total = total * x + c
    return total


ERFC_LOW = (
    2.326819970068386e-2, -1.387039388740657e-1, 3.687424674597105e-1, -5.824733027278666e-1,
    6.210004621745983e-1, -4.944515323274145e-1, 3.404879937665872e-1, -2.741127028184656e-1,
    5.638259427386472e-1,
)
ERFC_HIGH = (
    -1.047766399936249e1, 1.297719955372516e1, -7.495518717768503e0, 2.921019019210786e0,
    -1.015265279202700e0, 4.218463358204948e-1, -2.820767439740514e-1, 5.641895067754075e-1,
)
ERF_NEAR = (
    7.853861353153693e-5, -8.010193625184903e-4, 5.188327685732524e-3, -2.685381193529856e-2,
    1.128358514861418e-1, -3.761262582423300e-1, 1.128379165726710e0,
)


def erfc(x):
    size = jnp.abs(x)
    square = x * x
    far_exp = jnp.exp(-square)
    recip = 1.0 / jnp.maximum(size, 0.5)
    y = recip * recip
    far = far_exp * recip * jnp.where(size < 2.0, poly(y, ERFC_LOW), poly(y, ERFC_HIGH))
    far = jnp.where(x < 0, 2.0 - far, far)
    near = 1.0 - x * poly(square, ERF_NEAR)
    return jnp.where(size > 1.0, far, near), far_exp


def likelihood(center_out, scale_out, pix, keep, scale):
    target = pix / 127.5 - 1.0
    center = jnp.tanh(center_out)
    decay = jnp.exp(-jnp.abs(scale_out))
    sigma = 0.25 + (jnp.maximum(scale_out, 0.0) + jnp.log(1.0 + decay))
    gate = jnp.where(scale_out >= 0, 1.0, decay) / (1.0 + decay)
    low_end, high_end = pix == 0.0, pix == 255.0
    lower = jnp.where(low_end, -40.0, (target - half_bin - center) / sigma)
    upper = jnp.where(high_end, 40.0, (target + half_bin - center) / sigma)
    right = lower + upper > 0
    tail_a, exp_a = erfc(jnp.where(right, lower, -upper) * root_half)
    tail_b, exp_b = erfc(jnp.where(right, upper, -lower) * root_half)
    mass = 0.5 * (tail_a - tail_b)
    bits = jnp.where(keep, jnp.log(mass), 0.0)
    density = 1.0 / math.sqrt(2.0 * math.pi)
    slope = jnp.where(keep, scale * density / mass, 0.0)
    low_slope = jnp.where(low_end, 0.0, -slope * jnp.where(right, exp_a, exp_b))
    high_slope = jnp.where(high_end, 0.0, slope * jnp.where(right, exp_b, exp_a))
    center_grad = -(low_slope + high_slope) / sigma
    sigma_grad = -(low_slope * lower + high_slope * upper) / sigma
    return bits, center_grad * (1.0 - center * center), sigma_grad * gate


def head_links():
    for p in range(2):
        for q in range(2):
            for kh in range(4):
                for kw in range(4):
                    up, left = p + UP_SHIFT[kh], q + UP_SHIFT[kw]
                    out = (2 * p + kh % 2, 2 * q + kw % 2)
                    yield out, 4 * kh + kw, 2 * (up % 2) + left % 2, up // 2, left // 2


QUARTER = 448
KINDS = {"stride": (0, 256), "block": (256, 144), "mixer": (400, 16), "codes": (416, 16), "small": (432, 16)}


def store_rows(g_ref, kind, start, value):
    base, size = KINDS[kind]
    done = 0
    while done < value.shape[0]:
        place = start + done
        count = min(size - place % size, value.shape[0] - done)
        first = base + place % size
        g_ref[place // size, first : first + count, :] = value[done : done + count]
        done += count


def with_scalar(x, scalar):
    row = lax.broadcasted_iota(jnp.int32, (64, 64), 0)
    lane = lax.broadcasted_iota(jnp.int32, (64, 64), 1)
    return jnp.concatenate([x, jnp.where((row == 0) & (lane == 0), scalar, 0.0)], 1)


def block_backward(grad_out, resid_ref, u_ref, v_ref, q_ref, w_ref, first, dv_ref, g_ref):
    low = grad_out.astype(BF16)
    own_q = q_ref[:, 0:128].astype(F32).T[0:64].astype(BF16)
    store_rows(g_ref, "mixer", 0, nn(own_q, low))
    mid = nt(low, w_ref[first + 9])
    inner = v_ref[...] * mid
    store_three(dv_ref, inner)
    own = inner[:, 0:128].T[0:64].astype(BF16)
    for row in range(3):
        for col in range(3):
            tap = 3 * row + col
            store_rows(g_ref, "block", 64 * tap, nn(own, three(u_ref, row - 1, col - 1)))
    return grad_out + resid_ref[...] * same_backward(dv_ref, w_ref, first)


def forward_blocks(
    sizes, r0_ref, u0_ref, w_ref, pre_ref, post_ref, entries_ref,
    v0_ref, q0_ref, r1_ref, act_ref, diff_ref, zq_ref, r2_ref, u2_ref, v1_ref, q1_ref, r3_ref, u3_ref, waits,
):
    resid = block_forward(r0_ref[...], u0_ref, w_ref, 0, v0_ref, q0_ref)
    value, r1_ref[...] = gelu_both(resid)
    act = value.astype(BF16)
    act_ref[...] = act
    wait_all(waits)
    latent = nn(act, pre_ref[...])
    entries = entries_ref[...]
    diff = latent - entries
    diff_ref[...] = diff
    code = (latent + (entries - latent)).astype(BF16)
    zq_ref[...] = code
    resid = nt(code, post_ref[...])
    value, r2_ref[...] = gelu_both(resid)
    store_three(u2_ref, value)
    resid = block_forward(resid, u2_ref, w_ref, 10, v1_ref, q1_ref)
    value, r3_ref[...] = gelu_both(resid)
    store_three(u3_ref, value)
    return (1.0 + beta_commit) * jnp.sum(jnp.where(valid_cells(sizes), diff * diff, 0.0))


def main_body(
    sizes, total_ref, r0_ref, u0_ref, own, near, far, mine, other,
    pre_in, post_in, entries_in, head_in, pix_in, codes_in, stem_in, r0s_in, w0_in, a_in, x_in, patch_in,
    keep_ref, send_ref,
    wb_ref, w_ref, pre_ref, post_ref, entries_ref, head_ref, pix_ref, codes_ref, stem_ref, r0s_ref, w0_ref, a_ref, x_ref, patch_ref,
    v0_ref, q0_ref, r1_ref, act_ref, diff_ref, zq_ref, r2_ref, u2_ref, v1_ref, q1_ref, r3_ref, u3_ref,
    h4_ref, a4_ref, prod_ref, q_ref, dh_ref, dv_ref, back_ref, late_ref, gd_ref, g_ref, sems,
):
    tensor, core, _ = here()
    parts = (own, near, far, mine, other)
    pairs = gather_pairs(wb_ref, parts, tensor, core, True, 0, 18, lambda half: 0)
    pairs += [(pre_in, pre_ref), (post_in, post_ref), (entries_in, entries_ref)]
    pairs += gather_pairs(w_ref, parts, tensor, core, True, 10, 28, lambda half: 10)
    pairs += [(head_in, head_ref), (pix_in, pix_ref), (codes_in, codes_ref), (stem_in, stem_ref)]
    pairs += [(r0s_in, r0s_ref), (w0_in, w0_ref), (a_in, a_ref), (x_in, x_ref), (patch_in, patch_ref)]
    copies = copy_all(sems, pairs)
    start_all(copies[0:8])
    wait_all(copies[0:8])
    start_all(copies[8:])
    vq = forward_blocks(
        sizes, r0_ref, u0_ref, wb_ref, pre_ref, post_ref, entries_ref,
        v0_ref, q0_ref, r1_ref, act_ref, diff_ref, zq_ref, r2_ref, u2_ref, v1_ref, q1_ref, r3_ref, u3_ref, copies[8:11],
    )
    wait_all(copies[11:19])
    decode_back(
        sizes, total_ref, pix_ref, r3_ref, u3_ref, head_ref, r2_ref, u2_ref, v1_ref, q1_ref, wb_ref,
        gd_ref, w_ref, h4_ref, a4_ref, prod_ref, q_ref, dh_ref, dv_ref, zq_ref, post_ref, back_ref, copies[19:21],
    )
    wait_all(copies[21:])
    encode_back(
        sizes, total_ref, vq, back_ref, diff_ref, codes_ref, r1_ref, act_ref, pre_ref, stem_ref, x_ref, patch_ref, a_ref,
        r0s_ref, u0_ref, v0_ref, q0_ref, wb_ref, w0_ref, gd_ref, keep_ref, send_ref, dv_ref, dh_ref, g_ref, late_ref,
    )


def decode_back(
    sizes, total_ref, pix_ref, r3_ref, u3_ref, head_ref, r2_ref, u2_ref, v1_ref, q1_ref, w1_ref,
    g_ref, w_ref, h4_ref, a4_ref, prod_ref, q_ref, dh_ref, dv_ref, zq_ref, post_ref, back_ref, early,
):
    tensor, _, _ = here()
    high, wide = sizes[0, 0] // 4, sizes[0, 1] // 4
    wait_all(early)
    head = head_ref[...].astype(F32).T.astype(BF16)
    for p in range(2):
        for q in range(2):
            phase = 2 * p + q
            total = None
            for kh in (p, p + 2):
                for kw in (q, q + 2):
                    term = nt(three(u3_ref, UP_SHIFT[kh], UP_SHIFT[kw]), w_ref[4 * kh + kw])
                    total = term if total is None else total + term
            value, h4_ref[phase] = gelu_both(total)
            act = value.astype(BF16)
            a4_ref[phase] = act
            prod_ref[:, phase * CELLS : (phase + 1) * CELLS] = nt(head, act)
    outs = {}
    for out, tap, phase, up, left in head_links():
        term = moved_plane(
            prod_ref[8 * tap : 8 * tap + 8, phase * CELLS : (phase + 1) * CELLS], up, left
        )
        outs[out] = term if out not in outs else outs[out] + term
    sub = lax.broadcasted_iota(jnp.int32, (8, CELLS), 0)
    rows, cols = lane_grid((8, CELLS))
    keep = (rows < high) & (cols < wide) & (sub % 4 != 3)
    first = sub < 4
    scale = -1.0 / (math.log(2.0) * 48.0 * total_ref[0, 0])
    grads = {}
    bits = None
    for pair in range(8):
        row, col = pair // 2, 2 * (pair % 2)
        one, other = outs[row, col], outs[row, col + 1]
        centers = jnp.where(first, one, pltpu.roll(other, 4, 0))
        scales = jnp.where(first, pltpu.roll(one, 4, 0), other)
        part, center_grad, scale_grad = likelihood(centers, scales, pix_ref[pair], keep, scale)
        bits = part if bits is None else bits + part
        grads[row, col] = jnp.where(first, center_grad, pltpu.roll(scale_grad, 4, 0))
        grads[row, col + 1] = jnp.where(first, pltpu.roll(center_grad, 4, 0), scale_grad)
    bits = -jnp.sum(bits) / math.log(2.0)
    found = {}
    for out, tap, phase, up, left in head_links():
        found[tap, phase] = moved_plane(grads[out], -up, -left)
    for phase in range(4):
        for tap in range(0, 16, 2):
            q_ref[8 * tap : 8 * tap + 16, phase * CELLS : (phase + 1) * CELLS] = jnp.concatenate(
                [found[tap, phase], found[tap + 1, phase]], 0
            ).astype(BF16)
    head_grad = None
    for phase in range(4):
        spread = q_ref[:, phase * CELLS : (phase + 1) * CELLS]
        term = nn(spread, a4_ref[phase, :, 0:64])
        head_grad = term if head_grad is None else head_grad + term
        slope = h4_ref[phase] * nn(spread.T, head)
        store_two(dh_ref, phase, slope)
        own = slope[:, 0:128].T[0:64].astype(BF16)
        for kh in (phase // 2, phase // 2 + 2):
            for kw in (phase % 2, phase % 2 + 2):
                tap = 4 * kh + kw
                store_rows(g_ref, "stride", 64 * tap, nn(own, three(u3_ref, UP_SHIFT[kh], UP_SHIFT[kw])))
    total = None
    for kh in range(4):
        for kw in range(4):
            phase = 2 * (kh % 2) + kw % 2
            term = nn(two(dh_ref, phase, -UP_SHIFT[kh], -UP_SHIFT[kw]), w_ref[4 * kh + kw])
            total = term if total is None else total + term
    grad = r3_ref[...] * total
    grad = block_backward(grad, r2_ref, u2_ref, v1_ref, q1_ref, w1_ref, 10, dv_ref, g_ref)
    low = grad.astype(BF16)
    post_grad = nn(zq_ref[...].astype(F32).T.astype(BF16), own_lanes(grad, tensor).astype(BF16))
    small = jnp.concatenate([post_grad, head_grad[0:64], head_grad[64:128]], 1)
    store_rows(g_ref, "small", 0, with_scalar(small, bits))
    back_ref[...] = nn(low, post_ref[...])


def encode_back(
    sizes, total_ref, vq, back_ref, diff_ref, codes_ref, r1_ref, act_ref, pre_ref, stem_ref, x_ref, patch_ref, a_ref,
    r0_ref, u_ref, v_ref, q_ref, wb_ref, w_ref, gd_ref, keep_ref, send_ref, dv_ref, dr_ref, g_ref, late_ref,
):
    tensor, core, _ = here()
    scaled = jnp.where(valid_cells(sizes), diff_ref[...] / (64.0 * total_ref[0, 0]), 0.0)
    dz = (back_ref[...] + 2.0 * beta_commit * scaled).astype(BF16)
    hot = one_hot_codes(codes_ref)
    found = nt(jnp.concatenate(split_three((-2.0 * scaled).T), 0), hot)
    codes = (found[0:64] + found[64:128]) + found[128:192]
    store_rows(g_ref, "codes", 0, codes[:, 0:256])
    late_ref[...] = codes[:, 256:512]
    act = own_lanes(act_ref[...].astype(F32), tensor)
    pre_grad = nn(act.T.astype(BF16), dz)
    grad = r1_ref[...] * nt(dz, pre_ref[...])
    grad = block_backward(grad, r0_ref, u_ref, v_ref, q_ref, wb_ref, 0, dv_ref, g_ref)
    store_three(dr_ref, grad)
    own = own_lanes(grad, tensor).T.astype(BF16)
    for kh in range(4):
        for kw in range(4):
            tap = 4 * kh + kw
            phase = 2 * DOWN_PARITY[kh] + DOWN_PARITY[kw]
            term = nn(own, two(a_ref, phase, DOWN_SHIFT[kh], DOWN_SHIFT[kw]))
            store_rows(g_ref, "stride", 64 * tap, term)
    line = lax.broadcasted_iota(jnp.int32, (C, C), 0)
    lane = lax.broadcasted_iota(jnp.int32, (C, C), 1)
    shifts = [(up, left) for up in (-1, 0, 1) for left in (-1, 0, 1)]
    before = total = None
    stem = stem_ref[pl.ds(pl.multiple_of(64 * tensor, 64), 64), :].astype(F32).T.astype(BF16)
    for phase in range(4):
        place = (lane[0:64] == line[0:64] + 64 * phase).astype(F32).astype(BF16)
        wide = nn(stem, place).astype(BF16)
        term = nn(patch_ref[phase * CELLS : (phase + 1) * CELLS, :], wide)
        before = term if before is None else before + term
    picks = [
        ((lane == line - 64 * tensor + 64 * phase) & (lane // 64 == phase)).astype(F32).astype(BF16) for phase in range(4)
    ]
    for up, left in shifts:
        weight = None
        for kh in range(4):
            for kw in range(4):
                if (-DOWN_SHIFT[kh], -DOWN_SHIFT[kw]) == (up, left):
                    term = nn(w_ref[4 * kh + kw], picks[2 * DOWN_PARITY[kh] + DOWN_PARITY[kw]])
                    weight = term if weight is None else weight + term
        term = nn(three(dr_ref, up, left), weight.astype(BF16))
        total = term if total is None else total + term
    slope = (gelu_both(before)[1] * total).astype(BF16)
    stem_grad = None
    for phase in range(4):
        term = nn(x_ref[:, phase * CELLS : (phase + 1) * CELLS], slope)[:, 64 * phase : 64 * phase + 64]
        stem_grad = term if stem_grad is None else stem_grad + term
    small = jnp.concatenate([pre_grad, stem_grad[0:64], stem_grad[64:128]], 1)
    store_rows(g_ref, "small", 0, with_scalar(small, vq))
    base = KINDS["codes"][0]
    for part in range(4):
        gd_ref[part, base : base + 16, :] = late_ref[16 * part : 16 * part + 16, :]

    @pl.when(core == 0)
    def _():
        keep_ref[...] = g_ref[...]
        for part in range(4):
            put_sent(send_ref.at[part], gd_ref[part])

    @pl.when(core == 1)
    def _():
        keep_ref[...] = gd_ref[...]
        for part in range(4):
            put_sent(send_ref.at[part], g_ref[part])


SENT = QUARTER + 32
SMALL_ROWS = KINDS["small"][0]


def put_sent(out, value):
    out[0:SMALL_ROWS, :] = value[0:SMALL_ROWS].astype(BF16)
    for k, part in enumerate(split_three(value[SMALL_ROWS:QUARTER])):
        out[SMALL_ROWS + 16 * k : SMALL_ROWS + 16 * k + 16, :] = part


def small_of(ref):
    parts = [ref[SMALL_ROWS + 16 * k : SMALL_ROWS + 16 * k + 16, :].astype(F32) for k in range(3)]
    return (parts[0] + parts[1]) + parts[2]


def whole(ref):
    return jnp.concatenate([ref[0:SMALL_ROWS, :].astype(F32), small_of(ref)], 0)


def add_cores_body(keep_ref, other_ref, own_ref, *outs):
    _, _, place = here()
    own_ref[...] = keep_ref[place] + whole(other_ref.at[place])
    for k, out in enumerate(outs):
        part = (place + 1 + k) % 4
        put_sent(out, keep_ref[part] + whole(other_ref.at[part]))


def four(own, one, two_on, three_on):
    return (own + whole(two_on)) + (whole(one) + whole(three_on))


def add_first_body(own, one, three_on, two_on, out):
    put_sent(out, four(own[...], one, two_on, three_on))


def add_second_body(own, two_on, one, three_on, out):
    put_sent(out, four(whole(own), one, two_on, three_on))


def join_body(own, two_on, one, three_on, half_ref, square_ref):
    _, _, place = here()
    row = lax.broadcasted_iota(jnp.int32, (QUARTER, C), 0)
    lane = lax.broadcasted_iota(jnp.int32, (QUARTER, C), 1)
    share = jnp.where((row >= KINDS["codes"][0]) & (row < SMALL_ROWS), 0.25, 1.0)
    share = jnp.where((row >= SMALL_ROWS) & (lane >= 192), 0.0, share)
    total = jnp.zeros((QUARTER, C), F32)
    for k, part in enumerate((own, one, two_on, three_on)):
        half_ref[(place + k) % 4] = part[...]
        value = whole(part)
        total = total + value * value
    square_ref[...] = jnp.full((8, 128), jnp.sum(total * share), F32)


def adam(weight, moment, second, grad, rate):
    m_new = beta_one * moment + (1.0 - beta_one) * grad
    v_new = beta_two * second + ((1.0 - beta_two) * grad) * grad
    change = (rate / (1.0 - beta_one**STEP)) * m_new
    size = jnp.sqrt((1.0 / (1.0 - beta_two**STEP)) * v_new) + adam_eps
    return (1.0 - rate * decay_rate) * weight - change / size, m_new, v_new


RATES = (
    48.0 ** (-0.5),
    (16.0 * C) ** (-0.5),
    (9.0 * C) ** (-0.5),
    C ** (-0.5),
    C ** (-0.5),
    E ** (-0.5),
    0.6,
    (4.0 * C) ** (-0.5),
)


def adam_body(half_ref, other_ref, square_ref, total_ref, *refs):
    _, core, _ = here()
    given, outs, loss_ref, norm_ref = refs[0:24], refs[24:48], refs[48], refs[49]
    results, small_ref, sems = refs[50:74], refs[74], refs[75]
    norm = jnp.sqrt(square_ref[...])
    factor = jnp.minimum(1.0, clip_norm / (norm + 1e-06))[0:1, 0:1]
    norm_ref[0, 0] = jnp.max(norm)

    def rows_of(side, part, kind):
        if kind == "small":
            return jnp.where(core == side, small_of(half_ref.at[part]), small_of(other_ref.at[part]))
        base, size = KINDS[kind]
        mine, theirs = half_ref[part, base : base + size, :], other_ref[part, base : base + size, :]
        return jnp.where(core == side, mine.astype(F32), theirs.astype(F32))

    def update(weight, index, grad):
        values = [given[3 * weight + i][index] for i in range(3)]
        for i, value in enumerate(adam(*values, factor * grad, RATES[weight])):
            results[3 * weight + i][index] = value

    copies = []

    def finish(weight, index=None):
        for i in range(3):
            source, target = results[3 * weight + i], outs[3 * weight + i]
            if index is not None:
                source, target = source.at[index], target.at[index]
            copies.append(pltpu.make_async_copy(source, target, sems.at[len(copies)]))
            copies[-1].start()

    for side in range(2):
        for part in range(4):
            small_ref[side, 16 * part : 16 * part + 16, :] = rows_of(side, part, "small")
            update(3, (side, pl.ds(16 * part, 16), slice(None)), rows_of(side, part, "mixer"))
            update(6, (pl.ds(16 * part, 16), pl.ds(256 * side, 256)), rows_of(side, part, "codes"))
    finish(3)
    finish(6)
    for weight, side, channels in ((0, 0, 3), (7, 1, 6)):
        spread = small_ref[side, :, 64:192]
        for kh in range(4):
            block = spread[32 * (kh % 2) : 32 * (kh % 2) + 32, 64 * (kh // 2) : 64 * (kh // 2) + 64]
            for c in range(channels):
                slot = c + (c // 3 if channels == 6 else 0)
                lines = jnp.concatenate([block[8 * kw + slot : 8 * kw + slot + 1] for kw in range(4)], 0)
                update(weight, (kh, c), lines)
        finish(weight)
    for weight, side in ((4, 0), (5, 1)):
        update(weight, (slice(None), slice(None)), small_ref[side, :, 0:64])
        finish(weight)
    for weight, kind in ((1, "stride"), (2, "block")):
        size = KINDS[kind][1]
        for side in range(2):
            for part in range(4):
                index = (side, pl.ds(size * part, size), slice(None))
                update(weight, index, rows_of(side, part, kind))
                finish(weight, index)
    first = (lax.broadcasted_iota(jnp.int32, (16, 64), 0) == 0) & (lax.broadcasted_iota(jnp.int32, (16, 64), 1) == 0)
    for slot, side, share in ((0, 1, 48.0), (2, 0, 64.0)):
        loss_ref[0, slot] = jnp.sum(jnp.where(first, small_ref[side, 0:16, 192:256], 0.0))
        loss_ref[0, slot + 1] = share * total_ref[0, 0]
    wait_all(copies)


SMEM = pl.BlockSpec(memory_space=pltpu.SMEM)
VMEM = pl.BlockSpec(memory_space=pltpu.VMEM)


def run_kernel(name, body, scalars, arrays, outs, scratch=(), limit=6, sems=0, micros=1):
    anywhere = pl.BlockSpec(memory_space=pl.ANY)
    shapes, out_specs, specs, given = [], [], [SMEM] * len(scalars), list(scalars)
    for out in outs:
        if isinstance(out, int):
            shapes.append(pltpu.SMEM((1, out), F32))
            out_specs.append(SMEM)
        elif out[0] == "far":
            shapes.append(pltpu.HBM(*out[1:]))
            out_specs.append(anywhere)
        else:
            shapes.append(pltpu.VMEM(*out))
            out_specs.append(VMEM)
    for array in arrays:
        if isinstance(array, tuple):
            place, array = array
            given.append(pltpu.with_memory_space_constraint(array, pltpu.HBM) if place == "far" else array)
            specs.append(anywhere)
        else:
            given.append(pltpu.with_memory_space_constraint(array, pltpu.VMEM))
            specs.append(VMEM)
    return pl.pallas_call(
        body,
        out_shape=shapes,
        in_specs=specs,
        out_specs=out_specs,
        scratch_shapes=[pltpu.VMEM(*s) for s in scratch] + ([pltpu.SemaphoreType.DMA((sems,))] if sems else []),
        compiler_params=pltpu.CompilerParams(vmem_limit_bytes=limit * 2**20),
        cost_estimate=pl.CostEstimate(flops=int(micros * 1.1e9), bytes_accessed=0, transcendentals=0),
        name=name,
    )(*given)


THREE = ((3, PADDED, C), BF16)
EIGHT = ((8, PADDED, C), BF16)
WIDE = ((CELLS, C), F32)
WIDE_LOW = ((CELLS, C), BF16)
TWENTY = ((20, C, C), BF16)
THIN = ((CELLS, E), F32)
THIN_LOW = ((CELLS, E), BF16)
PATCH = ((4 * CELLS, 128), BF16)


def far(*arrays):
    return tuple(("far", array) for array in arrays)


def received(parts):
    return tuple(("any", part) for part in parts)


def far_out(*shapes):
    return tuple(("far", *shape) for shape in shapes)


SIXTEEN = ((16, C, C), BF16)


BOTH = ("dp", "tensor")


def send(value, target):
    pairs = []
    for x in range(4):
        for z in range(4):
            for core in range(2):
                for y in range(4):
                    to = target(x, z, core, y)
                    pairs.append(
                        (
                            ((x * 4 + z) * 2 + core) * 4 + y,
                            (((to[0] % 4) * 4 + to[1] % 4) * 2 + to[2]) * 4 + to[3] % 4,
                        )
                    )
    return lax.ppermute(value, BOTH, pairs)


def swap_cores(value):
    return send(value, lambda x, z, core, y: (x, z, 1 - core, y))


def along_first(value, k):
    return send(value, lambda x, z, core, y: (x + k, z, core, y) if core == 0 else (x, z + k, core, y))


def along_second(value, k):
    return send(value, lambda x, z, core, y: (x, z + k, core, y) if core == 0 else (x + k, z, core, y))


def three_others(along, *values, back=False):
    found = {}
    for k in (1, 3, 2):
        found[k] = along(values[k - 1] if len(values) > 1 else values[0], -k if back else k)
    return [found[k] for k in (1, 2, 3)]


def along_tensor(value, k):
    return send(value, lambda x, z, core, y: (x, z, core, y + k))


def from_one_side(local):
    return send(local, lambda x, z, core, y: (x, z, core, y - 1 if core == 0 else y + 1))


def after(value, *others):
    return lax.optimization_barrier((value, *others))[0]


def on_device(
    pixels,
    image_sizes,
    code_indices,
    stem_kernel,
    stride_kernels,
    block_kernels,
    block_mixers,
    pre_project,
    post_project,
    codebook,
    head_kernel,
    *moments,
):
    def add_along(value, step, along_x):
        return value + send(value, lambda x, z, core, y: (x ^ step, z, core, y) if along_x else (x, z ^ step, core, y))

    image_sizes = pltpu.with_memory_space_constraint(image_sizes, pltpu.HBM)
    stem_rows = stem_kernel.transpose(0, 2, 1, 3)
    head_rows = head_kernel.transpose(0, 3, 1, 2)
    stride_rows = stride_kernels.reshape(2, 16, 64, C)
    block_rows = block_kernels.reshape(2, 9, 64, C)
    small = (((E, E), F32), ((E, E), F32))
    taps = lambda count: ((count, 64, C), BF16)
    core = lax.axis_index("dp") % 2

    def half_of(near, step, taps):
        return lax.dynamic_slice_in_dim(near, core * step, taps, 0)

    (first,) = run_kernel(
        "pack_first", pack_first_body, (), far(stride_rows, stem_rows, head_rows, pre_project, post_project),
        (taps(18),),
        (((16, 64, C), F32), ((4, 3, 4, 64), F32), ((4, 6, 4, 64), F32), *small), limit=8, sems=6, micros=3,
    )
    near0 = from_one_side(first)
    (count,) = run_kernel("count", count_body, (after(image_sizes, first),), (), (((8, 128), F32),))
    (second,) = run_kernel(
        "pack_rest", pack_rest_body, (), far(stride_rows, block_rows, after(block_mixers, first)),
        far_out(taps(36)),
        (((16, 64, C), F32), ((2, 9, 64, C), F32), ((2, 64, C), F32), taps(36)), limit=10, sems=4, micros=3,
    )
    near1 = from_one_side(second)
    count = add_along(count, 1, True)
    code_row = code_indices.reshape(1, CELLS)
    image = after(pixels.reshape(384, 128), second, count)
    planes, lanes = ((8, 8, CELLS), F32), ((128, 4 * CELLS), BF16)
    pix, xt, entries = run_kernel(
        "patches", patch_body, (image_sizes,), far(image, code_row, codebook.T), far_out(planes, lanes, THIN),
        (((384, 128), jnp.int32), ((1, CELLS), jnp.int32), ((E, 512), F32), planes, lanes, THIN), limit=12, sems=6, micros=20,
    )
    count = add_along(count, 3, True)
    near0, xt, count = lax.optimization_barrier((near0, xt, count))
    mine0 = from_one_side(half_of(near0, 8, 10))
    stride0 = (first, near0, swap_cores(near0))
    count = add_along(add_along(count, 1, False), 3, False)
    count = count + swap_cores(count)
    mine0, part1, count = lax.optimization_barrier((mine0, half_of(near1, 18, 18), count))
    mine1 = from_one_side(part1)
    stride0 += (mine0, swap_cores(mine0))
    xt, *stride0 = lax.optimization_barrier((xt, *stride0))
    small = (((C, 128), BF16), ((C, 128), BF16), ((C, E), BF16), ((C, E), BF16))
    r0, u0, slope0, av, w0, stem, head, pre, post, patch = run_kernel(
        "front", front_body, (), (*far(xt), *received(stride0)), (WIDE, THREE, *far_out(WIDE, EIGHT, SIXTEEN, *small, PATCH)),
        (lanes, ((4, 2, 64, C), BF16), WIDE, EIGHT, SIXTEEN, *small, PATCH), limit=20, sems=25, micros=12,
    )
    mine1, post = lax.optimization_barrier((mine1, post))
    rest = (second, near1, swap_cores(near1), mine1, swap_cores(mine1))
    half, sent_half = ((4, QUARTER, C), F32), ((4, SENT, C), BF16)
    keep, other = run_kernel(
        "main", main_body, (image_sizes, count),
        (r0, u0, *received(rest[0:4]), rest[4], *far(pre, post, entries, head, pix, code_row, stem, slope0, w0, av, xt, patch)),
        (half, sent_half),
        (
            TWENTY, SIXTEEN, ((C, E), BF16), ((C, E), BF16), THIN, ((C, 128), BF16), planes, ((1, CELLS), jnp.int32),
            ((C, 128), BF16), WIDE, SIXTEEN, EIGHT, lanes, PATCH,
            WIDE, WIDE_LOW, WIDE, WIDE_LOW, THIN, THIN_LOW, WIDE, THREE, WIDE, WIDE_LOW, WIDE, THREE,
            ((4, CELLS, C), F32), ((4, CELLS, C), BF16), ((128, 4 * CELLS), F32), lanes,
            EIGHT, THREE, THIN, ((64, C), F32), half, half,
        ),
        limit=53, sems=28, micros=40,
    )

    quarter, sent = ((QUARTER, C), F32), ((SENT, C), BF16)
    parts = run_kernel("add_cores", add_cores_body, (), (keep, swap_cores(other)), (quarter, *(sent,) * 3))
    found = three_others(along_first, *parts[1:])
    (grad,) = run_kernel("add_first", add_first_body, (), (parts[0], found[0], found[2], found[1]), (sent,))
    found = three_others(along_second, grad)
    (grad,) = run_kernel("add_second", add_second_body, (), (grad, found[1], found[0], found[2]), (sent,))
    found = three_others(along_first, grad, back=True)

    own_half, square = run_kernel("join", join_body, (), (grad, found[1], found[0], found[2]), (sent_half, ((8, 128), F32)))
    other_half = swap_cores(own_half)
    found = three_others(along_tensor, square)
    square = (square + found[1]) + (found[0] + found[2])
    square = square + swap_cores(square)

    def viewed(stem, stride, block, mixer, pre, post, codes, head):
        return (
            stem.transpose(0, 2, 1, 3), stride.reshape(2, 1024, C), block.reshape(2, 576, C), mixer,
            pre, post, codes.T, head.transpose(0, 3, 1, 2),
        )

    sets = [
        viewed(
            stem_kernel, stride_kernels, block_kernels, block_mixers, pre_project, post_project, codebook, head_kernel
        ),
        viewed(*moments[:8]),
        viewed(*moments[8:]),
    ]
    given = [sets[i][weight] for weight in range(8) for i in range(3)]
    shapes = [(x.shape, x.dtype) for x in given]
    *news, loss_terms, norm = run_kernel(
        "adam", adam_body, (), (own_half, other_half, square, count, *given),
        (*far_out(*shapes), 4, 1), (*shapes, ((2, 64, C), F32)), limit=24, sems=66, micros=7,
    )

    def restored(stem, stride, block, mixer, pre, post, codes, head):
        return (
            stem.transpose(0, 2, 1, 3), stride.reshape(2, 4, 4, 64, C), block.reshape(2, 3, 3, 64, C), mixer,
            pre, post, codes.T, head.transpose(0, 2, 3, 1),
        )

    return (
        loss_terms.reshape(4),
        norm.reshape(()),
        *restored(*news[0::3]),
        *restored(*news[1::3]),
        *restored(*news[2::3]),
    )


def solution(mesh):
    in_specs = (
        P("dp", None, None, None),
        P("dp", None),
        P("dp", None, None),
        P(None, None, None, "tensor"),
        P(None, None, None, "tensor", None),
        P(None, None, None, "tensor", None),
        P(None, "tensor", None),
        P("tensor", None),
        P(None, "tensor"),
        P(),
        P(None, None, "tensor", None),
        P(None, None, None, "tensor"),
        P(None, None, None, "tensor", None),
        P(None, None, None, "tensor", None),
        P(None, "tensor", None),
        P("tensor", None),
        P(None, "tensor"),
        P(),
        P(None, None, "tensor", None),
        P(None, None, None, "tensor"),
        P(None, None, None, "tensor", None),
        P(None, None, None, "tensor", None),
        P(None, "tensor", None),
        P("tensor", None),
        P(None, "tensor"),
        P(),
        P(None, None, "tensor", None),
    )
    out_specs = (
        P(),
        P(),
        P(None, None, None, "tensor"),
        P(None, None, None, "tensor", None),
        P(None, None, None, "tensor", None),
        P(None, "tensor", None),
        P("tensor", None),
        P(None, "tensor"),
        P(),
        P(None, None, "tensor", None),
        P(None, None, None, "tensor"),
        P(None, None, None, "tensor", None),
        P(None, None, None, "tensor", None),
        P(None, "tensor", None),
        P("tensor", None),
        P(None, "tensor"),
        P(),
        P(None, None, "tensor", None),
        P(None, None, None, "tensor"),
        P(None, None, None, "tensor", None),
        P(None, None, None, "tensor", None),
        P(None, "tensor", None),
        P("tensor", None),
        P(None, "tensor"),
        P(),
        P(None, None, "tensor", None),
    )
    return jax.shard_map(
        on_device, mesh=mesh, in_specs=in_specs, out_specs=out_specs, check_vma=False
    )
```
